32 devices in a mesh: grp: 2 (over y), tile: 4 (over z), slc: 2 (over x), pos: 2 (over core).
Axes of the slice: x: 2, y: 2, z: 4, core: 2. Of those that a mesh axis runs over, the one named last changes fastest.
Arguments:
- object_field: bfloat16 [8, 1024, 2, 512], P(('grp', 'slc'), 'tile'), parts along dimension 0
- offsets: int32 [2, 64], P(None, ('grp', 'tile', 'pos')), parts along dimension 1, may hold values from 0 to 1023, as said below
- counts: int32 [8], P(('grp', 'tile')), parts along dimension 0, may hold values from 1 to 8, as said below
- measured: float32 [64, 256, 256], P(('grp', 'tile', 'pos')), parts along dimension 0, may hold values from 0 to 2
- probe_wave: bfloat16 [512, 512], P('grp'), parts along dimension 0, may hold values from -5 to 5
Outputs:
- object_grad: float32 [8, 1024, 2, 512], P(('grp', 'slc'), 'tile', None, 'pos'), parts along dimension 0
The draws below stay inside these ranges and needn't reach their ends.
There are 2 independent parts, one for each index of `grp`. The reference program is written for one: setup_inputs(seed, part) draws one part's arguments, and reference() takes and returns one part's arrays. A program takes and returns all parts, laid end to end along the dimension named above; each array names one. Nothing has to cross between parts.
Inputs may be any that keep to these rules, and one draw needn't show every extreme that they name: Slot s belongs to tile s // 8; offsets[0, s] is an absolute object row among the 256 rows of that tile, offsets[1, s] an object column. Slots t * 8 to t * 8 + counts[t] - 1 of tile t are live; the other slots of the tile carry no position. In every draw some tile has all 8 slots live.
All inputs are finite; a program needn't handle non-finite values.
Results may differ from the reference program's by a relative error of at most 0.029.
Values may be sent and summed in bfloat16 or wider, within the bound.
No kernel may reach another device: no remote copies, remote signals or barrier semaphores. Data moves between devices by JAX's collectives and lax.ppermute only.
A program may use at most 320 MiB of HBM per device.

```python
import math
import jax
import jax.numpy as jnp
from jax import lax

PIX = 256
TILE_R = 256
OBJ_C = 512
SLICES = 4
OBJ_R = 1024
SLOTS = 8
POSITIONS = 32
TILES = 4


def draw_object_field(key, part):
    key_amp, key_phase = jax.random.split(key)
    shape = (SLICES, OBJ_R, OBJ_C)
    amplitude = jax.random.uniform(key_amp, shape, jnp.float32, 0.9, 1.0)
    phases = jax.random.uniform(key_phase, shape, jnp.float32, -math.pi, math.pi)
    return jnp.stack([amplitude * jnp.cos(phases), amplitude * jnp.sin(phases)], axis=2).astype(jnp.bfloat16)


def draw_offsets(key, part):
    key_row, key_col = jax.random.split(jax.random.fold_in(key, 11))
    slot_ids = jnp.arange(POSITIONS, dtype=jnp.int32)
    rows_at = slot_ids // SLOTS * TILE_R + jax.random.randint(key_row, (POSITIONS,), 0, TILE_R, dtype=jnp.int32)
    cols_at = jax.random.randint(key_col, (POSITIONS,), 0, OBJ_C, dtype=jnp.int32)
    rows_at = jnp.where(slot_ids == 0, 0, rows_at)
    rows_at = jnp.where(slot_ids == POSITIONS - 1, OBJ_R - 1, rows_at)
    cols_at = jnp.where(slot_ids == 0, 0, cols_at)
    cols_at = jnp.where(slot_ids == POSITIONS - 1, OBJ_C - 1, cols_at)
    return jnp.stack([rows_at, cols_at]).astype(jnp.int32)


def draw_counts(key, part):
    key_count, key_full = jax.random.split(jax.random.fold_in(key, 23))
    drawn = jax.random.randint(key_count, (TILES,), 1, SLOTS + 1, dtype=jnp.int32)
    full_tile = jax.random.randint(key_full, (), 0, TILES, dtype=jnp.int32)
    return jnp.where(jnp.arange(TILES, dtype=jnp.int32) == full_tile, SLOTS, drawn).astype(jnp.int32)


def levels(own_key, dims, cuts, smallest, top_value):
    factor_of = 1.0
    for axis_at, parts in cuts:
        heights = jax.random.uniform(jax.random.fold_in(jax.random.fold_in(own_key, 6), axis_at), (parts,), jnp.float32, smallest / len(cuts), top_value / len(cuts))
        factor_of = factor_of * jnp.repeat(jnp.exp(heights), dims[axis_at] // parts).reshape((-1,) + (1,) * (len(dims) - 1 - axis_at))
    return factor_of


def centred(rng, shape, scale, limit, kind=jnp.bfloat16):
    array = jax.random.normal(rng, shape, jnp.float32) * scale
    return jnp.minimum(jnp.maximum(array, -limit), limit).astype(kind)


def setup_inputs(seed: int = 0, part: int = 0) -> dict:
    arg_keys = jax.random.split(jax.random.key(seed), 6)
    part_splits = jax.random.split(jax.random.fold_in(arg_keys[5], part), 6)
    return {
        "object_field": draw_object_field(jax.random.fold_in(jax.random.fold_in(arg_keys[5], part), 71), part),
        "offsets": draw_offsets(jax.random.fold_in(jax.random.fold_in(arg_keys[5], part), 71), part),
        "counts": draw_counts(jax.random.fold_in(jax.random.fold_in(arg_keys[5], part), 71), part),
        "measured": jnp.clip(2.0 * jax.random.uniform(part_splits[3], (POSITIONS, PIX, PIX), jnp.float32) ** levels(part_splits[3], (POSITIONS, PIX, PIX), ((0, 8),), -0.2, 0.2), 0.0, 2.0),
        "probe_wave": centred(part_splits[4], (PIX, 2 * PIX), 1.0, 5.0),
    }


def halves(values):
    middle = values.shape[-1] // 2
    return (values[..., :middle], values[..., middle:])

def complex_product(left_arg, right_arg):
    left_re, left_im = halves(left_arg.astype(jnp.float32))
    right_re, right_im = halves(right_arg.astype(jnp.float32))
    return jnp.concatenate([left_re * right_re - left_im * right_im, left_re * right_im + left_im * right_re], axis=-1)

def conj_product(left_arg, right_arg):
    left_re, left_im = halves(left_arg.astype(jnp.float32))
    right_re, right_im = halves(right_arg.astype(jnp.float32))
    return jnp.concatenate([left_re * right_re + left_im * right_im, left_re * right_im - left_im * right_re], axis=-1)

def dft_tables(pixels):
    indices = jnp.arange(pixels, dtype=jnp.int32)
    product = indices[:, None] * indices[None, :] % pixels
    angles = 2.0 * math.pi / pixels * product.astype(jnp.float32)
    norm_scale = 1.0 / math.sqrt(pixels)
    real_part = (jnp.cos(angles) * norm_scale).astype(jnp.bfloat16)
    imag_part = (-jnp.sin(angles) * norm_scale).astype(jnp.bfloat16)
    fwd_left = jnp.concatenate([real_part, imag_part], axis=0)
    fwd_right = jnp.concatenate([jnp.concatenate([real_part, imag_part], axis=1), jnp.concatenate([-imag_part, real_part], axis=1)], axis=0)
    inv_left = jnp.concatenate([real_part, -imag_part], axis=0)
    inv_right = jnp.concatenate([jnp.concatenate([real_part, -imag_part], axis=1), jnp.concatenate([imag_part, real_part], axis=1)], axis=0)
    return (fwd_left, fwd_right, inv_left, inv_right)

def propagator(pixels):
    indices = jnp.arange(pixels, dtype=jnp.int32)
    frequency = (indices + pixels // 2) % pixels - pixels // 2
    squared = frequency * frequency
    phases = -0.4 * math.pi / pixels * (squared[:, None] + squared[None, :]).astype(jnp.float32)
    return jnp.concatenate([jnp.cos(phases), jnp.sin(phases)], axis=1)

def apply_left(values, table):
    pixels = values.shape[0]
    products = jnp.dot(table, values, preferred_element_type=jnp.float32)
    real_part = products[:pixels, :pixels] - products[pixels:, pixels:]
    imag_part = products[pixels:, :pixels] + products[:pixels, pixels:]
    return jnp.concatenate([real_part, imag_part], axis=1)

def apply_right(values, table):
    return jnp.dot(values, table, preferred_element_type=jnp.float32)

def slice_forward(wave_in, patch, tables, prop_field):
    fwd_left, fwd_right, inv_left, inv_right = tables
    entrance = complex_product(patch, wave_in).astype(jnp.bfloat16)
    half_way = apply_left(entrance, fwd_left).astype(jnp.bfloat16)
    spectrum = complex_product(apply_right(half_way, fwd_right), prop_field)
    returning = apply_left(spectrum.astype(jnp.bfloat16), inv_left).astype(jnp.bfloat16)
    wave_out = apply_right(returning, inv_right).astype(jnp.bfloat16)
    return (wave_out, spectrum)

def spectrum_grad(wave_grad, tables):
    fwd_left, fwd_right, inv_left, inv_right = tables
    half_way = apply_left(wave_grad, fwd_left).astype(jnp.bfloat16)
    return apply_right(half_way, fwd_right)

def detector_grad(spectrum, light):
    real_part, imag_part = halves(spectrum)
    excess = real_part * real_part + imag_part * imag_part - light
    return jnp.concatenate([excess * real_part, excess * imag_part], axis=1)

def slice_backward(spec_grad, wave_in, patch, tables, prop_field):
    fwd_left, fwd_right, inv_left, inv_right = tables
    tilted = conj_product(prop_field, spec_grad).astype(jnp.bfloat16)
    half_way = apply_left(tilted, inv_left).astype(jnp.bfloat16)
    entrance_grad = apply_right(half_way, inv_right)
    patch_grad = conj_product(wave_in, entrance_grad)
    wave_grad = conj_product(patch, entrance_grad).astype(jnp.bfloat16)
    return (wave_grad, patch_grad)

def reference(object_field, offsets, counts, measured, probe_wave):
    tables = dft_tables(PIX)
    prop_field = propagator(PIX)
    widened = jnp.concatenate([object_field, object_field[:, :PIX]], axis=1)
    widened = jnp.concatenate([widened, widened[..., :PIX]], axis=3)
    anchor = jnp.zeros((), jnp.int32)
    patch_shape = (SLICES, PIX, 2, PIX)

    def one_position(grad_wide, slot_index):
        row_at = offsets[0, slot_index].astype(jnp.int32)
        col_at = offsets[1, slot_index].astype(jnp.int32)
        live_flag = (slot_index % SLOTS < counts[slot_index // SLOTS]).astype(jnp.float32)
        corner = (anchor, row_at, anchor, col_at)
        patches = lax.dynamic_slice(widened, corner, patch_shape).reshape(SLICES, PIX, 2 * PIX)
        wave_in = probe_wave
        stored = []
        spectrum = jnp.zeros((PIX, 2 * PIX), jnp.float32)
        for layer_index in range(SLICES):
            stored.append(wave_in)
            wave_in, spectrum = slice_forward(wave_in, patches[layer_index], tables, prop_field)
        spec_grad = detector_grad(spectrum, measured[slot_index]) * live_flag
        layer_grads = [None] * SLICES
        for layer_index in reversed(range(SLICES)):
            wave_grad, layer_grads[layer_index] = slice_backward(spec_grad, stored[layer_index], patches[layer_index], tables, prop_field)
            if layer_index > 0:
                spec_grad = spectrum_grad(wave_grad, tables)
        patch_grads = jnp.stack(layer_grads).reshape(patch_shape)
        current = lax.dynamic_slice(grad_wide, corner, patch_shape)
        grad_wide = lax.dynamic_update_slice(grad_wide, current + patch_grads, corner)
        return (grad_wide, None)
    grad_init = jnp.zeros(widened.shape, jnp.float32)
    grad_wide, unused = lax.scan(one_position, grad_init, jnp.arange(POSITIONS, dtype=jnp.int32))
    folded = grad_wide[..., :OBJ_C].at[..., :PIX].add(grad_wide[..., OBJ_C:])
    return folded[:, :OBJ_R].at[:, :PIX].add(folded[:, OBJ_R:])
```

```python
import functools
import math

import jax
import jax.numpy as jnp
import ml_dtypes
import numpy as np
from jax import lax
from jax.experimental import pallas as pl
from jax.experimental.pallas import tpu as pltpu
from jax.sharding import PartitionSpec as P

VMEM_LIMIT = 58 * 1024 * 1024


def passed(array, axis, by):
    peers = lax.axis_size(axis)
    return lax.ppermute(array, axis, [(i, (i + by) % peers) for i in range(peers)])


def base_tables(pix):
    index = np.arange(pix)
    angles = 2.0 * math.pi / pix * (np.outer(index, index) % pix)
    scale = 1.0 / math.sqrt(pix)
    rounded = lambda v: v.astype(np.float32).astype(ml_dtypes.bfloat16)
    wide = lambda v: rounded(v).astype(np.float64)
    w = wide(np.cos(angles) * scale) + 1j * wide(-np.sin(angles) * scale)
    freq = (index + pix // 2) % pix - pix // 2
    h = np.exp(-0.4j * math.pi / pix * (freq * freq))
    planes = []
    for factor in (np.ones_like(h), h, np.conj(h)):
        b = factor[:, None] * w
        planes += [b.real, b.imag]
    stack = np.stack(planes)
    return rounded(np.stack([stack, stack.transpose(0, 2, 1)]))


def prep_kernel(mine, pix, info, base, probe, tabs, psi0):
    def put(m, slot, re, im, transposed):
        upper, lower = (im, -im) if transposed else (-im, im)
        tabs[m, slot, :pix, :pix] = re.astype(jnp.bfloat16)
        tabs[m, slot, :pix, pix:] = upper.astype(jnp.bfloat16)
        tabs[m, slot, pix:, :pix] = lower.astype(jnp.bfloat16)
        tabs[m, slot, pix:, pix:] = re.astype(jnp.bfloat16)

    for m in range(mine):
        r0 = info[2 + 4 * m]
        c0 = info[4 + 4 * m]

        def rolled(side, f, shift, axis):
            re = pltpu.roll(base[side, 2 * f].astype(jnp.float32), shift, axis)
            im = pltpu.roll(base[side, 2 * f + 1].astype(jnp.float32), shift, axis)
            return re, im

        for f in range(3):
            put(m, f, *rolled(0, f, r0, 1), False)
            put(m, 4 + f, *rolled(1, f, c0, 0), True)
        put(m, 3, *rolled(1, 0, r0, 0), True)
        put(m, 7, *rolled(0, 0, c0, 1), False)
        for part in range(2):
            plane = probe[:, part * pix : (part + 1) * pix].astype(jnp.float32)
            plane = pltpu.roll(pltpu.roll(plane, r0, 0), c0, 1)
            psi0[m, part] = plane.astype(jnp.bfloat16)


def main_kernel(
    groups, depth, mine, pix, info, own, nown, nown_x, oth, oth_x, noth, noth_x,
    tabs_any, psi0_any, light_any, keep, send, obj, tp, psi, tabs, light, sems
):
    layers = groups * depth
    rank = info[0]
    core = info[1]
    copies = []

    def fetch(src, dst):
        copy = pltpu.make_async_copy(src, dst, sems.at[len(copies)])
        copy.start()
        copies.append(copy)

    def layer_of(s, i):
        group = lax.rem(rank - s + groups, groups)
        return group * depth + i

    for i in range(depth):
        for col in range(2):
            fetch(own.at[col, i], obj.at[layer_of(0, i), 0, col])
        fetch(nown.at[i], obj.at[layer_of(0, i), 1, core])
        fetch(nown_x.at[i], obj.at[layer_of(0, i), 1, 1 - core])
        for s in range(1, groups):
            fetch(oth.at[s - 1, i], obj.at[layer_of(s, i), 0, core])
            fetch(oth_x.at[s - 1, i], obj.at[layer_of(s, i), 0, 1 - core])
            fetch(noth.at[s - 1, i], obj.at[layer_of(s, i), 1, core])
            fetch(noth_x.at[s - 1, i], obj.at[layer_of(s, i), 1, 1 - core])
    fetch(tabs_any, tabs)
    fetch(psi0_any, psi.at[0])
    fetch(light_any, light)
    for copy in copies:
        copy.wait()

    row_at = lax.broadcasted_iota(jnp.int32, (pix, pix), 0)
    col_at = lax.broadcasted_iota(jnp.int32, (pix, pix), 1)
    members = range(mine)
    r0 = [info[2 + 4 * m] for m in members]
    q = [info[3 + 4 * m] for m in members]
    c0 = [info[4 + 4 * m] for m in members]
    live = [info[5 + 4 * m].astype(jnp.float32) for m in members]
    f32 = jnp.float32
    bf16 = jnp.bfloat16

    def patch(j, m, part):
        right = col_at >= c0[m]
        here = jnp.where(right, obj[j, 0, q[m], part].astype(f32), obj[j, 0, 1 - q[m], part].astype(f32))
        there = jnp.where(right, obj[j, 1, q[m], part].astype(f32), obj[j, 1, 1 - q[m], part].astype(f32))
        return jnp.where(row_at >= r0[m], here, there).astype(bf16)

    def left(m, slot, re, im):
        out = jnp.dot(tabs[m, slot], jnp.concatenate([re, im], axis=0), preferred_element_type=f32)
        return out[:pix], out[pix:]

    def right(m, slot, re, im):
        out = jnp.dot(
            jnp.concatenate([re.astype(bf16), im.astype(bf16)], axis=1), tabs[m, slot],
            preferred_element_type=f32,
        )
        return out[:, :pix], out[:, pix:]

    def both(slots, pairs):
        lf, rf = slots
        halfway = [left(m, lf, re.astype(bf16), im.astype(bf16)) for m, (re, im) in zip(members, pairs)]
        return [right(m, rf, re, im) for m, (re, im) in zip(members, halfway)]

    def entrance(j):
        pairs = []
        for m in members:
            tr, ti = patch(j, m, 0), patch(j, m, 1)
            tp[j, m, 0] = tr
            tp[j, m, 1] = ti
            tr, ti = tr.astype(f32), ti.astype(f32)
            pr, pi = psi[j, m, 0].astype(f32), psi[j, m, 1].astype(f32)
            pairs.append((tr * pr - ti * pi, tr * pi + ti * pr))
        return pairs

    def forward(j, carry):
        spectra = both((1, 5), entrance(j))
        for m, (re, im) in enumerate(both((3, 7), spectra)):
            psi[j + 1, m, 0] = re.astype(bf16)
            psi[j + 1, m, 1] = im.astype(bf16)
        return carry

    lax.fori_loop(0, layers - 1, forward, 0)
    spectra = both((0, 4), entrance(layers - 1))
    tilted = []
    for m, (re, im) in enumerate(spectra):
        excess = (re * re + im * im - light[m]) * live[m]
        tilted.append((excess * re, excess * im))
    exits = both((3, 7), tilted)

    def scatter(j, exits):
        place = lax.rem(j // depth - rank + groups, groups)
        place = lax.rem(groups - place, groups) * depth + lax.rem(j, depth)
        grads = []
        for m, (re, im) in enumerate(exits):
            pr, pi = psi[j, m, 0].astype(f32), psi[j, m, 1].astype(f32)
            grads.append((pr * re + pi * im, pr * im - pi * re))
        for below in range(2):
            for away in range(2):
                target = (1 - core) if away else core
                ref = send if away else keep
                for part in range(2):
                    total = None
                    for m in members:
                        rows = (row_at < r0[m]) if below else (row_at >= r0[m])
                        same = target == q[m]
                        low = jnp.where(same, c0[m], 0)
                        high = jnp.where(same, pix, c0[m])
                        mask = rows & (col_at >= low) & (col_at < high)
                        term = jnp.where(mask, grads[m][part], 0.0)
                        total = term if total is None else total + term
                    ref[below, place, part] = total.astype(bf16)

    def wave_grads(j, exits):
        pairs = []
        for m, (re, im) in enumerate(exits):
            tr, ti = tp[j, m, 0].astype(f32), tp[j, m, 1].astype(f32)
            pairs.append((tr * re + ti * im, tr * im - ti * re))
        return pairs

    hold = tuple(part for pair in exits for part in pair)

    def backward(step, flat):
        j = layers - 1 - step
        exits = [(flat[2 * m], flat[2 * m + 1]) for m in members]
        scatter(j, exits)
        tilted = both((2, 6), wave_grads(j, exits))
        exits = both((3, 7), tilted)
        return tuple(part for pair in exits for part in pair)

    hold = lax.fori_loop(0, layers - 1, backward, hold)
    scatter(0, [(hold[2 * m], hold[2 * m + 1]) for m in members])


def body(object_field, offsets, counts, measured, probe_wave):
    depth, rows, _, cols = object_field.shape
    pix = probe_wave.shape[0]
    slots_here = offsets.shape[1]
    groups = lax.axis_size("slc")
    rank = lax.axis_index("slc").astype(jnp.int32)
    tile = lax.axis_index("tile").astype(jnp.int32)
    core = lax.axis_index("pos").astype(jnp.int32)
    mine = slots_here // groups
    layers = groups * depth
    first = rank * mine
    bf16 = jnp.bfloat16

    off = lax.dynamic_slice(offsets, (jnp.int32(0), first), (2, mine))
    in_tile = core * slots_here + first + jnp.arange(mine, dtype=jnp.int32)
    alive = (in_tile < counts[0]).astype(jnp.int32)
    places = jnp.stack([off[0] - tile * rows, off[1] // pix, off[1] % pix, alive], axis=1)
    info = jnp.concatenate([jnp.stack([rank, core]), places.reshape(-1)])
    light = lax.dynamic_slice(measured, (first, jnp.int32(0), jnp.int32(0)), (mine, pix, pix))

    blocks = object_field.reshape(depth, rows, 2, 2, pix).transpose(3, 0, 2, 1, 4)
    part = lax.dynamic_index_in_dim(blocks, core, 0, keepdims=False)
    half = depth // 2

    nown_hi = passed(part[half:], "tile", -1)
    oth_lo = [passed(part[:half], "slc", s) for s in range(1, groups)]
    nown_lo = passed(part[:half], "tile", -1)
    oth_hi = [passed(part[half:], "slc", s) for s in range(1, groups)]
    noth_lo = [passed(o, "tile", -1) for o in oth_lo]
    noth_hi = [passed(nown_hi, "slc", s) for s in range(1, groups)]
    nown = jnp.concatenate([nown_lo, nown_hi])
    oth = jnp.stack([jnp.concatenate(p) for p in zip(oth_lo, oth_hi)])
    noth = jnp.stack([jnp.concatenate(p) for p in zip(noth_lo, noth_hi)])
    nown_x = passed(nown, "pos", 1)
    oth_x = passed(oth, "pos", 1)
    noth_x = passed(noth, "pos", 1)

    smem = pl.BlockSpec(memory_space=pltpu.SMEM)
    vmem = pl.BlockSpec(memory_space=pltpu.VMEM)
    anywhere = pl.BlockSpec(memory_space=pl.ANY)
    tabs, psi0 = pl.pallas_call(
        functools.partial(prep_kernel, mine, pix),
        out_shape=(
            jax.ShapeDtypeStruct((mine, 8, 2 * pix, 2 * pix), bf16),
            jax.ShapeDtypeStruct((mine, 2, pix, pix), bf16),
        ),
        in_specs=[smem, vmem, vmem],
        out_specs=(vmem, vmem),
        compiler_params=pltpu.CompilerParams(vmem_limit_bytes=VMEM_LIMIT),
        name="tables",
    )(info, jnp.asarray(base_tables(pix)), probe_wave)

    grads_shape = (2, layers, 2, pix, pix)
    fetches = depth * (4 + 4 * (groups - 1)) + 3
    keep, send = pl.pallas_call(
        functools.partial(main_kernel, groups, depth, mine, pix),
        out_shape=(jax.ShapeDtypeStruct(grads_shape, bf16),) * 2,
        in_specs=[smem] + [anywhere] * 10,
        out_specs=(vmem, vmem),
        scratch_shapes=[
            pltpu.VMEM((layers, 2, 2, 2, pix, pix), bf16),
            pltpu.VMEM((layers, mine, 2, pix, pix), bf16),
            pltpu.VMEM((layers, mine, 2, pix, pix), bf16),
            pltpu.VMEM((mine, 8, 2 * pix, 2 * pix), bf16),
            pltpu.VMEM((mine, pix, pix), jnp.float32),
            pltpu.SemaphoreType.DMA((fetches,)),
        ],
        compiler_params=pltpu.CompilerParams(vmem_limit_bytes=VMEM_LIMIT),
        name="waves",
    )(info, blocks, nown, nown_x, oth, oth_x, noth, noth_x, tabs, psi0, light)

    total = (keep.astype(jnp.float32) + passed(send, "pos", 1).astype(jnp.float32)).astype(bf16)
    here = total[0].reshape(groups, depth, 2, pix, pix)
    rim = total[1].reshape(groups, depth, 2, pix, pix)
    wide = lambda v: v.astype(jnp.float32)
    rim_lo = wide(rim[0, :half])
    tile_lo = wide(here[0, :half])
    tile_hi = wide(here[0, half:])
    for s in range(1, groups):
        rim_lo += wide(passed(rim[s, :half], "slc", -s))
        tile_lo += wide(passed(here[s, :half], "slc", -s))
        other_hi = wide(here[s, half:]) + wide(passed(rim[s, half:], "tile", 1))
        tile_hi += wide(passed(other_hi.astype(bf16), "slc", -s))
    tile_hi += wide(passed(rim[0, half:], "tile", 1))
    tile_lo += wide(passed(rim_lo.astype(bf16), "tile", 1))
    return jnp.concatenate([tile_lo, tile_hi]).transpose(0, 2, 1, 3)


def solution(mesh):
    placed = (
        P(("grp", "slc"), "tile", None, None),
        P(None, ("grp", "tile", "pos")),
        P(("grp", "tile")),
        P(("grp", "tile", "pos"), None, None),
        P("grp", None),
    )
    return jax.shard_map(
        body,
        mesh=mesh,
        in_specs=placed,
        out_specs=P(("grp", "slc"), "tile", None, "pos"),
        check_vma=False,
    )
```

```python
import functools
import math

import jax
import jax.numpy as jnp
import ml_dtypes
import numpy as np
from jax import lax
from jax.experimental import pallas as pl
from jax.experimental.pallas import tpu as pltpu
from jax.sharding import PartitionSpec as P

VMEM_LIMIT = 58 * 1024 * 1024


def passed(array, axis, by):
    peers = lax.axis_size(axis)
    return lax.ppermute(array, axis, [(i, (i + by) % peers) for i in range(peers)])


def base_tables(pix):
    index = np.arange(pix)
    angles = 2.0 * math.pi / pix * (np.outer(index, index) % pix)
    scale = 1.0 / math.sqrt(pix)
    rounded = lambda v: v.astype(np.float32).astype(ml_dtypes.bfloat16)
    wide = lambda v: rounded(v).astype(np.float64)
    w = wide(np.cos(angles) * scale) + 1j * wide(-np.sin(angles) * scale)
    freq = (index + pix // 2) % pix - pix // 2
    h = np.exp(-0.4j * math.pi / pix * (freq * freq))
    planes = []
    for factor in (np.ones_like(h), h, np.conj(h)):
        b = factor[:, None] * w
        planes += [b.real, b.imag]
    stack = np.stack(planes)
    return rounded(np.stack([stack, stack.transpose(0, 2, 1)]))


def prep_kernel(mine, pix, info, base, probe, lefts, rights, psi0):
    bf16 = jnp.bfloat16
    for m in range(mine):
        r0 = info[2 + 4 * m]
        c0 = info[4 + 4 * m]

        def rolled(side, f, shift, axis):
            re = pltpu.roll(base[side, 2 * f].astype(jnp.float32), shift, axis)
            im = pltpu.roll(base[side, 2 * f + 1].astype(jnp.float32), shift, axis)
            return re.astype(bf16), im.astype(bf16)

        def inverse(side, shift, axis):
            re = pltpu.roll(base[side, 0].astype(jnp.float32), shift, axis)
            im = pltpu.roll(base[side, 1].astype(jnp.float32), shift, axis)
            return re.astype(bf16), (-im).astype(bf16)

        for t in range(4):
            re, im = rolled(0, t, r0, 1) if t < 3 else inverse(1, r0, 0)
            lefts[m, t, :, :pix] = re
            lefts[m, t, :, pix:] = im
            re, im = rolled(1, t, c0, 0) if t < 3 else inverse(0, c0, 1)
            rights[m, t, :pix, :] = re
            rights[m, t, pix:, :] = im
        for part in range(2):
            plane = probe[:, part * pix : (part + 1) * pix].astype(jnp.float32)
            plane = pltpu.roll(pltpu.roll(plane, r0, 0), c0, 1)
            psi0[m, part] = plane.astype(bf16)


def main_kernel(groups, depth, mine, pix, pieces, info, *refs):
    count = len(pieces) + 1
    own, operands = refs[0], refs[1:count]
    lefts_any, rights_any, psi0_any, light_any = refs[count : count + 4]
    outs = refs[count + 4 : count + 4 + 4 * groups]
    obj, tp, psi, lefts, rights, light, grads, sems, tab_sems, out_sems = refs[count + 4 + 4 * groups :]
    layers = groups * depth
    rank = info[0]
    core = info[1]
    members = range(mine)

    def layer_of(s, i):
        group = lax.rem(rank - s + groups, groups)
        return group * depth + i

    def table_copies(t):
        return [
            pltpu.make_async_copy(lefts_any.at[:, t], lefts.at[:, t], tab_sems.at[t, 0]),
            pltpu.make_async_copy(rights_any.at[:, t], rights.at[:, t], tab_sems.at[t, 1]),
        ]

    def wait_tables(t):
        for copy in table_copies(t):
            copy.wait()

    psi_copy = pltpu.make_async_copy(psi0_any, psi.at[0], tab_sems.at[4, 0])
    light_copy = pltpu.make_async_copy(light_any, light, tab_sems.at[4, 1])
    psi_copy.start()
    for copy in table_copies(1) + table_copies(3):
        copy.start()
    for i in range(depth):
        j = layer_of(0, i)
        for col in range(2):
            pltpu.make_async_copy(own.at[col, i], obj.at[j, 0, col], sems.at[j, col]).start()
    for (s, start, below, away), ref in zip(pieces, operands):
        for i in range(ref.shape[0]):
            j = layer_of(s, start + i)
            col = (1 - core) if away else core
            at = 2 * below + col
            pltpu.make_async_copy(ref.at[i], obj.at[j, below, col], sems.at[j, at]).start()
    light_copy.start()
    for copy in table_copies(0) + table_copies(2):
        copy.start()

    def wait_object(j):
        for below in range(2):
            for col in range(2):
                pltpu.make_async_copy(own.at[0, 0], obj.at[j, below, col], sems.at[j, 2 * below + col]).wait()

    row_at = lax.broadcasted_iota(jnp.int32, (pix, pix), 0)
    col_at = lax.broadcasted_iota(jnp.int32, (pix, pix), 1)
    r0 = [info[2 + 4 * m] for m in members]
    q = [info[3 + 4 * m] for m in members]
    c0 = [info[4 + 4 * m] for m in members]
    live = [info[5 + 4 * m].astype(jnp.float32) for m in members]
    f32 = jnp.float32
    bf16 = jnp.bfloat16

    def patch(j, m, part):
        right = col_at >= c0[m]
        here = jnp.where(right, obj[j, 0, q[m], part].astype(f32), obj[j, 0, 1 - q[m], part].astype(f32))
        there = jnp.where(right, obj[j, 1, q[m], part].astype(f32), obj[j, 1, 1 - q[m], part].astype(f32))
        return jnp.where(row_at >= r0[m], here, there).astype(bf16)

    def left(m, t, re, im):
        paired = jnp.concatenate(
            [jnp.concatenate([re, im], axis=1), jnp.concatenate([-im, re], axis=1)], axis=0
        )
        out = jnp.dot(lefts[m, t], paired, preferred_element_type=f32)
        return out[:, :pix].astype(bf16), out[:, pix:].astype(bf16)

    def right(m, t, re, im):
        paired = jnp.concatenate(
            [jnp.concatenate([re, -im], axis=1), jnp.concatenate([im, re], axis=1)], axis=0
        )
        out = jnp.dot(paired, rights[m, t], preferred_element_type=f32)
        return out[:pix], out[pix:]

    def both(t, pairs):
        halfway = [left(m, t, re.astype(bf16), im.astype(bf16)) for m, (re, im) in zip(members, pairs)]
        return [right(m, t, re, im) for m, (re, im) in zip(members, halfway)]

    def entrance(j):
        pairs = []
        for m in members:
            tr, ti = patch(j, m, 0), patch(j, m, 1)
            tp[j, m, 0] = tr
            tp[j, m, 1] = ti
            tr, ti = tr.astype(f32), ti.astype(f32)
            pr, pi = psi[j, m, 0].astype(f32), psi[j, m, 1].astype(f32)
            pairs.append((tr * pr - ti * pi, tr * pi + ti * pr))
        return pairs

    psi_copy.wait()
    wait_tables(1)
    wait_tables(3)

    def forward(j, carry):
        wait_object(j)
        spectra = both(1, entrance(j))
        for m, (re, im) in enumerate(both(3, spectra)):
            psi[j + 1, m, 0] = re.astype(bf16)
            psi[j + 1, m, 1] = im.astype(bf16)
        return carry

    lax.fori_loop(0, layers - 1, forward, 0)
    wait_object(layers - 1)
    wait_tables(0)
    light_copy.wait()
    spectra = both(0, entrance(layers - 1))
    tilted = []
    for m, (re, im) in enumerate(spectra):
        excess = (re * re + im * im - light[m]) * live[m]
        tilted.append((excess * re, excess * im))
    exits = both(3, tilted)

    def out_copy(away, below, s, i):
        place = s * depth + i
        out = outs[(away * 2 + below) * groups + s]
        return pltpu.make_async_copy(grads.at[away, below, place], out.at[i], out_sems.at[away, below, place])

    def scatter(j, exits):
        step = lax.rem(rank - j // depth + groups, groups)
        within = lax.rem(j, depth)
        place = step * depth + within
        terms = []
        for m, (re, im) in enumerate(exits):
            pr, pi = psi[j, m, 0].astype(f32), psi[j, m, 1].astype(f32)
            terms.append((pr * re + pi * im, pr * im - pi * re))
        for below in range(2):
            for away in range(2):
                target = (1 - core) if away else core
                for part in range(2):
                    total = None
                    for m in members:
                        rows = (row_at < r0[m]) if below else (row_at >= r0[m])
                        same = target == q[m]
                        low = jnp.where(same, c0[m], 0)
                        high = jnp.where(same, pix, c0[m])
                        mask = rows & (col_at >= low) & (col_at < high)
                        term = jnp.where(mask, terms[m][part], 0.0)
                        total = term if total is None else total + term
                    grads[away, below, place, part] = total.astype(bf16)
        for s in range(groups):

            @pl.when(step == s)
            def _():
                for below in range(2):
                    for away in range(2):
                        out_copy(away, below, s, within).start()

    def wave_grads(j, exits):
        pairs = []
        for m, (re, im) in enumerate(exits):
            tr, ti = tp[j, m, 0].astype(f32), tp[j, m, 1].astype(f32)
            pairs.append((tr * re + ti * im, tr * im - ti * re))
        return pairs

    wait_tables(2)
    hold = tuple(part for pair in exits for part in pair)

    def backward(step, flat):
        j = layers - 1 - step
        exits = [(flat[2 * m], flat[2 * m + 1]) for m in members]
        scatter(j, exits)
        tilted = both(2, wave_grads(j, exits))
        exits = both(3, tilted)
        return tuple(part for pair in exits for part in pair)

    hold = lax.fori_loop(0, layers - 1, backward, hold)
    scatter(0, [(hold[2 * m], hold[2 * m + 1]) for m in members])
    for away in range(2):
        for below in range(2):
            for s in range(groups):
                for i in range(depth):
                    out_copy(away, below, s, i).wait()


def body(object_field, offsets, counts, measured, probe_wave):
    depth, rows, _, cols = object_field.shape
    pix = probe_wave.shape[0]
    slots_here = offsets.shape[1]
    groups = lax.axis_size("slc")
    rank = lax.axis_index("slc").astype(jnp.int32)
    tile = lax.axis_index("tile").astype(jnp.int32)
    core = lax.axis_index("pos").astype(jnp.int32)
    mine = slots_here // groups
    layers = groups * depth
    first = rank * mine
    bf16 = jnp.bfloat16

    off = lax.dynamic_slice(offsets, (jnp.int32(0), first), (2, mine))
    in_tile = core * slots_here + first + jnp.arange(mine, dtype=jnp.int32)
    alive = (in_tile < counts[0]).astype(jnp.int32)
    places = jnp.stack([off[0] - tile * rows, off[1] // pix, off[1] % pix, alive], axis=1)
    info = jnp.concatenate([jnp.stack([rank, core]), places.reshape(-1)])
    light = lax.dynamic_slice(measured, (first, jnp.int32(0), jnp.int32(0)), (mine, pix, pix))

    zero = jnp.int32(0)
    part = lax.dynamic_slice(object_field, (zero, zero, zero, core * pix), (depth, rows, 2, pix))
    part = part.transpose(0, 2, 1, 3)
    half = depth // 2
    lo, hi = part[:half], part[half:]

    steps = range(1, groups)
    here = {(s, 0): passed(lo, "slc", s) for s in steps}
    nown_hi = passed(hi, "tile", -1)
    here |= {(s, half): passed(hi, "slc", s) for s in steps}
    nown_lo = passed(lo, "tile", -1)
    below = {(0, half): nown_hi, (0, 0): nown_lo}
    below |= {(s, 0): passed(here[s, 0], "tile", -1) for s in steps}
    below |= {(s, half): passed(nown_hi, "slc", s) for s in steps}
    pieces, operands = [], []
    for row_block, found in ((0, here), (1, below)):
        for (s, start), array in found.items():
            pieces += [(s, start, row_block, 0), (s, start, row_block, 1)]
            operands += [array, passed(array, "pos", 1)]
    blocks = object_field.reshape(depth, rows, 2, 2, pix).transpose(3, 0, 2, 1, 4)

    smem = pl.BlockSpec(memory_space=pltpu.SMEM)
    vmem = pl.BlockSpec(memory_space=pltpu.VMEM)
    anywhere = pl.BlockSpec(memory_space=pl.ANY)
    lefts, rights, psi0 = pl.pallas_call(
        functools.partial(prep_kernel, mine, pix),
        out_shape=(
            jax.ShapeDtypeStruct((mine, 4, pix, 2 * pix), bf16),
            jax.ShapeDtypeStruct((mine, 4, 2 * pix, pix), bf16),
            jax.ShapeDtypeStruct((mine, 2, pix, pix), bf16),
        ),
        in_specs=[smem, vmem, vmem],
        out_specs=(vmem, vmem, vmem),
        compiler_params=pltpu.CompilerParams(vmem_limit_bytes=VMEM_LIMIT),
        cost_estimate=pl.CostEstimate(flops=8 * 10**9, bytes_accessed=8 * 2**20, transcendentals=0),
        name="tables",
    )(info, jnp.asarray(base_tables(pix)), probe_wave)

    outs = pl.pallas_call(
        functools.partial(main_kernel, groups, depth, mine, pix, tuple(pieces)),
        out_shape=(jax.ShapeDtypeStruct((depth, 2, pix, pix), bf16),) * (4 * groups),
        in_specs=[smem] + [anywhere] * (5 + len(operands)),
        out_specs=(anywhere,) * (4 * groups),
        scratch_shapes=[
            pltpu.VMEM((layers, 2, 2, 2, pix, pix), bf16),
            pltpu.VMEM((layers, mine, 2, pix, pix), bf16),
            pltpu.VMEM((layers, mine, 2, pix, pix), bf16),
            pltpu.VMEM((mine, 4, pix, 2 * pix), bf16),
            pltpu.VMEM((mine, 4, 2 * pix, pix), bf16),
            pltpu.VMEM((mine, pix, pix), jnp.float32),
            pltpu.VMEM((2, 2, layers, 2, pix, pix), bf16),
            pltpu.SemaphoreType.DMA((layers, 4)),
            pltpu.SemaphoreType.DMA((5, 2)),
            pltpu.SemaphoreType.DMA((2, 2, layers)),
        ],
        compiler_params=pltpu.CompilerParams(vmem_limit_bytes=VMEM_LIMIT),
        cost_estimate=pl.CostEstimate(flops=15 * 10**9, bytes_accessed=16 * 2**20, transcendentals=0),
        name="waves",
    )(info, blocks, *operands, lefts, rights, psi0, light)

    wide = lambda v: v.astype(jnp.float32)
    sums = {}
    for s in [*steps, 0]:
        for row_block in (1, 0):
            at = row_block * groups + s
            sums[row_block, s] = wide(outs[at]) + wide(passed(outs[2 * groups + at], "pos", 1))
    rim_lo = sums[1, 0][:half]
    rim_hi = sums[1, 0][half:].astype(bf16)
    tile_lo = sums[0, 0][:half]
    tile_hi = sums[0, 0][half:]
    for s in steps:
        rim, tile_part = sums[1, s], sums[0, s]
        rim_lo += wide(passed(rim[:half].astype(bf16), "slc", -s))
        other_hi = tile_part[half:] + wide(passed(rim[half:].astype(bf16), "tile", 1))
        tile_lo += wide(passed(tile_part[:half].astype(bf16), "slc", -s))
        tile_hi += wide(passed(other_hi.astype(bf16), "slc", -s))
    tile_hi += wide(passed(rim_hi, "tile", 1))
    tile_lo += wide(passed(rim_lo.astype(bf16), "tile", 1))
    return jnp.concatenate([tile_lo, tile_hi]).transpose(0, 2, 1, 3)


def solution(mesh):
    placed = (
        P(("grp", "slc"), "tile", None, None),
        P(None, ("grp", "tile", "pos")),
        P(("grp", "tile")),
        P(("grp", "tile", "pos"), None, None),
        P("grp", None),
    )
    return jax.shard_map(
        body,
        mesh=mesh,
        in_specs=placed,
        out_specs=P(("grp", "slc"), "tile", None, "pos"),
        check_vma=False,
    )
```

```python
import functools
import math

import jax
import jax.numpy as jnp
import ml_dtypes
import numpy as np
from jax import lax
from jax.experimental import pallas as pl
from jax.experimental.pallas import tpu as pltpu
from jax.sharding import PartitionSpec as P

VMEM_LIMIT = 58 * 1024 * 1024


def passed(array, axis, by):
    peers = lax.axis_size(axis)
    return lax.ppermute(array, axis, [(i, (i + by) % peers) for i in range(peers)])


def split_roles(array, tile_by, slc_by, slc_core, with_tile=True):
    tiles, groups, cores = (lax.axis_size(name) for name in ("tile", "slc", "pos"))
    at = lambda t, g, c: ((t % tiles) * groups + g % groups) * cores + c
    pairs = []
    for t in range(tiles):
        for g in range(groups):
            pairs.append((at(t, g, slc_core), at(t, g + slc_by, slc_core)))
            if with_tile:
                pairs.append((at(t, g, 1 - slc_core), at(t + tile_by, g, 1 - slc_core)))
    return lax.ppermute(array, ("tile", "slc", "pos"), pairs)


def base_tables(pix):
    index = np.arange(pix)
    angles = 2.0 * math.pi / pix * (np.outer(index, index) % pix)
    scale = 1.0 / math.sqrt(pix)
    rounded = lambda v: v.astype(np.float32).astype(ml_dtypes.bfloat16)
    wide = lambda v: rounded(v).astype(np.float64)
    w = wide(np.cos(angles) * scale) + 1j * wide(-np.sin(angles) * scale)
    freq = (index + pix // 2) % pix - pix // 2
    h = np.exp(-0.4j * math.pi / pix * (freq * freq))
    planes = []
    for factor in (np.ones_like(h), h, np.conj(h)):
        b = factor[:, None] * w
        planes += [b.real, b.imag]
    stack = np.stack(planes)
    return rounded(np.stack([stack, stack.transpose(0, 2, 1)]))


def prep_kernel(mine, pix, info, base, probe, lefts, rights, psi0):
    bf16 = jnp.bfloat16
    for m in range(mine):
        r0 = info[2 + 4 * m]
        c0 = info[4 + 4 * m]

        def rolled(side, f, shift, axis):
            re = pltpu.roll(base[side, 2 * f].astype(jnp.float32), shift, axis)
            im = pltpu.roll(base[side, 2 * f + 1].astype(jnp.float32), shift, axis)
            return re.astype(bf16), im.astype(bf16)

        def inverse(side, shift, axis):
            re = pltpu.roll(base[side, 0].astype(jnp.float32), shift, axis)
            im = pltpu.roll(base[side, 1].astype(jnp.float32), shift, axis)
            return re.astype(bf16), (-im).astype(bf16)

        for t in range(4):
            re, im = rolled(0, t, r0, 1) if t < 3 else inverse(1, r0, 0)
            lefts[m, t, :, :pix] = re
            lefts[m, t, :, pix:] = im
            re, im = rolled(1, t, c0, 0) if t < 3 else inverse(0, c0, 1)
            rights[m, t, :pix, :] = re
            rights[m, t, pix:, :] = im
        for part in range(2):
            plane = probe[:, part * pix : (part + 1) * pix].astype(jnp.float32)
            plane = pltpu.roll(pltpu.roll(plane, r0, 0), c0, 1)
            psi0[m, part] = plane.astype(bf16)


def main_kernel(groups, depth, mine, pix, pieces, results, info, *refs):
    count = len(pieces) + 1
    own, operands = refs[0], refs[1:count]
    lefts_any, rights_any, psi0_any, light_any = refs[count : count + 4]
    outs = refs[count + 4 : count + 4 + len(results)]
    own_out = refs[count + 4 + len(results)]
    obj, tp, psi, lefts, rights, light, grads, sems, tab_sems, out_sems = refs[count + 5 + len(results) :]
    layers = groups * depth
    half = depth // 2
    rank = info[0]
    core = info[1]
    members = range(mine)

    def layer_of(s, i):
        group = lax.rem(rank - s + groups, groups)
        return group * depth + i

    def table_copies(t):
        return [
            pltpu.make_async_copy(lefts_any.at[:, t], lefts.at[:, t], tab_sems.at[t, 0]),
            pltpu.make_async_copy(rights_any.at[:, t], rights.at[:, t], tab_sems.at[t, 1]),
        ]

    def wait_tables(t):
        for copy in table_copies(t):
            copy.wait()

    psi_copy = pltpu.make_async_copy(psi0_any, psi.at[0], tab_sems.at[4, 0])
    light_copy = pltpu.make_async_copy(light_any.at[pl.ds(rank * mine, mine)], light, tab_sems.at[4, 1])
    psi_copy.start()
    for copy in table_copies(1) + table_copies(3):
        copy.start()
    for i in range(depth):
        j = layer_of(0, i)
        pltpu.make_async_copy(own.at[i], obj.at[j, 0], sems.at[j, 0]).start()
    for holds, ref in zip(pieces, operands):
        for c in range(2):
            if holds[c] is None:
                continue
            s, high, below = holds[c]

            @pl.when(core == c)
            def _():
                for i in range(half):
                    j = layer_of(s, high * half + i)
                    pltpu.make_async_copy(ref.at[i], obj.at[j, below], sems.at[j, below]).start()

    light_copy.start()
    for copy in table_copies(0) + table_copies(2):
        copy.start()

    def wait_object(j):
        for below in range(2):
            pltpu.make_async_copy(own.at[0], obj.at[j, below], sems.at[j, below]).wait()

    row_at = lax.broadcasted_iota(jnp.int32, (pix, pix), 0)
    col_at = lax.broadcasted_iota(jnp.int32, (pix, pix), 1)
    r0 = [info[2 + 4 * m] for m in members]
    q = [info[3 + 4 * m] for m in members]
    c0 = [info[4 + 4 * m] for m in members]
    live = [info[5 + 4 * m].astype(jnp.float32) for m in members]
    f32 = jnp.float32
    bf16 = jnp.bfloat16

    def patch(j, m, part):
        right = col_at >= c0[m]
        at = pl.ds(pl.multiple_of(q[m] * pix, pix), pix)
        after = pl.ds(pl.multiple_of((1 - q[m]) * pix, pix), pix)
        here = jnp.where(right, obj[j, 0, part, :, at].astype(f32), obj[j, 0, part, :, after].astype(f32))
        there = jnp.where(right, obj[j, 1, part, :, at].astype(f32), obj[j, 1, part, :, after].astype(f32))
        return jnp.where(row_at >= r0[m], here, there).astype(bf16)

    def left(m, t, re, im):
        paired = jnp.concatenate(
            [jnp.concatenate([re, im], axis=1), jnp.concatenate([-im, re], axis=1)], axis=0
        )
        out = jnp.dot(lefts[m, t], paired, preferred_element_type=f32)
        return out[:, :pix].astype(bf16), out[:, pix:].astype(bf16)

    def right(m, t, re, im):
        paired = jnp.concatenate(
            [jnp.concatenate([re, -im], axis=1), jnp.concatenate([im, re], axis=1)], axis=0
        )
        out = jnp.dot(paired, rights[m, t], preferred_element_type=f32)
        return out[:pix], out[pix:]

    def both(t, pairs):
        halfway = [left(m, t, re.astype(bf16), im.astype(bf16)) for m, (re, im) in zip(members, pairs)]
        return [right(m, t, re, im) for m, (re, im) in zip(members, halfway)]

    def entrance(j):
        pairs = []
        for m in members:
            tr, ti = patch(j, m, 0), patch(j, m, 1)
            tp[j, m, 0] = tr
            tp[j, m, 1] = ti
            tr, ti = tr.astype(f32), ti.astype(f32)
            pr, pi = psi[j, m, 0].astype(f32), psi[j, m, 1].astype(f32)
            pairs.append((tr * pr - ti * pi, tr * pi + ti * pr))
        return pairs

    psi_copy.wait()
    wait_tables(1)
    wait_tables(3)

    def forward(j, carry):
        wait_object(j)
        spectra = both(1, entrance(j))
        for m, (re, im) in enumerate(both(3, spectra)):
            psi[j + 1, m, 0] = re.astype(bf16)
            psi[j + 1, m, 1] = im.astype(bf16)
        return carry

    lax.fori_loop(0, layers - 1, forward, 0)
    wait_object(layers - 1)
    wait_tables(0)
    light_copy.wait()
    spectra = both(0, entrance(layers - 1))
    tilted = []
    for m, (re, im) in enumerate(spectra):
        excess = (re * re + im * im - light[m]) * live[m]
        tilted.append((excess * re, excess * im))
    exits = both(3, tilted)

    def out_copy(below, place, out):
        return pltpu.make_async_copy(grads.at[below, place], out, out_sems.at[below, place])

    def send_out(step, within):
        place = step * depth + within

        @pl.when(step == 0)
        def _():
            out_copy(0, place, own_out.at[within]).start()

        for takes, ref in zip(results, outs):
            for c in range(2):
                if takes[c] is None:
                    continue
                s, high, below = takes[c]
                inside = (within >= half) if high else (within < half)

                @pl.when((core == c) & (step == s) & inside)
                def _():
                    out_copy(below, place, ref.at[within - high * half]).start()

    def scatter(j, exits):
        step = lax.rem(rank - j // depth + groups, groups)
        within = lax.rem(j, depth)
        place = step * depth + within
        terms = []
        for m, (re, im) in enumerate(exits):
            pr, pi = psi[j, m, 0].astype(f32), psi[j, m, 1].astype(f32)
            terms.append((pr * re + pi * im, pr * im - pi * re))
        for below in range(2):
            for col in range(2):
                for part in range(2):
                    total = None
                    for m in members:
                        rows = (row_at < r0[m]) if below else (row_at >= r0[m])
                        low = jnp.where(q[m] == col, c0[m], 0)
                        high = jnp.where(q[m] == col, pix, c0[m])
                        mask = rows & (col_at >= low) & (col_at < high)
                        term = jnp.where(mask, terms[m][part], 0.0)
                        total = term if total is None else total + term
                    grads[below, place, part, :, col * pix : (col + 1) * pix] = total.astype(bf16)
        send_out(step, within)

    def wave_grads(j, exits):
        pairs = []
        for m, (re, im) in enumerate(exits):
            tr, ti = tp[j, m, 0].astype(f32), tp[j, m, 1].astype(f32)
            pairs.append((tr * re + ti * im, tr * im - ti * re))
        return pairs

    wait_tables(2)
    hold = tuple(part for pair in exits for part in pair)

    def backward(step, flat):
        j = layers - 1 - step
        exits = [(flat[2 * m], flat[2 * m + 1]) for m in members]
        scatter(j, exits)
        tilted = both(2, wave_grads(j, exits))
        exits = both(3, tilted)
        return tuple(part for pair in exits for part in pair)

    hold = lax.fori_loop(0, layers - 1, backward, hold)
    scatter(0, [(hold[2 * m], hold[2 * m + 1]) for m in members])
    for below in range(2):
        for place in range(layers):
            out_copy(below, place, own_out.at[0]).wait()


def body(object_field, offsets, counts, measured, probe_wave):
    depth, rows, _, cols = object_field.shape
    pix = probe_wave.shape[0]
    slots_here = offsets.shape[1]
    groups = lax.axis_size("slc")
    rank = lax.axis_index("slc").astype(jnp.int32)
    tile = lax.axis_index("tile").astype(jnp.int32)
    core = lax.axis_index("pos").astype(jnp.int32)
    mine = slots_here // groups
    layers = groups * depth
    first = rank * mine
    bf16 = jnp.bfloat16

    off = lax.dynamic_slice(offsets, (jnp.int32(0), first), (2, mine))
    in_tile = core * slots_here + first + jnp.arange(mine, dtype=jnp.int32)
    alive = (in_tile < counts[0]).astype(jnp.int32)
    places = jnp.stack([off[0] - tile * rows, off[1] // pix, off[1] % pix, alive], axis=1)
    info = jnp.concatenate([jnp.stack([rank, core]), places.reshape(-1)])

    planes = object_field.transpose(0, 2, 1, 3)
    half = depth // 2
    steps = range(1, groups)
    halves_of = lambda high: lax.dynamic_slice_in_dim(planes, high * half, half, axis=0)
    first_half, last_half = halves_of(core), halves_of(1 - core)
    got_first = [split_roles(first_half, -1, s, 0, s == 1) for s in steps]
    got_last = [split_roles(last_half, -1, s, 0, s == 1) for s in steps]

    smem = pl.BlockSpec(memory_space=pltpu.SMEM)
    vmem = pl.BlockSpec(memory_space=pltpu.VMEM)
    anywhere = pl.BlockSpec(memory_space=pl.ANY)
    lefts, rights, psi0 = pl.pallas_call(
        functools.partial(prep_kernel, mine, pix),
        out_shape=(
            jax.ShapeDtypeStruct((mine, 4, pix, 2 * pix), bf16),
            jax.ShapeDtypeStruct((mine, 4, 2 * pix, pix), bf16),
            jax.ShapeDtypeStruct((mine, 2, pix, pix), bf16),
        ),
        in_specs=[smem, vmem, vmem],
        out_specs=(vmem, vmem, vmem),
        compiler_params=pltpu.CompilerParams(vmem_limit_bytes=VMEM_LIMIT),
        cost_estimate=pl.CostEstimate(flops=8 * 10**9, bytes_accessed=8 * 2**20, transcendentals=0),
        name="tables",
    )(info, jnp.asarray(base_tables(pix)), probe_wave)

    got_first, lefts, rights, psi0 = lax.optimization_barrier((got_first, lefts, rights, psi0))
    passed_on = [split_roles(got_first[s - 1], -1, s, 1) for s in steps]
    pieces, operands = [], []
    for s in steps:
        rim_hi, rim_lo = ((0, 1, 1), (0, 0, 1)) if s == 1 else (None, None)
        for array, holds in (
            (got_first[s - 1], ((s, 0, 0), rim_hi)),
            (got_last[s - 1], ((s, 1, 0), rim_lo)),
            (passed_on[s - 1], ((s, 0, 1), (s, 1, 1))),
        ):
            pieces += [holds, holds[::-1]]
            operands += [array, passed(array, "pos", 1)]
    results = []
    for s in steps:
        rim_hi, rim_lo = ((0, 1, 1), (0, 0, 1)) if s == 1 else (None, None)
        for holds in (((s, 1, 1), (s, 0, 1)), ((s, 0, 0), rim_hi), ((s, 1, 0), rim_lo)):
            results += [holds, holds[::-1]]

    half_shape = jax.ShapeDtypeStruct((half, 2, rows, cols), bf16)
    *outs, own_grads = pl.pallas_call(
        functools.partial(main_kernel, groups, depth, mine, pix, tuple(pieces), tuple(results)),
        out_shape=(half_shape,) * len(results) + (jax.ShapeDtypeStruct((depth, 2, rows, cols), bf16),),
        in_specs=[smem] + [anywhere] * (5 + len(operands)),
        out_specs=(anywhere,) * (len(results) + 1),
        scratch_shapes=[
            pltpu.VMEM((layers, 2, 2, pix, cols), bf16),
            pltpu.VMEM((layers, mine, 2, pix, pix), bf16),
            pltpu.VMEM((layers, mine, 2, pix, pix), bf16),
            pltpu.VMEM((mine, 4, pix, 2 * pix), bf16),
            pltpu.VMEM((mine, 4, 2 * pix, pix), bf16),
            pltpu.VMEM((mine, pix, pix), jnp.float32),
            pltpu.VMEM((2, layers, 2, pix, cols), bf16),
            pltpu.SemaphoreType.DMA((layers, 2)),
            pltpu.SemaphoreType.DMA((5, 2)),
            pltpu.SemaphoreType.DMA((2, layers)),
        ],
        compiler_params=pltpu.CompilerParams(vmem_limit_bytes=VMEM_LIMIT),
        cost_estimate=pl.CostEstimate(flops=15 * 10**9, bytes_accessed=16 * 2**20, transcendentals=0),
        name="waves",
    )(info, planes, *operands, lefts, rights, psi0, measured)

    wide = lambda v: v.astype(jnp.float32)
    kept = lambda s, which: wide(outs[6 * (s - 1) + 2 * which])
    twin = lambda s, which: wide(passed(outs[6 * (s - 1) + 2 * which + 1], "pos", 1))
    rims = {s: (kept(s, 0) + twin(s, 0)).astype(bf16) for s in steps}
    firsts = {s: (kept(s, 1) + twin(s, 1)).astype(bf16) for s in steps}
    lasts = {s: kept(s, 2) + twin(s, 2) for s in steps}
    back = {s: split_roles(rims[s], 1, -s, 1) for s in steps}
    come_first = sum(wide(split_roles(firsts[s], 1, -s, 0, s == 1)) for s in steps)
    summed = sum(wide(back[s]) for s in steps)
    lasts = {s: (lasts[s] + (jnp.where(core == 1, summed, wide(back[s])))).astype(bf16) for s in steps}
    come_last = sum(wide(split_roles(lasts[s], 1, -s, 0, s == 1)) for s in steps)
    on_first = jnp.where(core == 0, 1.0, 0.0)
    own_sum = wide(own_grads) + jnp.concatenate([come_first * on_first, come_first * (1.0 - on_first)])
    mine_of = lambda v: lax.dynamic_slice_in_dim(v, core * pix, pix, axis=3)
    twins_of = lambda v: lax.dynamic_slice_in_dim(v, (1 - core) * pix, pix, axis=3)
    early = mine_of(own_sum) + wide(passed(twins_of(own_sum).astype(bf16), "pos", 1))
    here = mine_of(come_last)
    away = wide(passed(twins_of(come_last).astype(bf16), "pos", 1))
    late = jnp.concatenate([jnp.where(core == 0, away, here), jnp.where(core == 0, here, away)])
    return (early + late).transpose(0, 2, 1, 3)


def solution(mesh):
    placed = (
        P(("grp", "slc"), "tile", None, None),
        P(None, ("grp", "tile", "pos")),
        P(("grp", "tile")),
        P(("grp", "tile", "pos"), None, None),
        P("grp", None),
    )
    return jax.shard_map(
        body,
        mesh=mesh,
        in_specs=placed,
        out_specs=P(("grp", "slc"), "tile", None, "pos"),
        check_vma=False,
    )
```

```python
import functools
import math

import jax
import jax.numpy as jnp
import ml_dtypes
import numpy as np
from jax import lax
from jax.experimental import pallas as pl
from jax.experimental.pallas import tpu as pltpu
from jax.sharding import PartitionSpec as P

VMEM_LIMIT = 58 * 1024 * 1024


def passed(array, axis, by):
    peers = lax.axis_size(axis)
    return lax.ppermute(array, axis, [(i, (i + by) % peers) for i in range(peers)])


def split_roles(array, tile_by, slc_by, slc_core, with_tile=True):
    tiles, groups, cores = (lax.axis_size(name) for name in ("tile", "slc", "pos"))
    at = lambda t, g, c: ((t % tiles) * groups + g % groups) * cores + c
    pairs = []
    for t in range(tiles):
        for g in range(groups):
            pairs.append((at(t, g, slc_core), at(t, g + slc_by, slc_core)))
            if with_tile:
                pairs.append((at(t, g, 1 - slc_core), at(t + tile_by, g, 1 - slc_core)))
    return lax.ppermute(array, ("tile", "slc", "pos"), pairs)


def base_tables(pix):
    index = np.arange(pix)
    angles = 2.0 * math.pi / pix * (np.outer(index, index) % pix)
    scale = 1.0 / math.sqrt(pix)
    rounded = lambda v: v.astype(np.float32).astype(ml_dtypes.bfloat16)
    wide = lambda v: rounded(v).astype(np.float64)
    w = wide(np.cos(angles) * scale) + 1j * wide(-np.sin(angles) * scale)
    freq = (index + pix // 2) % pix - pix // 2
    h = np.exp(-0.4j * math.pi / pix * (freq * freq))
    planes = []
    for factor in (np.ones_like(h), h, np.conj(h)):
        b = (factor[:, None] * w)[np.concatenate([index[::2], index[1::2]])]
        planes += [b.real, b.imag]
    stack = np.stack(planes)
    return rounded(np.stack([stack, stack.transpose(0, 2, 1)]))


def prep_kernel(mine, pix, info, base, probe, measured, lefts, rights, psi0, light):
    bf16, f32 = jnp.bfloat16, jnp.float32
    mid = pix // 2

    def rolled(side, f, shift, axis):
        found = []
        for part in range(2):
            whole = pltpu.roll(base[side, 2 * f + part].astype(f32), shift, axis)
            found.append(whole[:, :mid] if axis else whole[:mid])
        return found

    def put(ref, m, t, re, im, by_rows, from_left):
        for odd in range(2):
            at = slice(odd * mid, (odd + 1) * mid)
            re_part, im_part = (re[at], im[at]) if by_rows else (re[:, at], im[:, at])
            upper, lower = (-im_part, im_part) if from_left else (im_part, -im_part)
            ref[m, t, odd, :mid, :mid] = re_part.astype(bf16)
            ref[m, t, odd, :mid, mid:] = upper.astype(bf16)
            ref[m, t, odd, mid:, :mid] = lower.astype(bf16)
            ref[m, t, odd, mid:, mid:] = re_part.astype(bf16)

    row_at = lax.broadcasted_iota(jnp.int32, (pix, pix), 0)
    col_at = lax.broadcasted_iota(jnp.int32, (pix, pix), 1)
    order = lambda at: jnp.where(at < mid, 2 * at, 2 * at - (pix - 1))
    pick_rows = (col_at == order(row_at)).astype(f32).astype(bf16)
    pick_cols = (row_at == order(col_at)).astype(f32).astype(bf16)

    def exact(values, product):
        total = None
        for _ in range(3):
            term = values.astype(bf16)
            values = values - term.astype(f32)
            moved = product(term)
            total = moved if total is None else total + moved
        return total

    for m in range(mine):
        r0 = info[2 + 4 * m]
        c0 = info[4 + 4 * m]
        for t in range(3):
            put(lefts, m, t, *rolled(0, t, r0, 1), True, True)
            put(rights, m, t, *rolled(1, t, c0, 0), False, False)
        re, im = rolled(1, 0, r0, 0)
        put(lefts, m, 3, re, -im, False, True)
        re, im = rolled(0, 0, c0, 1)
        put(rights, m, 3, re, -im, True, False)
        for part in range(2):
            plane = probe[:, part * pix : (part + 1) * pix].astype(f32)
            plane = pltpu.roll(pltpu.roll(plane, r0, 0), c0, 1)
            psi0[m, part] = plane.astype(bf16)
        seen = measured[info[0] * mine + m]
        seen = exact(seen, lambda v: jnp.dot(pick_rows, v, preferred_element_type=f32))
        light[m] = exact(seen, lambda v: jnp.dot(v, pick_cols, preferred_element_type=f32))


def main_kernel(groups, depth, mine, pix, pieces, results, info, *refs):
    count = len(pieces) + 1
    own, operands = refs[0], refs[1:count]
    lefts_any, rights_any, psi0_any, light_any = refs[count : count + 4]
    outs = refs[count + 4 : count + 4 + len(results)]
    own_out = refs[count + 4 + len(results)]
    obj, tp, psi, lefts, rights, light, grads, sems, tab_sems, out_sems = refs[count + 5 + len(results) :]
    layers = groups * depth
    half = depth // 2
    rank = info[0]
    core = info[1]
    members = range(mine)

    def layer_of(s, i):
        group = lax.rem(rank - s + groups, groups)
        return group * depth + i

    def table_copies(t):
        return [
            pltpu.make_async_copy(lefts_any.at[:, t], lefts.at[:, t], tab_sems.at[t, 0]),
            pltpu.make_async_copy(rights_any.at[:, t], rights.at[:, t], tab_sems.at[t, 1]),
        ]

    def wait_tables(t):
        for copy in table_copies(t):
            copy.wait()

    psi_copy = pltpu.make_async_copy(psi0_any, psi.at[0], tab_sems.at[4, 0])
    light_copy = pltpu.make_async_copy(light_any, light, tab_sems.at[4, 1])
    psi_copy.start()
    for copy in table_copies(1) + table_copies(3):
        copy.start()
    for i in range(depth):
        j = layer_of(0, i)
        pltpu.make_async_copy(own.at[i], obj.at[j, 0], sems.at[j, 0]).start()
    for holds, ref in zip(pieces, operands):
        for c in range(2):
            if holds[c] is None:
                continue
            s, high, below = holds[c]

            @pl.when(core == c)
            def _():
                for i in range(half):
                    j = layer_of(s, high * half + i)
                    pltpu.make_async_copy(ref.at[i], obj.at[j, below], sems.at[j, below]).start()

    light_copy.start()
    for copy in table_copies(0) + table_copies(2):
        copy.start()

    def wait_object(j):
        for below in range(2):
            pltpu.make_async_copy(own.at[0], obj.at[j, below], sems.at[j, below]).wait()

    row_at = lax.broadcasted_iota(jnp.int32, (pix, pix), 0)
    col_at = lax.broadcasted_iota(jnp.int32, (pix, pix), 1)
    r0 = [info[2 + 4 * m] for m in members]
    q = [info[3 + 4 * m] for m in members]
    c0 = [info[4 + 4 * m] for m in members]
    live = [info[5 + 4 * m].astype(jnp.float32) for m in members]
    f32 = jnp.float32
    bf16 = jnp.bfloat16

    def patch(j, m, part):
        right = col_at >= c0[m]
        at = pl.ds(pl.multiple_of(q[m] * pix, pix), pix)
        after = pl.ds(pl.multiple_of((1 - q[m]) * pix, pix), pix)
        here = jnp.where(right, obj[j, 0, part, :, at].astype(f32), obj[j, 0, part, :, after].astype(f32))
        there = jnp.where(right, obj[j, 1, part, :, at].astype(f32), obj[j, 1, part, :, after].astype(f32))
        return jnp.where(row_at >= r0[m], here, there).astype(bf16)

    mid = pix // 2
    cat = lambda parts, axis: jnp.concatenate(parts, axis=axis)

    def product(a, b):
        return jnp.dot(a, b, preferred_element_type=f32)

    def spectrum_of(t, pairs):
        halfway = []
        for m, (re, im) in zip(members, pairs):
            plus = cat([re[:mid] + re[mid:], im[:mid] + im[mid:]], 0).astype(bf16)
            minus = cat([re[:mid] - re[mid:], im[:mid] - im[mid:]], 0).astype(bf16)
            halfway.append((product(lefts[m, t, 0], plus), product(lefts[m, t, 1], minus)))
        found = []
        for m, groups_of_rows in zip(members, halfway):
            plus = cat([cat([g[:mid, :mid] + g[:mid, mid:], g[mid:, :mid] + g[mid:, mid:]], 1) for g in groups_of_rows], 0)
            minus = cat([cat([g[:mid, :mid] - g[:mid, mid:], g[mid:, :mid] - g[mid:, mid:]], 1) for g in groups_of_rows], 0)
            found.append((product(plus.astype(bf16), rights[m, t, 0]), product(minus.astype(bf16), rights[m, t, 1])))
        return found

    def wave_of(spectra):
        halfway = []
        for m, (even, odd) in zip(members, spectra):
            even, odd = even.astype(bf16), odd.astype(bf16)
            terms = []
            for half_at in range(2):
                at = slice(half_at * mid, (half_at + 1) * mid)
                stacked = cat([cat([even[at, :mid], odd[at, :mid]], 1), cat([even[at, mid:], odd[at, mid:]], 1)], 0)
                terms.append(product(lefts[m, 3, half_at], stacked))
            halfway.append(((terms[0] + terms[1]).astype(bf16), (terms[0] - terms[1]).astype(bf16)))
        found = []
        for m, blocks in zip(members, halfway):
            terms = []
            for half_at in range(2):
                at = slice(half_at * mid, (half_at + 1) * mid)
                rows = cat([cat([b[:mid, at], b[mid:, at]], 1) for b in blocks], 0)
                terms.append(product(rows, rights[m, 3, half_at]))
            near, far = terms[0] + terms[1], terms[0] - terms[1]
            found.append((cat([near[:, :mid], far[:, :mid]], 1), cat([near[:, mid:], far[:, mid:]], 1)))
        return found

    def entrance(j):
        pairs = []
        for m in members:
            tr, ti = patch(j, m, 0), patch(j, m, 1)
            tp[j, m, 0] = tr
            tp[j, m, 1] = ti
            tr, ti = tr.astype(f32), ti.astype(f32)
            pr, pi = psi[j, m, 0].astype(f32), psi[j, m, 1].astype(f32)
            pairs.append((tr * pr - ti * pi, tr * pi + ti * pr))
        return pairs

    psi_copy.wait()
    wait_tables(1)
    wait_tables(3)

    def forward(j, carry):
        wait_object(j)
        spectra = spectrum_of(1, entrance(j))
        for m, (re, im) in enumerate(wave_of(spectra)):
            psi[j + 1, m, 0] = re.astype(bf16)
            psi[j + 1, m, 1] = im.astype(bf16)
        return carry

    lax.fori_loop(0, layers - 1, forward, 0)
    wait_object(layers - 1)
    wait_tables(0)
    light_copy.wait()
    spectra = spectrum_of(0, entrance(layers - 1))
    tilted = []
    for m, parts in enumerate(spectra):
        scaled = []
        for odd, values in enumerate(parts):
            re, im = values[:, :mid], values[:, mid:]
            excess = (re * re + im * im - light[m, :, odd * mid : (odd + 1) * mid]) * live[m]
            scaled.append(cat([excess * re, excess * im], 1))
        tilted.append(tuple(scaled))
    exits = wave_of(tilted)

    def out_copy(below, place, out):
        return pltpu.make_async_copy(grads.at[below, place], out, out_sems.at[below, place])

    def send_out(step, within):
        place = step * depth + within

        @pl.when(step == 0)
        def _():
            out_copy(0, place, own_out.at[within]).start()

        for takes, ref in zip(results, outs):
            for c in range(2):
                if takes[c] is None:
                    continue
                s, high, below = takes[c]
                inside = (within >= half) if high else (within < half)

                @pl.when((core == c) & (step == s) & inside)
                def _():
                    out_copy(below, place, ref.at[within - high * half]).start()

    def scatter(j, exits):
        step = lax.rem(rank - j // depth + groups, groups)
        within = lax.rem(j, depth)
        place = step * depth + within
        terms = []
        for m, (re, im) in enumerate(exits):
            pr, pi = psi[j, m, 0].astype(f32), psi[j, m, 1].astype(f32)
            terms.append((pr * re + pi * im, pr * im - pi * re))
        for below in range(2):
            for col in range(2):
                for part in range(2):
                    total = None
                    for m in members:
                        rows = (row_at < r0[m]) if below else (row_at >= r0[m])
                        low = jnp.where(q[m] == col, c0[m], 0)
                        high = jnp.where(q[m] == col, pix, c0[m])
                        mask = rows & (col_at >= low) & (col_at < high)
                        term = jnp.where(mask, terms[m][part], 0.0)
                        total = term if total is None else total + term
                    grads[below, place, part, :, col * pix : (col + 1) * pix] = total.astype(bf16)
        send_out(step, within)

    def wave_grads(j, exits):
        pairs = []
        for m, (re, im) in enumerate(exits):
            tr, ti = tp[j, m, 0].astype(f32), tp[j, m, 1].astype(f32)
            pairs.append((tr * re + ti * im, tr * im - ti * re))
        return pairs

    wait_tables(2)
    hold = tuple(part for pair in exits for part in pair)

    def backward(step, flat):
        j = layers - 1 - step
        exits = [(flat[2 * m], flat[2 * m + 1]) for m in members]
        scatter(j, exits)
        exits = wave_of(spectrum_of(2, wave_grads(j, exits)))
        return tuple(part for pair in exits for part in pair)

    hold = lax.fori_loop(0, layers - 1, backward, hold)
    scatter(0, [(hold[2 * m], hold[2 * m + 1]) for m in members])
    for below in range(2):
        for place in range(layers):
            out_copy(below, place, own_out.at[0]).wait()


def body(object_field, offsets, counts, measured, probe_wave):
    depth, rows, _, cols = object_field.shape
    pix = probe_wave.shape[0]
    slots_here = offsets.shape[1]
    groups = lax.axis_size("slc")
    rank = lax.axis_index("slc").astype(jnp.int32)
    tile = lax.axis_index("tile").astype(jnp.int32)
    core = lax.axis_index("pos").astype(jnp.int32)
    mine = slots_here // groups
    layers = groups * depth
    first = rank * mine
    bf16 = jnp.bfloat16

    off = lax.dynamic_slice(offsets, (jnp.int32(0), first), (2, mine))
    in_tile = core * slots_here + first + jnp.arange(mine, dtype=jnp.int32)
    alive = (in_tile < counts[0]).astype(jnp.int32)
    places = jnp.stack([off[0] - tile * rows, off[1] // pix, off[1] % pix, alive], axis=1)
    info = jnp.concatenate([jnp.stack([rank, core]), places.reshape(-1)])

    planes = object_field.transpose(0, 2, 1, 3)
    half = depth // 2
    steps = range(1, groups)
    halves_of = lambda high: lax.dynamic_slice_in_dim(planes, high * half, half, axis=0)
    first_half, last_half = halves_of(core), halves_of(1 - core)
    got_first = [split_roles(first_half, -1, s, 0, s == 1) for s in steps]
    got_last = [split_roles(last_half, -1, s, 0, s == 1) for s in steps]

    smem = pl.BlockSpec(memory_space=pltpu.SMEM)
    vmem = pl.BlockSpec(memory_space=pltpu.VMEM)
    anywhere = pl.BlockSpec(memory_space=pl.ANY)
    tables_shape = jax.ShapeDtypeStruct((mine, 4, 2, pix, pix), bf16)
    lefts, rights, psi0, light = pl.pallas_call(
        functools.partial(prep_kernel, mine, pix),
        out_shape=(
            tables_shape,
            tables_shape,
            jax.ShapeDtypeStruct((mine, 2, pix, pix), bf16),
            jax.ShapeDtypeStruct((mine, pix, pix), jnp.float32),
        ),
        in_specs=[smem, vmem, vmem, vmem],
        out_specs=(vmem,) * 4,
        compiler_params=pltpu.CompilerParams(vmem_limit_bytes=VMEM_LIMIT),
        cost_estimate=pl.CostEstimate(flops=8 * 10**9, bytes_accessed=8 * 2**20, transcendentals=0),
        name="tables",
    )(info, jnp.asarray(base_tables(pix)), probe_wave, measured)

    got_first, lefts, rights, psi0, light = lax.optimization_barrier(
        (got_first, lefts, rights, psi0, light)
    )
    passed_on = [split_roles(got_first[s - 1], -1, s, 1) for s in steps]
    pieces, operands = [], []
    for s in steps:
        rim_hi, rim_lo = ((0, 1, 1), (0, 0, 1)) if s == 1 else (None, None)
        for array, holds in (
            (got_first[s - 1], ((s, 0, 0), rim_hi)),
            (got_last[s - 1], ((s, 1, 0), rim_lo)),
            (passed_on[s - 1], ((s, 0, 1), (s, 1, 1))),
        ):
            pieces += [holds, holds[::-1]]
            operands += [array, passed(array, "pos", 1)]
    results = []
    for s in steps:
        rim_hi, rim_lo = ((0, 1, 1), (0, 0, 1)) if s == 1 else (None, None)
        for holds in (((s, 1, 1), (s, 0, 1)), ((s, 0, 0), rim_hi), ((s, 1, 0), rim_lo)):
            results += [holds, holds[::-1]]

    half_shape = jax.ShapeDtypeStruct((half, 2, rows, cols), bf16)
    *outs, own_grads = pl.pallas_call(
        functools.partial(main_kernel, groups, depth, mine, pix, tuple(pieces), tuple(results)),
        out_shape=(half_shape,) * len(results) + (jax.ShapeDtypeStruct((depth, 2, rows, cols), bf16),),
        in_specs=[smem] + [anywhere] * (5 + len(operands)),
        out_specs=(anywhere,) * (len(results) + 1),
        scratch_shapes=[
            pltpu.VMEM((layers, 2, 2, pix, cols), bf16),
            pltpu.VMEM((layers, mine, 2, pix, pix), bf16),
            pltpu.VMEM((layers, mine, 2, pix, pix), bf16),
            pltpu.VMEM((mine, 4, 2, pix, pix), bf16),
            pltpu.VMEM((mine, 4, 2, pix, pix), bf16),
            pltpu.VMEM((mine, pix, pix), jnp.float32),
            pltpu.VMEM((2, layers, 2, pix, cols), bf16),
            pltpu.SemaphoreType.DMA((layers, 2)),
            pltpu.SemaphoreType.DMA((5, 2)),
            pltpu.SemaphoreType.DMA((2, layers)),
        ],
        compiler_params=pltpu.CompilerParams(vmem_limit_bytes=VMEM_LIMIT),
        cost_estimate=pl.CostEstimate(flops=15 * 10**9, bytes_accessed=16 * 2**20, transcendentals=0),
        name="waves",
    )(info, planes, *operands, lefts, rights, psi0, light)

    wide = lambda v: v.astype(jnp.float32)
    kept = lambda s, which: wide(outs[6 * (s - 1) + 2 * which])
    twin = lambda s, which: wide(passed(outs[6 * (s - 1) + 2 * which + 1], "pos", 1))
    rims = {s: (kept(s, 0) + twin(s, 0)).astype(bf16) for s in steps}
    firsts = {s: (kept(s, 1) + twin(s, 1)).astype(bf16) for s in steps}
    lasts = {s: kept(s, 2) + twin(s, 2) for s in steps}
    back = {s: split_roles(rims[s], 1, -s, 1) for s in steps}
    come_first = sum(wide(split_roles(firsts[s], 1, -s, 0, s == 1)) for s in steps)
    summed = sum(wide(back[s]) for s in steps)
    lasts = {s: (lasts[s] + (jnp.where(core == 1, summed, wide(back[s])))).astype(bf16) for s in steps}
    come_last = sum(wide(split_roles(lasts[s], 1, -s, 0, s == 1)) for s in steps)
    on_first = jnp.where(core == 0, 1.0, 0.0)
    own_sum = wide(own_grads) + jnp.concatenate([come_first * on_first, come_first * (1.0 - on_first)])
    mine_of = lambda v: lax.dynamic_slice_in_dim(v, core * pix, pix, axis=3)
    twins_of = lambda v: lax.dynamic_slice_in_dim(v, (1 - core) * pix, pix, axis=3)
    early = mine_of(own_sum) + wide(passed(twins_of(own_sum).astype(bf16), "pos", 1))
    here = mine_of(come_last)
    away = wide(passed(twins_of(come_last).astype(bf16), "pos", 1))
    late = jnp.concatenate([jnp.where(core == 0, away, here), jnp.where(core == 0, here, away)])
    return (early + late).transpose(0, 2, 1, 3)


def solution(mesh):
    placed = (
        P(("grp", "slc"), "tile", None, None),
        P(None, ("grp", "tile", "pos")),
        P(("grp", "tile")),
        P(("grp", "tile", "pos"), None, None),
        P("grp", None),
    )
    return jax.shard_map(
        body,
        mesh=mesh,
        in_specs=placed,
        out_specs=P(("grp", "slc"), "tile", None, "pos"),
        check_vma=False,
    )
```

```python
import functools
import math

import jax
import jax.numpy as jnp
import ml_dtypes
import numpy as np
from jax import lax
from jax.experimental import pallas as pl
from jax.experimental.pallas import tpu as pltpu
from jax.sharding import PartitionSpec as P

VMEM_LIMIT = 58 * 1024 * 1024


def passed(array, axis, by):
    peers = lax.axis_size(axis)
    return lax.ppermute(array, axis, [(i, (i + by) % peers) for i in range(peers)])


def split_roles(array, tile_by, slc_by, slc_core, with_tile=True):
    tiles, groups, cores = (lax.axis_size(name) for name in ("tile", "slc", "pos"))
    at = lambda t, g, c: ((t % tiles) * groups + g % groups) * cores + c
    pairs = []
    for t in range(tiles):
        for g in range(groups):
            pairs.append((at(t, g, slc_core), at(t, g + slc_by, slc_core)))
            if with_tile:
                pairs.append((at(t, g, 1 - slc_core), at(t + tile_by, g, 1 - slc_core)))
    return lax.ppermute(array, ("tile", "slc", "pos"), pairs)


def base_tables(pix):
    index = np.arange(pix)
    angles = 2.0 * math.pi / pix * (np.outer(index, index) % pix)
    scale = 1.0 / math.sqrt(pix)
    rounded = lambda v: v.astype(np.float32).astype(ml_dtypes.bfloat16)
    wide = lambda v: rounded(v).astype(np.float64)
    w = wide(np.cos(angles) * scale) + 1j * wide(-np.sin(angles) * scale)
    freq = (index + pix // 2) % pix - pix // 2
    h = np.exp(-0.4j * math.pi / pix * (freq * freq))
    planes = []
    for factor in (np.ones_like(h), h, np.conj(h)):
        b = (factor[:, None] * w)[np.concatenate([index[::2], index[1::2]])]
        planes += [b.real, b.imag]
    stack = np.stack(planes)
    return rounded(np.stack([stack, stack.transpose(0, 2, 1)]))


def table_kernel(mine, pix, info, base, lefts, rights):
    bf16, f32 = jnp.bfloat16, jnp.float32
    mid = pix // 2

    def rolled(side, f, shift, axis):
        found = []
        for part in range(2):
            whole = pltpu.roll(base[side, 2 * f + part].astype(f32), shift, axis)
            found.append(whole[:, :mid] if axis else whole[:mid])
        return found

    def put(ref, m, t, re, im, by_rows, from_left):
        for odd in range(2):
            at = slice(odd * mid, (odd + 1) * mid)
            re_part, im_part = (re[at], im[at]) if by_rows else (re[:, at], im[:, at])
            upper, lower = (-im_part, im_part) if from_left else (im_part, -im_part)
            ref[m, t, odd, :mid, :mid] = re_part.astype(bf16)
            ref[m, t, odd, :mid, mid:] = upper.astype(bf16)
            ref[m, t, odd, mid:, :mid] = lower.astype(bf16)
            ref[m, t, odd, mid:, mid:] = re_part.astype(bf16)

    for m in range(mine):
        r0 = info[2 + 4 * m]
        c0 = info[4 + 4 * m]
        for t in range(3):
            put(lefts, m, t, *rolled(0, t, r0, 1), True, True)
            put(rights, m, t, *rolled(1, t, c0, 0), False, False)
        re, im = rolled(1, 0, r0, 0)
        put(lefts, m, 3, re, -im, False, True)
        re, im = rolled(0, 0, c0, 1)
        put(rights, m, 3, re, -im, True, False)


def slot_kernel(mine, pix, info, probe, measured, psi0, light):
    bf16, f32 = jnp.bfloat16, jnp.float32
    mid = pix // 2
    row_at = lax.broadcasted_iota(jnp.int32, (pix, pix), 0)
    col_at = lax.broadcasted_iota(jnp.int32, (pix, pix), 1)
    order = lambda at: jnp.where(at < mid, 2 * at, 2 * at - (pix - 1))
    pick_rows = (col_at == order(row_at)).astype(f32).astype(bf16)
    pick_cols = (row_at == order(col_at)).astype(f32).astype(bf16)

    def exact(values, product):
        total = None
        for _ in range(3):
            term = values.astype(bf16)
            values = values - term.astype(f32)
            moved = product(term)
            total = moved if total is None else total + moved
        return total

    for m in range(mine):
        r0 = info[2 + 4 * m]
        c0 = info[4 + 4 * m]
        for part in range(2):
            plane = probe[:, part * pix : (part + 1) * pix].astype(f32)
            plane = pltpu.roll(pltpu.roll(plane, r0, 0), c0, 1)
            psi0[m, part] = plane.astype(bf16)
        seen = measured[info[0] * mine + m]
        seen = exact(seen, lambda v: jnp.dot(pick_rows, v, preferred_element_type=f32))
        light[m] = exact(seen, lambda v: jnp.dot(v, pick_cols, preferred_element_type=f32))


def main_kernel(groups, depth, mine, pix, pieces, results, info, *refs):
    count = len(pieces) + 1
    own, operands = refs[0], refs[1:count]
    lefts_any, rights_any, psi0_any, light_any = refs[count : count + 4]
    outs = refs[count + 4 : count + 4 + len(results)]
    own_keep, own_send = refs[count + 4 + len(results) : count + 6 + len(results)]
    obj, tp, psi, lefts, rights, light, grads, sems, tab_sems, out_sems = refs[count + 6 + len(results) :]
    layers = groups * depth
    half = depth // 2
    rank = info[0]
    core = info[1]
    members = range(mine)

    def layer_of(s, i):
        group = lax.rem(rank - s + groups, groups)
        return group * depth + i

    def table_copies(t):
        return [
            pltpu.make_async_copy(lefts_any.at[:, t], lefts.at[:, t], tab_sems.at[t, 0]),
            pltpu.make_async_copy(rights_any.at[:, t], rights.at[:, t], tab_sems.at[t, 1]),
        ]

    def wait_tables(t):
        for copy in table_copies(t):
            copy.wait()

    psi_copy = pltpu.make_async_copy(psi0_any, psi.at[0], tab_sems.at[4, 0])
    light_copy = pltpu.make_async_copy(light_any, light, tab_sems.at[4, 1])
    psi_copy.start()
    for copy in table_copies(1) + table_copies(3):
        copy.start()
    for i in range(depth):
        j = layer_of(0, i)
        pltpu.make_async_copy(own.at[i], obj.at[j, 0], sems.at[j, 0]).start()
    for holds, ref in zip(pieces, operands):
        for c in range(2):
            if holds[c] is None:
                continue
            s, high, below = holds[c]

            @pl.when(core == c)
            def _():
                for i in range(half):
                    j = layer_of(s, high * half + i)
                    pltpu.make_async_copy(ref.at[i], obj.at[j, below], sems.at[j, below]).start()

    light_copy.start()
    for copy in table_copies(0) + table_copies(2):
        copy.start()

    def wait_object(j):
        for below in range(2):
            pltpu.make_async_copy(own.at[0], obj.at[j, below], sems.at[j, below]).wait()

    row_at = lax.broadcasted_iota(jnp.int32, (pix, pix), 0)
    col_at = lax.broadcasted_iota(jnp.int32, (pix, pix), 1)
    r0 = [info[2 + 4 * m] for m in members]
    q = [info[3 + 4 * m] for m in members]
    c0 = [info[4 + 4 * m] for m in members]
    live = [info[5 + 4 * m].astype(jnp.float32) for m in members]
    f32 = jnp.float32
    bf16 = jnp.bfloat16

    def patch(j, m, part):
        right = col_at >= c0[m]
        at = pl.ds(pl.multiple_of(q[m] * pix, pix), pix)
        after = pl.ds(pl.multiple_of((1 - q[m]) * pix, pix), pix)
        here = jnp.where(right, obj[j, 0, part, :, at].astype(f32), obj[j, 0, part, :, after].astype(f32))
        there = jnp.where(right, obj[j, 1, part, :, at].astype(f32), obj[j, 1, part, :, after].astype(f32))
        return jnp.where(row_at >= r0[m], here, there).astype(bf16)

    mid = pix // 2
    cat = lambda parts, axis: jnp.concatenate(parts, axis=axis)

    def product(a, b):
        return jnp.dot(a, b, preferred_element_type=f32)

    def spectrum_of(t, pairs):
        halfway = []
        for m, (re, im) in zip(members, pairs):
            plus = cat([re[:mid] + re[mid:], im[:mid] + im[mid:]], 0).astype(bf16)
            minus = cat([re[:mid] - re[mid:], im[:mid] - im[mid:]], 0).astype(bf16)
            halfway.append((product(lefts[m, t, 0], plus), product(lefts[m, t, 1], minus)))
        found = []
        for m, groups_of_rows in zip(members, halfway):
            plus = cat([cat([g[:mid, :mid] + g[:mid, mid:], g[mid:, :mid] + g[mid:, mid:]], 1) for g in groups_of_rows], 0)
            minus = cat([cat([g[:mid, :mid] - g[:mid, mid:], g[mid:, :mid] - g[mid:, mid:]], 1) for g in groups_of_rows], 0)
            found.append((product(plus.astype(bf16), rights[m, t, 0]), product(minus.astype(bf16), rights[m, t, 1])))
        return found

    def wave_of(spectra):
        halfway = []
        for m, (even, odd) in zip(members, spectra):
            even, odd = even.astype(bf16), odd.astype(bf16)
            terms = []
            for half_at in range(2):
                at = slice(half_at * mid, (half_at + 1) * mid)
                stacked = cat([cat([even[at, :mid], odd[at, :mid]], 1), cat([even[at, mid:], odd[at, mid:]], 1)], 0)
                terms.append(product(lefts[m, 3, half_at], stacked))
            halfway.append(((terms[0] + terms[1]).astype(bf16), (terms[0] - terms[1]).astype(bf16)))
        found = []
        for m, blocks in zip(members, halfway):
            terms = []
            for half_at in range(2):
                at = slice(half_at * mid, (half_at + 1) * mid)
                rows = cat([cat([b[:mid, at], b[mid:, at]], 1) for b in blocks], 0)
                terms.append(product(rows, rights[m, 3, half_at]))
            near, far = terms[0] + terms[1], terms[0] - terms[1]
            found.append((cat([near[:, :mid], far[:, :mid]], 1), cat([near[:, mid:], far[:, mid:]], 1)))
        return found

    def entrance(j):
        pairs = []
        for m in members:
            tr, ti = patch(j, m, 0), patch(j, m, 1)
            tp[j, m, 0] = tr
            tp[j, m, 1] = ti
            tr, ti = tr.astype(f32), ti.astype(f32)
            pr, pi = psi[j, m, 0].astype(f32), psi[j, m, 1].astype(f32)
            pairs.append((tr * pr - ti * pi, tr * pi + ti * pr))
        return pairs

    psi_copy.wait()
    wait_tables(1)
    wait_tables(3)

    def forward(j, carry):
        wait_object(j)
        spectra = spectrum_of(1, entrance(j))
        for m, (re, im) in enumerate(wave_of(spectra)):
            psi[j + 1, m, 0] = re.astype(bf16)
            psi[j + 1, m, 1] = im.astype(bf16)
        return carry

    lax.fori_loop(0, layers - 1, forward, 0)
    wait_object(layers - 1)
    wait_tables(0)
    light_copy.wait()
    spectra = spectrum_of(0, entrance(layers - 1))
    tilted = []
    for m, parts in enumerate(spectra):
        scaled = []
        for odd, values in enumerate(parts):
            re, im = values[:, :mid], values[:, mid:]
            excess = (re * re + im * im - light[m, :, odd * mid : (odd + 1) * mid]) * live[m]
            scaled.append(cat([excess * re, excess * im], 1))
        tilted.append(tuple(scaled))
    exits = wave_of(tilted)

    def out_copy(below, place, out):
        return pltpu.make_async_copy(grads.at[below, place], out, out_sems.at[below, place])

    def own_copies(i):
        copies = []
        for away, out in enumerate((own_keep, own_send)):
            at = pl.multiple_of(((1 - core) if away else core) * pix, pix)
            columns = grads.at[0, i, :, :, pl.ds(at, pix)]
            copies.append(pltpu.make_async_copy(columns, out.at[i], out_sems.at[2 * away, i]))
        return copies

    def send_out(step, within):
        place = step * depth + within

        @pl.when(step == 0)
        def _():
            for copy in own_copies(within):
                copy.start()

        for takes, ref in zip(results, outs):
            for c in range(2):
                if takes[c] is None:
                    continue
                s, high, below = takes[c]
                inside = (within >= half) if high else (within < half)

                @pl.when((core == c) & (step == s) & inside)
                def _():
                    out_copy(below, place, ref.at[within - high * half]).start()

    def scatter(j, exits):
        step = lax.rem(rank - j // depth + groups, groups)
        within = lax.rem(j, depth)
        place = step * depth + within
        terms = []
        for m, (re, im) in enumerate(exits):
            pr, pi = psi[j, m, 0].astype(f32), psi[j, m, 1].astype(f32)
            terms.append((pr * re + pi * im, pr * im - pi * re))
        for part in range(2):
            total = [[None, None], [None, None]]
            for m in members:
                value = terms[m][part]
                after = jnp.where(col_at >= c0[m], value, 0.0)
                before = value - after
                by_col = [jnp.where(q[m] == 0, after, before), jnp.where(q[m] == 0, before, after)]
                for col in range(2):
                    below = jnp.where(row_at < r0[m], by_col[col], 0.0)
                    for row_block, found in ((0, by_col[col] - below), (1, below)):
                        so_far = total[row_block][col]
                        total[row_block][col] = found if so_far is None else so_far + found
            for row_block in range(2):
                for col in range(2):
                    values = total[row_block][col].astype(bf16)
                    grads[row_block, place, part, :, col * pix : (col + 1) * pix] = values
        send_out(step, within)

    def wave_grads(j, exits):
        pairs = []
        for m, (re, im) in enumerate(exits):
            tr, ti = tp[j, m, 0].astype(f32), tp[j, m, 1].astype(f32)
            pairs.append((tr * re + ti * im, tr * im - ti * re))
        return pairs

    wait_tables(2)
    hold = tuple(part for pair in exits for part in pair)

    def backward(step, flat):
        j = layers - 1 - step
        exits = [(flat[2 * m], flat[2 * m + 1]) for m in members]
        scatter(j, exits)
        exits = wave_of(spectrum_of(2, wave_grads(j, exits)))
        return tuple(part for pair in exits for part in pair)

    hold = lax.fori_loop(0, layers - 1, backward, hold)
    scatter(0, [(hold[2 * m], hold[2 * m + 1]) for m in members])
    for below in range(2):
        for place in range(0 if below else depth, layers):
            out_copy(below, place, outs[0].at[0]).wait()
    for i in range(depth):
        for copy in own_copies(i):
            copy.wait()


def body(object_field, offsets, counts, measured, probe_wave):
    depth, rows, _, cols = object_field.shape
    pix = probe_wave.shape[0]
    slots_here = offsets.shape[1]
    groups = lax.axis_size("slc")
    rank = lax.axis_index("slc").astype(jnp.int32)
    tile = lax.axis_index("tile").astype(jnp.int32)
    core = lax.axis_index("pos").astype(jnp.int32)
    mine = slots_here // groups
    layers = groups * depth
    first = rank * mine
    bf16 = jnp.bfloat16

    off = lax.dynamic_slice(offsets, (jnp.int32(0), first), (2, mine))
    in_tile = core * slots_here + first + jnp.arange(mine, dtype=jnp.int32)
    alive = (in_tile < counts[0]).astype(jnp.int32)
    places = jnp.stack([off[0] - tile * rows, off[1] // pix, off[1] % pix, alive], axis=1)
    info = jnp.concatenate([jnp.stack([rank, core]), places.reshape(-1)])

    planes = object_field.transpose(0, 2, 1, 3)
    half = depth // 2
    steps = range(1, groups)
    halves_of = lambda high: lax.dynamic_slice_in_dim(planes, high * half, half, axis=0)
    first_half, last_half = halves_of(core), halves_of(1 - core)
    smem = pl.BlockSpec(memory_space=pltpu.SMEM)
    vmem = pl.BlockSpec(memory_space=pltpu.VMEM)
    anywhere = pl.BlockSpec(memory_space=pl.ANY)
    tables_shape = jax.ShapeDtypeStruct((mine, 4, 2, pix, pix), bf16)
    params = pltpu.CompilerParams(vmem_limit_bytes=VMEM_LIMIT)
    lefts, rights = pl.pallas_call(
        functools.partial(table_kernel, mine, pix),
        out_shape=(tables_shape, tables_shape),
        in_specs=[smem, vmem],
        out_specs=(vmem, vmem),
        compiler_params=params,
        cost_estimate=pl.CostEstimate(flops=5 * 10**9, bytes_accessed=8 * 2**20, transcendentals=0),
        name="tables",
    )(info, jnp.asarray(base_tables(pix)))
    psi0, light = pl.pallas_call(
        functools.partial(slot_kernel, mine, pix),
        out_shape=(
            jax.ShapeDtypeStruct((mine, 2, pix, pix), bf16),
            jax.ShapeDtypeStruct((mine, pix, pix), jnp.float32),
        ),
        in_specs=[smem, vmem, vmem],
        out_specs=(vmem, vmem),
        compiler_params=params,
        cost_estimate=pl.CostEstimate(flops=2 * 10**9, bytes_accessed=2 * 2**20, transcendentals=0),
        name="slots",
    )(info, probe_wave, measured)

    got_first = [split_roles(first_half, -1, s, 0, s == 1) for s in steps]
    last_half, lefts, rights = lax.optimization_barrier((last_half, lefts, rights))
    got_last = [split_roles(last_half, -1, s, 0, s == 1) for s in steps]
    passed_on = [split_roles(got_first[s - 1], -1, s, 1) for s in steps]
    got_last, psi0, light = lax.optimization_barrier((got_last, psi0, light))
    pieces, operands = [], []
    for s in steps:
        rim_hi, rim_lo = ((0, 1, 1), (0, 0, 1)) if s == 1 else (None, None)
        for array, holds in (
            (got_first[s - 1], ((s, 0, 0), rim_hi)),
            (got_last[s - 1], ((s, 1, 0), rim_lo)),
            (passed_on[s - 1], ((s, 0, 1), (s, 1, 1))),
        ):
            pieces += [holds, holds[::-1]]
            operands += [array, passed(array, "pos", 1)]
    results = []
    for s in steps:
        rim_hi, rim_lo = ((0, 1, 1), (0, 0, 1)) if s == 1 else (None, None)
        for holds in (((s, 1, 1), (s, 0, 1)), ((s, 0, 0), rim_hi), ((s, 1, 0), rim_lo)):
            results += [holds, holds[::-1]]

    half_shape = jax.ShapeDtypeStruct((half, 2, rows, cols), bf16)
    *outs, own_keep, own_send = pl.pallas_call(
        functools.partial(main_kernel, groups, depth, mine, pix, tuple(pieces), tuple(results)),
        out_shape=(half_shape,) * len(results) + (jax.ShapeDtypeStruct((depth, 2, rows, pix), bf16),) * 2,
        in_specs=[smem] + [anywhere] * (5 + len(operands)),
        out_specs=(anywhere,) * (len(results) + 2),
        scratch_shapes=[
            pltpu.VMEM((layers, 2, 2, pix, cols), bf16),
            pltpu.VMEM((layers, mine, 2, pix, pix), bf16),
            pltpu.VMEM((layers, mine, 2, pix, pix), bf16),
            pltpu.VMEM((mine, 4, 2, pix, pix), bf16),
            pltpu.VMEM((mine, 4, 2, pix, pix), bf16),
            pltpu.VMEM((mine, pix, pix), jnp.float32),
            pltpu.VMEM((2, layers, 2, pix, cols), bf16),
            pltpu.SemaphoreType.DMA((layers, 2)),
            pltpu.SemaphoreType.DMA((5, 2)),
            pltpu.SemaphoreType.DMA((3, layers)),
        ],
        compiler_params=pltpu.CompilerParams(vmem_limit_bytes=VMEM_LIMIT),
        cost_estimate=pl.CostEstimate(flops=15 * 10**9, bytes_accessed=16 * 2**20, transcendentals=0),
        name="waves",
    )(info, planes, *operands, lefts, rights, psi0, light)

    wide = lambda v: v.astype(jnp.float32)
    kept = lambda s, which: wide(outs[6 * (s - 1) + 2 * which])
    twin = lambda s, which: wide(passed(outs[6 * (s - 1) + 2 * which + 1], "pos", 1))
    rims = {s: (kept(s, 0) + twin(s, 0)).astype(bf16) for s in steps}
    back = {s: split_roles(rims[s], 1, -s, 1) for s in steps}
    firsts = {s: (kept(s, 1) + twin(s, 1)).astype(bf16) for s in steps}
    lasts = {s: kept(s, 2) + twin(s, 2) for s in steps}
    early = (wide(own_keep) + wide(passed(own_send, "pos", 1))).transpose(0, 2, 1, 3)
    back, firsts, lasts = lax.optimization_barrier((back, firsts, lasts))
    come_first = [split_roles(firsts[s], 1, -s, 0, s == 1) for s in steps]
    summed = sum(wide(back[s]) for s in steps)
    lasts = {s: (lasts[s] + jnp.where(core == 1, summed, wide(back[s]))).astype(bf16) for s in steps}
    come_last = [split_roles(lasts[s], 1, -s, 0, s == 1) for s in steps]
    come_first, early = lax.optimization_barrier((come_first, early))
    come_first = sum(map(wide, come_first)).astype(bf16)
    come_last = sum(map(wide, come_last)).astype(bf16)
    mine_of = lambda v: lax.dynamic_slice_in_dim(v, core * pix, pix, axis=3)
    twins_of = lambda v: lax.dynamic_slice_in_dim(v, (1 - core) * pix, pix, axis=3)
    in_place = lambda v: v.transpose(0, 2, 1, 3)
    here_first, here_last = in_place(mine_of(come_first)), in_place(mine_of(come_last))
    away_first = in_place(passed(twins_of(come_first), "pos", 1))
    away_last = in_place(passed(twins_of(come_last), "pos", 1))
    one = wide(here_first) + wide(away_last)
    other = wide(here_last) + wide(away_first)
    late = jnp.concatenate([jnp.where(core == 0, one, other), jnp.where(core == 0, other, one)])
    return early + late


def solution(mesh):
    placed = (
        P(("grp", "slc"), "tile", None, None),
        P(None, ("grp", "tile", "pos")),
        P(("grp", "tile")),
        P(("grp", "tile", "pos"), None, None),
        P("grp", None),
    )
    return jax.shard_map(
        body,
        mesh=mesh,
        in_specs=placed,
        out_specs=P(("grp", "slc"), "tile", None, "pos"),
        check_vma=False,
    )
```

```python
import functools
import math

import jax
import jax.numpy as jnp
import ml_dtypes
import numpy as np
from jax import lax
from jax.experimental import pallas as pl
from jax.experimental.pallas import tpu as pltpu
from jax.sharding import PartitionSpec as P

VMEM_LIMIT = 38 * 1024 * 1024


def passed(array, axis, by):
    peers = lax.axis_size(axis)
    return lax.ppermute(array, axis, [(i, (i + by) % peers) for i in range(peers)])


def split_roles(array, tile_by, slc_by, slc_core, with_tile=True):
    tiles, groups, cores = (lax.axis_size(name) for name in ("tile", "slc", "pos"))
    at = lambda t, g, c: ((t % tiles) * groups + g % groups) * cores + c
    pairs = []
    for t in range(tiles):
        for g in range(groups):
            pairs.append((at(t, g, slc_core), at(t, g + slc_by, slc_core)))
            if with_tile:
                pairs.append((at(t, g, 1 - slc_core), at(t + tile_by, g, 1 - slc_core)))
    return lax.ppermute(array, ("tile", "slc", "pos"), pairs)


def base_tables(pix):
    index = np.arange(pix)
    angles = 2.0 * math.pi / pix * (np.outer(index, index) % pix)
    scale = 1.0 / math.sqrt(pix)
    rounded = lambda v: v.astype(np.float32).astype(ml_dtypes.bfloat16)
    wide = lambda v: rounded(v).astype(np.float64)
    w = wide(np.cos(angles) * scale) + 1j * wide(-np.sin(angles) * scale)
    freq = (index + pix // 2) % pix - pix // 2
    h = np.exp(-0.4j * math.pi / pix * (freq * freq))
    planes = []
    for factor in (np.ones_like(h), h, np.conj(h)):
        b = (factor[:, None] * w)[np.concatenate([index[::2], index[1::2]])]
        planes += [b.real, b.imag]
    stack = np.stack(planes)
    return rounded(np.stack([stack, stack.transpose(0, 2, 1)]))


def prep_kernel(mine, pix, info, base, probe, measured, lefts, rights, psi0, light, masks):
    bf16, f32 = jnp.bfloat16, jnp.float32
    mid = pix // 2

    def rolled(side, f, shift, axis):
        found = []
        for part in range(2):
            whole = pltpu.roll(base[side, 2 * f + part].astype(f32), shift, axis)
            found.append(whole[:, :mid] if axis else whole[:mid])
        return found

    def put(ref, m, t, re, im, by_rows, from_left):
        for odd in range(2):
            at = slice(odd * mid, (odd + 1) * mid)
            re_part, im_part = (re[at], im[at]) if by_rows else (re[:, at], im[:, at])
            upper, lower = (-im_part, im_part) if from_left else (im_part, -im_part)
            ref[m, t, odd, :mid, :mid] = re_part.astype(bf16)
            ref[m, t, odd, :mid, mid:] = upper.astype(bf16)
            ref[m, t, odd, mid:, :mid] = lower.astype(bf16)
            ref[m, t, odd, mid:, mid:] = re_part.astype(bf16)

    row_at = lax.broadcasted_iota(jnp.int32, (pix, pix), 0)
    col_at = lax.broadcasted_iota(jnp.int32, (pix, pix), 1)
    order = lambda at: jnp.where(at < mid, 2 * at, 2 * at - (pix - 1))
    pick_rows = (col_at == order(row_at)).astype(f32).astype(bf16)
    pick_cols = (row_at == order(col_at)).astype(f32).astype(bf16)

    def exact(values, product):
        total = None
        for _ in range(3):
            term = values.astype(bf16)
            values = values - term.astype(f32)
            moved = product(term)
            total = moved if total is None else total + moved
        return total

    for m in range(mine):
        r0 = info[2 + 4 * m]
        c0 = info[4 + 4 * m]
        for t in range(3):
            put(lefts, m, t, *rolled(0, t, r0, 1), True, True)
            put(rights, m, t, *rolled(1, t, c0, 0), False, False)
        re, im = rolled(1, 0, r0, 0)
        put(lefts, m, 3, re, -im, False, True)
        re, im = rolled(0, 0, c0, 1)
        put(rights, m, 3, re, -im, True, False)
        for part in range(2):
            plane = probe[:, part * pix : (part + 1) * pix].astype(f32)
            plane = pltpu.roll(pltpu.roll(plane, r0, 0), c0, 1)
            psi0[m, part] = plane.astype(bf16)
        for below in range(2):
            rows = (row_at < r0) if below else (row_at >= r0)
            for col in range(2):
                low = jnp.where(info[3 + 4 * m] == col, c0, 0)
                high = jnp.where(info[3 + 4 * m] == col, pix, c0)
                inside = rows & (col_at >= low) & (col_at < high)
                masks[m, below, col] = jnp.where(inside, 1.0, 0.0).astype(bf16)
        seen = measured[info[0] * mine + m]
        seen = exact(seen, lambda v: jnp.dot(pick_rows, v, preferred_element_type=f32))
        light[m] = exact(seen, lambda v: jnp.dot(v, pick_cols, preferred_element_type=f32))


def main_kernel(groups, depth, mine, pix, pieces, results, info, *refs):
    count = len(pieces) + 1
    own, operands = refs[0], refs[1:count]
    lefts_any, rights_any, psi0_any, light_any, masks_any = refs[count : count + 5]
    outs = refs[count + 5 : count + 5 + len(results)]
    own_out = refs[count + 5 + len(results)]
    obj, tp, psi, lefts, rights, light, masks, grads, sems, tab_sems, out_sems = refs[count + 6 + len(results) :]
    layers = groups * depth
    half = depth // 2
    rank = info[0]
    core = info[1]
    members = range(mine)

    def layer_of(s, i):
        group = lax.rem(rank - s + groups, groups)
        return group * depth + i

    def table_copies(t):
        return [
            pltpu.make_async_copy(lefts_any.at[:, t], lefts.at[:, t], tab_sems.at[t, 0]),
            pltpu.make_async_copy(rights_any.at[:, t], rights.at[:, t], tab_sems.at[t, 1]),
        ]

    def wait_tables(t):
        for copy in table_copies(t):
            copy.wait()

    psi_copy = pltpu.make_async_copy(psi0_any, psi.at[0], tab_sems.at[4, 0])
    light_copy = pltpu.make_async_copy(light_any, light, tab_sems.at[4, 1])
    mask_copy = pltpu.make_async_copy(masks_any, masks, tab_sems.at[5, 0])
    psi_copy.start()
    mask_copy.start()
    for copy in table_copies(1) + table_copies(3):
        copy.start()
    for i in range(depth):
        j = layer_of(0, i)
        pltpu.make_async_copy(own.at[i], obj.at[j, 0], sems.at[j, 0]).start()
    for holds, ref in zip(pieces, operands):
        for c in range(2):
            if holds[c] is None:
                continue
            s, high, below = holds[c]

            @pl.when(core == c)
            def _():
                for i in range(half):
                    j = layer_of(s, high * half + i)
                    pltpu.make_async_copy(ref.at[i], obj.at[j, below], sems.at[j, below]).start()

    light_copy.start()
    for copy in table_copies(0) + table_copies(2):
        copy.start()

    def wait_object(j):
        for below in range(2):
            pltpu.make_async_copy(own.at[0], obj.at[j, below], sems.at[j, below]).wait()

    live = [info[5 + 4 * m].astype(jnp.float32) for m in members]
    f32 = jnp.float32
    bf16 = jnp.bfloat16

    def patch(j, m, part):
        total = None
        for below in range(2):
            for col in range(2):
                term = obj[j, below, part, :, col * pix : (col + 1) * pix] * masks[m, below, col]
                total = term if total is None else total + term
        return total

    mid = pix // 2
    cat = lambda parts, axis: jnp.concatenate(parts, axis=axis)

    def product(a, b):
        return jnp.dot(a, b, preferred_element_type=f32)

    def spectrum_of(t, pairs):
        halfway = []
        for m, (re, im) in zip(members, pairs):
            plus = cat([re[:mid] + re[mid:], im[:mid] + im[mid:]], 0).astype(bf16)
            minus = cat([re[:mid] - re[mid:], im[:mid] - im[mid:]], 0).astype(bf16)
            halfway.append((product(lefts[m, t, 0], plus), product(lefts[m, t, 1], minus)))
        found = []
        for m, groups_of_rows in zip(members, halfway):
            plus = cat([cat([g[:mid, :mid] + g[:mid, mid:], g[mid:, :mid] + g[mid:, mid:]], 1) for g in groups_of_rows], 0)
            minus = cat([cat([g[:mid, :mid] - g[:mid, mid:], g[mid:, :mid] - g[mid:, mid:]], 1) for g in groups_of_rows], 0)
            found.append((product(plus.astype(bf16), rights[m, t, 0]), product(minus.astype(bf16), rights[m, t, 1])))
        return found

    def wave_of(spectra):
        halfway = []
        for m, (even, odd) in zip(members, spectra):
            even, odd = even.astype(bf16), odd.astype(bf16)
            terms = []
            for half_at in range(2):
                at = slice(half_at * mid, (half_at + 1) * mid)
                stacked = cat([cat([even[at, :mid], odd[at, :mid]], 1), cat([even[at, mid:], odd[at, mid:]], 1)], 0)
                terms.append(product(lefts[m, 3, half_at], stacked))
            halfway.append(((terms[0] + terms[1]).astype(bf16), (terms[0] - terms[1]).astype(bf16)))
        found = []
        for m, blocks in zip(members, halfway):
            terms = []
            for half_at in range(2):
                at = slice(half_at * mid, (half_at + 1) * mid)
                rows = cat([cat([b[:mid, at], b[mid:, at]], 1) for b in blocks], 0)
                terms.append(product(rows, rights[m, 3, half_at]))
            near, far = terms[0] + terms[1], terms[0] - terms[1]
            found.append((cat([near[:, :mid], far[:, :mid]], 1), cat([near[:, mid:], far[:, mid:]], 1)))
        return found

    def entrance(j):
        pairs = []
        for m in members:
            tr, ti = patch(j, m, 0), patch(j, m, 1)
            tp[j, m, 0] = tr
            tp[j, m, 1] = ti
            pr, pi = psi[j, m, 0], psi[j, m, 1]
            pairs.append(((tr * pr - ti * pi).astype(f32), (tr * pi + ti * pr).astype(f32)))
        return pairs

    psi_copy.wait()
    mask_copy.wait()
    wait_tables(1)
    wait_tables(3)

    def forward(j, carry):
        wait_object(j)
        spectra = spectrum_of(1, entrance(j))
        for m, (re, im) in enumerate(wave_of(spectra)):
            psi[j + 1, m, 0] = re.astype(bf16)
            psi[j + 1, m, 1] = im.astype(bf16)
        return carry

    lax.fori_loop(0, layers - 1, forward, 0)
    wait_object(layers - 1)
    wait_tables(0)
    light_copy.wait()
    spectra = spectrum_of(0, entrance(layers - 1))
    tilted = []
    for m, parts in enumerate(spectra):
        scaled = []
        for odd, values in enumerate(parts):
            re, im = values[:, :mid], values[:, mid:]
            excess = (re * re + im * im - light[m, :, odd * mid : (odd + 1) * mid]) * live[m]
            scaled.append(cat([excess * re, excess * im], 1))
        tilted.append(tuple(scaled))
    exits = wave_of(tilted)

    def out_copy(below, place, out):
        return pltpu.make_async_copy(grads.at[below, place], out, out_sems.at[below, place])

    def send_out(step, within):
        place = step * depth + within

        @pl.when(step == 0)
        def _():
            out_copy(0, place, own_out.at[within]).start()

        for takes, ref in zip(results, outs):
            for c in range(2):
                if takes[c] is None:
                    continue
                s, high, below = takes[c]
                inside = (within >= half) if high else (within < half)

                @pl.when((core == c) & (step == s) & inside)
                def _():
                    out_copy(below, place, ref.at[within - high * half]).start()

    def scatter(j, exits):
        step = lax.rem(rank - j // depth + groups, groups)
        within = lax.rem(j, depth)
        place = step * depth + within
        terms = []
        for m, (re, im) in enumerate(exits):
            re, im = re.astype(bf16), im.astype(bf16)
            pr, pi = psi[j, m, 0], psi[j, m, 1]
            terms.append((pr * re + pi * im, pr * im - pi * re))
        for below in range(2):
            for col in range(2):
                for part in range(2):
                    total = None
                    for m in members:
                        term = terms[m][part] * masks[m, below, col]
                        total = term if total is None else total + term
                    grads[below, place, part, :, col * pix : (col + 1) * pix] = total
        send_out(step, within)

    def wave_grads(j, exits):
        pairs = []
        for m, (re, im) in enumerate(exits):
            re, im = re.astype(bf16), im.astype(bf16)
            tr, ti = tp[j, m, 0], tp[j, m, 1]
            pairs.append(((tr * re + ti * im).astype(f32), (tr * im - ti * re).astype(f32)))
        return pairs

    wait_tables(2)
    hold = tuple(part for pair in exits for part in pair)

    def backward(step, flat):
        j = layers - 1 - step
        exits = [(flat[2 * m], flat[2 * m + 1]) for m in members]
        scatter(j, exits)
        exits = wave_of(spectrum_of(2, wave_grads(j, exits)))
        return tuple(part for pair in exits for part in pair)

    hold = lax.fori_loop(0, layers - 1, backward, hold)
    scatter(0, [(hold[2 * m], hold[2 * m + 1]) for m in members])
    for below in range(2):
        for place in range(layers):
            out_copy(below, place, own_out.at[0]).wait()


def body(object_field, offsets, counts, measured, probe_wave):
    depth, rows, _, cols = object_field.shape
    pix = probe_wave.shape[0]
    slots_here = offsets.shape[1]
    groups = lax.axis_size("slc")
    rank = lax.axis_index("slc").astype(jnp.int32)
    tile = lax.axis_index("tile").astype(jnp.int32)
    core = lax.axis_index("pos").astype(jnp.int32)
    mine = slots_here // groups
    layers = groups * depth
    first = rank * mine
    bf16 = jnp.bfloat16

    off = lax.dynamic_slice(offsets, (jnp.int32(0), first), (2, mine))
    in_tile = core * slots_here + first + jnp.arange(mine, dtype=jnp.int32)
    alive = (in_tile < counts[0]).astype(jnp.int32)
    places = jnp.stack([off[0] - tile * rows, off[1] // pix, off[1] % pix, alive], axis=1)
    info = jnp.concatenate([jnp.stack([rank, core]), places.reshape(-1)])

    planes = object_field.transpose(0, 2, 1, 3)
    half = depth // 2
    steps = range(1, groups)
    halves_of = lambda high: lax.dynamic_slice_in_dim(planes, high * half, half, axis=0)
    first_half, last_half = halves_of(core), halves_of(1 - core)
    got_first = [split_roles(first_half, -1, s, 0, s == 1) for s in steps]
    got_last = [split_roles(last_half, -1, s, 0, s == 1) for s in steps]

    smem = pl.BlockSpec(memory_space=pltpu.SMEM)
    vmem = pl.BlockSpec(memory_space=pltpu.VMEM)
    anywhere = pl.BlockSpec(memory_space=pl.ANY)
    tables_shape = jax.ShapeDtypeStruct((mine, 4, 2, pix, pix), bf16)
    lefts, rights, psi0, light, masks = pl.pallas_call(
        functools.partial(prep_kernel, mine, pix),
        out_shape=(
            tables_shape,
            tables_shape,
            jax.ShapeDtypeStruct((mine, 2, pix, pix), bf16),
            jax.ShapeDtypeStruct((mine, pix, pix), jnp.float32),
            jax.ShapeDtypeStruct((mine, 2, 2, pix, pix), bf16),
        ),
        in_specs=[smem, vmem, vmem, vmem],
        out_specs=(vmem,) * 5,
        compiler_params=pltpu.CompilerParams(vmem_limit_bytes=VMEM_LIMIT),
        cost_estimate=pl.CostEstimate(flops=8 * 10**9, bytes_accessed=8 * 2**20, transcendentals=0),
        name="tables",
    )(info, jnp.asarray(base_tables(pix)), probe_wave, measured)

    got_first, lefts, rights, psi0, light, masks = lax.optimization_barrier(
        (got_first, lefts, rights, psi0, light, masks)
    )
    passed_on = [split_roles(got_first[s - 1], -1, s, 1) for s in steps]
    pieces, operands = [], []
    for s in steps:
        rim_hi, rim_lo = ((0, 1, 1), (0, 0, 1)) if s == 1 else (None, None)
        for array, holds in (
            (got_first[s - 1], ((s, 0, 0), rim_hi)),
            (got_last[s - 1], ((s, 1, 0), rim_lo)),
            (passed_on[s - 1], ((s, 0, 1), (s, 1, 1))),
        ):
            pieces += [holds, holds[::-1]]
            operands += [array, passed(array, "pos", 1)]
    results = []
    for s in steps:
        rim_hi, rim_lo = ((0, 1, 1), (0, 0, 1)) if s == 1 else (None, None)
        for holds in (((s, 1, 1), (s, 0, 1)), ((s, 0, 0), rim_hi), ((s, 1, 0), rim_lo)):
            results += [holds, holds[::-1]]

    half_shape = jax.ShapeDtypeStruct((half, 2, rows, cols), bf16)
    *outs, own_grads = pl.pallas_call(
        functools.partial(main_kernel, groups, depth, mine, pix, tuple(pieces), tuple(results)),
        out_shape=(half_shape,) * len(results) + (jax.ShapeDtypeStruct((depth, 2, rows, cols), bf16),),
        in_specs=[smem] + [anywhere] * (6 + len(operands)),
        out_specs=(anywhere,) * (len(results) + 1),
        scratch_shapes=[
            pltpu.VMEM((layers, 2, 2, pix, cols), bf16),
            pltpu.VMEM((layers, mine, 2, pix, pix), bf16),
            pltpu.VMEM((layers, mine, 2, pix, pix), bf16),
            pltpu.VMEM((mine, 4, 2, pix, pix), bf16),
            pltpu.VMEM((mine, 4, 2, pix, pix), bf16),
            pltpu.VMEM((mine, pix, pix), jnp.float32),
            pltpu.VMEM((mine, 2, 2, pix, pix), bf16),
            pltpu.VMEM((2, layers, 2, pix, cols), bf16),
            pltpu.SemaphoreType.DMA((layers, 2)),
            pltpu.SemaphoreType.DMA((6, 2)),
            pltpu.SemaphoreType.DMA((2, layers)),
        ],
        compiler_params=pltpu.CompilerParams(vmem_limit_bytes=VMEM_LIMIT),
        cost_estimate=pl.CostEstimate(flops=15 * 10**9, bytes_accessed=16 * 2**20, transcendentals=0),
        name="waves",
    )(info, planes, *operands, lefts, rights, psi0, light, masks)

    wide = lambda v: v.astype(jnp.float32)
    kept = lambda s, which: wide(outs[6 * (s - 1) + 2 * which])
    twin = lambda s, which: wide(passed(outs[6 * (s - 1) + 2 * which + 1], "pos", 1))
    rims = {s: (kept(s, 0) + twin(s, 0)).astype(bf16) for s in steps}
    firsts = {s: (kept(s, 1) + twin(s, 1)).astype(bf16) for s in steps}
    lasts = {s: kept(s, 2) + twin(s, 2) for s in steps}
    back = {s: split_roles(rims[s], 1, -s, 1) for s in steps}
    come_first = sum(wide(split_roles(firsts[s], 1, -s, 0, s == 1)) for s in steps)
    summed = sum(wide(back[s]) for s in steps)
    lasts = {s: (lasts[s] + (jnp.where(core == 1, summed, wide(back[s])))).astype(bf16) for s in steps}
    come_last = sum(wide(split_roles(lasts[s], 1, -s, 0, s == 1)) for s in steps)
    on_first = jnp.where(core == 0, 1.0, 0.0)
    own_sum = wide(own_grads) + jnp.concatenate([come_first * on_first, come_first * (1.0 - on_first)])
    mine_of = lambda v: lax.dynamic_slice_in_dim(v, core * pix, pix, axis=3)
    twins_of = lambda v: lax.dynamic_slice_in_dim(v, (1 - core) * pix, pix, axis=3)
    early = mine_of(own_sum) + wide(passed(twins_of(own_sum).astype(bf16), "pos", 1))
    here = mine_of(come_last)
    away = wide(passed(twins_of(come_last).astype(bf16), "pos", 1))
    late = jnp.concatenate([jnp.where(core == 0, away, here), jnp.where(core == 0, here, away)])
    return (early + late).transpose(0, 2, 1, 3)


def solution(mesh):
    placed = (
        P(("grp", "slc"), "tile", None, None),
        P(None, ("grp", "tile", "pos")),
        P(("grp", "tile")),
        P(("grp", "tile", "pos"), None, None),
        P("grp", None),
    )
    return jax.shard_map(
        body,
        mesh=mesh,
        in_specs=placed,
        out_specs=P(("grp", "slc"), "tile", None, "pos"),
        check_vma=False,
    )
```

```python
import functools
import math

import jax
import jax.numpy as jnp
import ml_dtypes
import numpy as np
from jax import lax
from jax.experimental import pallas as pl
from jax.experimental.pallas import tpu as pltpu
from jax.sharding import PartitionSpec as P

VMEM_LIMIT = 38 * 1024 * 1024


def passed(array, axis, by):
    peers = lax.axis_size(axis)
    return lax.ppermute(array, axis, [(i, (i + by) % peers) for i in range(peers)])


def split_roles(array, tile_by, slc_by, slc_core, with_tile=True):
    tiles, groups, cores = (lax.axis_size(name) for name in ("tile", "slc", "pos"))
    at = lambda t, g, c: ((t % tiles) * groups + g % groups) * cores + c
    pairs = []
    for t in range(tiles):
        for g in range(groups):
            pairs.append((at(t, g, slc_core), at(t, g + slc_by, slc_core)))
            if with_tile:
                pairs.append((at(t, g, 1 - slc_core), at(t + tile_by, g, 1 - slc_core)))
    return lax.ppermute(array, ("tile", "slc", "pos"), pairs)


def base_tables(pix):
    index = np.arange(pix)
    angles = 2.0 * math.pi / pix * (np.outer(index, index) % pix)
    scale = 1.0 / math.sqrt(pix)
    rounded = lambda v: v.astype(np.float32).astype(ml_dtypes.bfloat16)
    wide = lambda v: rounded(v).astype(np.float64)
    w = wide(np.cos(angles) * scale) + 1j * wide(-np.sin(angles) * scale)
    freq = (index + pix // 2) % pix - pix // 2
    h = np.exp(-0.4j * math.pi / pix * (freq * freq))
    planes = []
    for factor in (np.ones_like(h), h, np.conj(h)):
        b = (factor[:, None] * w)[np.concatenate([index[::2], index[1::2]])]
        planes += [b.real, b.imag]
    stack = np.stack(planes)
    return rounded(np.stack([stack, stack.transpose(0, 2, 1)]))


def prep_kernel(mine, pix, info, base, probe, measured, lefts, rights, psi0, light, masks):
    bf16, f32 = jnp.bfloat16, jnp.float32
    mid = pix // 2

    def rolled(side, f, shift, axis):
        found = []
        for part in range(2):
            whole = pltpu.roll(base[side, 2 * f + part].astype(f32), shift, axis)
            found.append(whole[:, :mid] if axis else whole[:mid])
        return found

    def put(ref, m, t, re, im, by_rows, from_left):
        for odd in range(2):
            at = slice(odd * mid, (odd + 1) * mid)
            re_part, im_part = (re[at], im[at]) if by_rows else (re[:, at], im[:, at])
            upper, lower = (-im_part, im_part) if from_left else (im_part, -im_part)
            ref[m, t, odd, :mid, :mid] = re_part.astype(bf16)
            ref[m, t, odd, :mid, mid:] = upper.astype(bf16)
            ref[m, t, odd, mid:, :mid] = lower.astype(bf16)
            ref[m, t, odd, mid:, mid:] = re_part.astype(bf16)

    row_at = lax.broadcasted_iota(jnp.int32, (pix, pix), 0)
    col_at = lax.broadcasted_iota(jnp.int32, (pix, pix), 1)
    order = lambda at: jnp.where(at < mid, 2 * at, 2 * at - (pix - 1))
    pick_rows = (col_at == order(row_at)).astype(f32).astype(bf16)
    pick_cols = (row_at == order(col_at)).astype(f32).astype(bf16)

    def exact(values, product):
        total = None
        for _ in range(3):
            term = values.astype(bf16)
            values = values - term.astype(f32)
            moved = product(term)
            total = moved if total is None else total + moved
        return total

    for m in range(mine):
        r0 = info[2 + 4 * m]
        c0 = info[4 + 4 * m]
        for t in range(3):
            put(lefts, m, t, *rolled(0, t, r0, 1), True, True)
            put(rights, m, t, *rolled(1, t, c0, 0), False, False)
        re, im = rolled(1, 0, r0, 0)
        put(lefts, m, 3, re, -im, False, True)
        re, im = rolled(0, 0, c0, 1)
        put(rights, m, 3, re, -im, True, False)
        for part in range(2):
            plane = probe[:, part * pix : (part + 1) * pix].astype(f32)
            plane = pltpu.roll(pltpu.roll(plane, r0, 0), c0, 1)
            psi0[m, part] = plane.astype(bf16)
        for below in range(2):
            rows = (row_at < r0) if below else (row_at >= r0)
            for col in range(2):
                low = jnp.where(info[3 + 4 * m] == col, c0, 0)
                high = jnp.where(info[3 + 4 * m] == col, pix, c0)
                inside = rows & (col_at >= low) & (col_at < high)
                masks[m, below, col] = jnp.where(inside, 1.0, 0.0).astype(bf16)
        seen = measured[info[0] * mine + m]
        seen = exact(seen, lambda v: jnp.dot(pick_rows, v, preferred_element_type=f32))
        light[m] = exact(seen, lambda v: jnp.dot(v, pick_cols, preferred_element_type=f32))


def main_kernel(groups, depth, mine, pix, pieces, info, *refs):
    count = len(pieces) + 1
    own, operands = refs[0], refs[1:count]
    lefts_any, rights_any, psi0_any, light_any, masks_any = refs[count : count + 5]
    outs = refs[count + 5 : count + 5 + 4 * groups]
    obj, tp, psi, lefts, rights, light, masks, grads, sems, tab_sems, out_sems = refs[count + 5 + 4 * groups :]
    layers = groups * depth
    half = depth // 2
    rank = info[0]
    core = info[1]
    members = range(mine)

    def layer_of(s, i):
        group = lax.rem(rank - s + groups, groups)
        return group * depth + i

    def table_copies(t):
        return [
            pltpu.make_async_copy(lefts_any.at[:, t], lefts.at[:, t], tab_sems.at[t, 0]),
            pltpu.make_async_copy(rights_any.at[:, t], rights.at[:, t], tab_sems.at[t, 1]),
        ]

    def wait_tables(t):
        for copy in table_copies(t):
            copy.wait()

    psi_copy = pltpu.make_async_copy(psi0_any, psi.at[0], tab_sems.at[4, 0])
    light_copy = pltpu.make_async_copy(light_any, light, tab_sems.at[4, 1])
    mask_copy = pltpu.make_async_copy(masks_any, masks, tab_sems.at[5, 0])
    psi_copy.start()
    mask_copy.start()
    for copy in table_copies(1) + table_copies(3):
        copy.start()
    for i in range(depth):
        j = layer_of(0, i)
        pltpu.make_async_copy(own.at[i], obj.at[j, 0], sems.at[j, 0]).start()
    for holds, ref in zip(pieces, operands):
        for c in range(2):
            if holds[c] is None:
                continue
            s, high, below = holds[c]

            @pl.when(core == c)
            def _():
                for i in range(half):
                    j = layer_of(s, high * half + i)
                    pltpu.make_async_copy(ref.at[i], obj.at[j, below], sems.at[j, below]).start()

    light_copy.start()
    for copy in table_copies(0) + table_copies(2):
        copy.start()

    def wait_object(j):
        for below in range(2):
            pltpu.make_async_copy(own.at[0], obj.at[j, below], sems.at[j, below]).wait()

    live = [info[5 + 4 * m].astype(jnp.float32) for m in members]
    f32 = jnp.float32
    bf16 = jnp.bfloat16

    def patch(j, m, part):
        total = None
        for below in range(2):
            for col in range(2):
                term = obj[j, below, part, :, col * pix : (col + 1) * pix] * masks[m, below, col]
                total = term if total is None else total + term
        return total

    mid = pix // 2
    cat = lambda parts, axis: jnp.concatenate(parts, axis=axis)

    def product(a, b):
        return jnp.dot(a, b, preferred_element_type=f32)

    def spectrum_of(t, pairs):
        halfway = []
        for m, (re, im) in zip(members, pairs):
            plus = cat([re[:mid] + re[mid:], im[:mid] + im[mid:]], 0).astype(bf16)
            minus = cat([re[:mid] - re[mid:], im[:mid] - im[mid:]], 0).astype(bf16)
            halfway.append((product(lefts[m, t, 0], plus), product(lefts[m, t, 1], minus)))
        found = []
        for m, groups_of_rows in zip(members, halfway):
            plus = cat([cat([g[:mid, :mid] + g[:mid, mid:], g[mid:, :mid] + g[mid:, mid:]], 1) for g in groups_of_rows], 0)
            minus = cat([cat([g[:mid, :mid] - g[:mid, mid:], g[mid:, :mid] - g[mid:, mid:]], 1) for g in groups_of_rows], 0)
            found.append((product(plus.astype(bf16), rights[m, t, 0]), product(minus.astype(bf16), rights[m, t, 1])))
        return found

    def wave_of(spectra):
        halfway = []
        for m, (even, odd) in zip(members, spectra):
            even, odd = even.astype(bf16), odd.astype(bf16)
            terms = []
            for half_at in range(2):
                at = slice(half_at * mid, (half_at + 1) * mid)
                stacked = cat([cat([even[at, :mid], odd[at, :mid]], 1), cat([even[at, mid:], odd[at, mid:]], 1)], 0)
                terms.append(product(lefts[m, 3, half_at], stacked))
            halfway.append(((terms[0] + terms[1]).astype(bf16), (terms[0] - terms[1]).astype(bf16)))
        found = []
        for m, blocks in zip(members, halfway):
            terms = []
            for half_at in range(2):
                at = slice(half_at * mid, (half_at + 1) * mid)
                rows = cat([cat([b[:mid, at], b[mid:, at]], 1) for b in blocks], 0)
                terms.append(product(rows, rights[m, 3, half_at]))
            near, far = terms[0] + terms[1], terms[0] - terms[1]
            found.append((cat([near[:, :mid], far[:, :mid]], 1), cat([near[:, mid:], far[:, mid:]], 1)))
        return found

    def entrance(j):
        pairs = []
        for m in members:
            tr, ti = patch(j, m, 0), patch(j, m, 1)
            tp[j, m, 0] = tr
            tp[j, m, 1] = ti
            pr, pi = psi[j, m, 0], psi[j, m, 1]
            pairs.append(((tr * pr - ti * pi).astype(f32), (tr * pi + ti * pr).astype(f32)))
        return pairs

    psi_copy.wait()
    mask_copy.wait()
    wait_tables(1)
    wait_tables(3)

    def forward(j, carry):
        wait_object(j)
        spectra = spectrum_of(1, entrance(j))
        for m, (re, im) in enumerate(wave_of(spectra)):
            psi[j + 1, m, 0] = re.astype(bf16)
            psi[j + 1, m, 1] = im.astype(bf16)
        return carry

    lax.fori_loop(0, layers - 1, forward, 0)
    wait_object(layers - 1)
    wait_tables(0)
    light_copy.wait()
    spectra = spectrum_of(0, entrance(layers - 1))
    tilted = []
    for m, parts in enumerate(spectra):
        scaled = []
        for odd, values in enumerate(parts):
            re, im = values[:, :mid], values[:, mid:]
            excess = (re * re + im * im - light[m, :, odd * mid : (odd + 1) * mid]) * live[m]
            scaled.append(cat([excess * re, excess * im], 1))
        tilted.append(tuple(scaled))
    exits = wave_of(tilted)

    def out_copies(s, i):
        place = s * depth + i
        copies = []
        for away in range(2):
            at = pl.multiple_of(((1 - core) if away else core) * pix, pix)
            for below in range(2):
                out = outs[(away * 2 + below) * groups + s]
                columns = grads.at[below, place, :, :, pl.ds(at, pix)]
                copies.append(pltpu.make_async_copy(columns, out.at[i], out_sems.at[away * 2 + below, place]))
        return copies

    def send_out(step, within):
        for s in range(groups):

            @pl.when(step == s)
            def _():
                for copy in out_copies(s, within):
                    copy.start()

    def scatter(j, exits):
        step = lax.rem(rank - j // depth + groups, groups)
        within = lax.rem(j, depth)
        place = step * depth + within
        terms = []
        for m, (re, im) in enumerate(exits):
            re, im = re.astype(bf16), im.astype(bf16)
            pr, pi = psi[j, m, 0], psi[j, m, 1]
            terms.append((pr * re + pi * im, pr * im - pi * re))
        for below in range(2):
            for col in range(2):
                for part in range(2):
                    total = None
                    for m in members:
                        term = terms[m][part] * masks[m, below, col]
                        total = term if total is None else total + term
                    grads[below, place, part, :, col * pix : (col + 1) * pix] = total
        send_out(step, within)

    def wave_grads(j, exits):
        pairs = []
        for m, (re, im) in enumerate(exits):
            re, im = re.astype(bf16), im.astype(bf16)
            tr, ti = tp[j, m, 0], tp[j, m, 1]
            pairs.append(((tr * re + ti * im).astype(f32), (tr * im - ti * re).astype(f32)))
        return pairs

    wait_tables(2)
    hold = tuple(part for pair in exits for part in pair)

    def backward(step, flat):
        j = layers - 1 - step
        exits = [(flat[2 * m], flat[2 * m + 1]) for m in members]
        scatter(j, exits)
        exits = wave_of(spectrum_of(2, wave_grads(j, exits)))
        return tuple(part for pair in exits for part in pair)

    hold = lax.fori_loop(0, layers - 1, backward, hold)
    scatter(0, [(hold[2 * m], hold[2 * m + 1]) for m in members])
    for s in range(groups):
        for i in range(depth):
            for copy in out_copies(s, i):
                copy.wait()


def body(object_field, offsets, counts, measured, probe_wave):
    depth, rows, _, cols = object_field.shape
    pix = probe_wave.shape[0]
    slots_here = offsets.shape[1]
    groups = lax.axis_size("slc")
    rank = lax.axis_index("slc").astype(jnp.int32)
    tile = lax.axis_index("tile").astype(jnp.int32)
    core = lax.axis_index("pos").astype(jnp.int32)
    mine = slots_here // groups
    layers = groups * depth
    first = rank * mine
    bf16 = jnp.bfloat16

    off = lax.dynamic_slice(offsets, (jnp.int32(0), first), (2, mine))
    in_tile = core * slots_here + first + jnp.arange(mine, dtype=jnp.int32)
    alive = (in_tile < counts[0]).astype(jnp.int32)
    places = jnp.stack([off[0] - tile * rows, off[1] // pix, off[1] % pix, alive], axis=1)
    info = jnp.concatenate([jnp.stack([rank, core]), places.reshape(-1)])

    planes = object_field.transpose(0, 2, 1, 3)
    half = depth // 2
    steps = range(1, groups)
    halves_of = lambda high: lax.dynamic_slice_in_dim(planes, high * half, half, axis=0)
    first_half, last_half = halves_of(core), halves_of(1 - core)
    got_first = [split_roles(first_half, -1, s, 0, s == 1) for s in steps]
    got_last = [split_roles(last_half, -1, s, 0, s == 1) for s in steps]

    smem = pl.BlockSpec(memory_space=pltpu.SMEM)
    vmem = pl.BlockSpec(memory_space=pltpu.VMEM)
    anywhere = pl.BlockSpec(memory_space=pl.ANY)
    tables_shape = jax.ShapeDtypeStruct((mine, 4, 2, pix, pix), bf16)
    lefts, rights, psi0, light, masks = pl.pallas_call(
        functools.partial(prep_kernel, mine, pix),
        out_shape=(
            tables_shape,
            tables_shape,
            jax.ShapeDtypeStruct((mine, 2, pix, pix), bf16),
            jax.ShapeDtypeStruct((mine, pix, pix), jnp.float32),
            jax.ShapeDtypeStruct((mine, 2, 2, pix, pix), bf16),
        ),
        in_specs=[smem, vmem, vmem, vmem],
        out_specs=(vmem,) * 5,
        compiler_params=pltpu.CompilerParams(vmem_limit_bytes=VMEM_LIMIT),
        cost_estimate=pl.CostEstimate(flops=8 * 10**9, bytes_accessed=8 * 2**20, transcendentals=0),
        name="tables",
    )(info, jnp.asarray(base_tables(pix)), probe_wave, measured)

    got_first, lefts, rights, psi0, light, masks = lax.optimization_barrier(
        (got_first, lefts, rights, psi0, light, masks)
    )
    passed_on = [split_roles(got_first[s - 1], -1, s, 1) for s in steps]
    pieces, operands = [], []
    for s in steps:
        rim_hi, rim_lo = ((0, 1, 1), (0, 0, 1)) if s == 1 else (None, None)
        for array, holds in (
            (got_first[s - 1], ((s, 0, 0), rim_hi)),
            (got_last[s - 1], ((s, 1, 0), rim_lo)),
            (passed_on[s - 1], ((s, 0, 1), (s, 1, 1))),
        ):
            pieces += [holds, holds[::-1]]
            operands += [array, passed(array, "pos", 1)]

    outs = pl.pallas_call(
        functools.partial(main_kernel, groups, depth, mine, pix, tuple(pieces)),
        out_shape=(jax.ShapeDtypeStruct((depth, 2, rows, pix), bf16),) * (4 * groups),
        in_specs=[smem] + [anywhere] * (6 + len(operands)),
        out_specs=(anywhere,) * (4 * groups),
        scratch_shapes=[
            pltpu.VMEM((layers, 2, 2, pix, cols), bf16),
            pltpu.VMEM((layers, mine, 2, pix, pix), bf16),
            pltpu.VMEM((layers, mine, 2, pix, pix), bf16),
            pltpu.VMEM((mine, 4, 2, pix, pix), bf16),
            pltpu.VMEM((mine, 4, 2, pix, pix), bf16),
            pltpu.VMEM((mine, pix, pix), jnp.float32),
            pltpu.VMEM((mine, 2, 2, pix, pix), bf16),
            pltpu.VMEM((2, layers, 2, pix, cols), bf16),
            pltpu.SemaphoreType.DMA((layers, 2)),
            pltpu.SemaphoreType.DMA((6, 2)),
            pltpu.SemaphoreType.DMA((4, layers)),
        ],
        compiler_params=pltpu.CompilerParams(vmem_limit_bytes=VMEM_LIMIT),
        cost_estimate=pl.CostEstimate(flops=15 * 10**9, bytes_accessed=16 * 2**20, transcendentals=0),
        name="waves",
    )(info, planes, *operands, lefts, rights, psi0, light, masks)

    wide = lambda v: v.astype(jnp.float32)
    sums = {}
    for s in [*steps, 0]:
        for row_block in (1, 0):
            at = row_block * groups + s
            sums[row_block, s] = wide(outs[at]) + wide(passed(outs[2 * groups + at], "pos", 1))
    rim_lo = sums[1, 0][:half]
    rim_hi = sums[1, 0][half:].astype(bf16)
    tile_lo = sums[0, 0][:half]
    tile_hi = sums[0, 0][half:]
    for s in steps:
        rim, tile_part = sums[1, s], sums[0, s]
        rim_lo += wide(passed(rim[:half].astype(bf16), "slc", -s))
        other_hi = tile_part[half:] + wide(passed(rim[half:].astype(bf16), "tile", 1))
        tile_lo += wide(passed(tile_part[:half].astype(bf16), "slc", -s))
        tile_hi += wide(passed(other_hi.astype(bf16), "slc", -s))
    tile_hi += wide(passed(rim_hi, "tile", 1))
    tile_lo += wide(passed(rim_lo.astype(bf16), "tile", 1))
    return jnp.concatenate([tile_lo, tile_hi]).transpose(0, 2, 1, 3)


def solution(mesh):
    placed = (
        P(("grp", "slc"), "tile", None, None),
        P(None, ("grp", "tile", "pos")),
        P(("grp", "tile")),
        P(("grp", "tile", "pos"), None, None),
        P("grp", None),
    )
    return jax.shard_map(
        body,
        mesh=mesh,
        in_specs=placed,
        out_specs=P(("grp", "slc"), "tile", None, "pos"),
        check_vma=False,
    )
```

```python
import functools
import math

import jax
import jax.numpy as jnp
import ml_dtypes
import numpy as np
from jax import lax
from jax.experimental import pallas as pl
from jax.experimental.pallas import tpu as pltpu
from jax.sharding import PartitionSpec as P

VMEM_LIMIT = 38 * 1024 * 1024


def passed(array, axis, by):
    peers = lax.axis_size(axis)
    return lax.ppermute(array, axis, [(i, (i + by) % peers) for i in range(peers)])


def split_roles(array, tile_by, slc_by, slc_core, with_tile=True):
    tiles, groups, cores = (lax.axis_size(name) for name in ("tile", "slc", "pos"))
    at = lambda t, g, c: ((t % tiles) * groups + g % groups) * cores + c
    pairs = []
    for t in range(tiles):
        for g in range(groups):
            pairs.append((at(t, g, slc_core), at(t, g + slc_by, slc_core)))
            if with_tile:
                pairs.append((at(t, g, 1 - slc_core), at(t + tile_by, g, 1 - slc_core)))
    return lax.ppermute(array, ("tile", "slc", "pos"), pairs)


def base_tables(pix):
    index = np.arange(pix)
    angles = 2.0 * math.pi / pix * (np.outer(index, index) % pix)
    scale = 1.0 / math.sqrt(pix)
    rounded = lambda v: v.astype(np.float32).astype(ml_dtypes.bfloat16)
    wide = lambda v: rounded(v).astype(np.float64)
    w = wide(np.cos(angles) * scale) + 1j * wide(-np.sin(angles) * scale)
    freq = (index + pix // 2) % pix - pix // 2
    h = np.exp(-0.4j * math.pi / pix * (freq * freq))
    planes = []
    for factor in (np.ones_like(h), h, np.conj(h)):
        b = (factor[:, None] * w)[np.concatenate([index[::2], index[1::2]])]
        planes += [b.real, b.imag]
    stack = np.stack(planes)
    return rounded(np.stack([stack, stack.transpose(0, 2, 1)]))


def prep_kernel(mine, pix, info, base, probe, measured, lefts, rights, psi0, light, masks):
    bf16, f32 = jnp.bfloat16, jnp.float32
    mid = pix // 2

    def rolled(side, f, shift, axis):
        found = []
        for part in range(2):
            whole = pltpu.roll(base[side, 2 * f + part].astype(f32), shift, axis)
            found.append(whole[:, :mid] if axis else whole[:mid])
        return found

    def put(ref, m, t, re, im, by_rows, from_left):
        for odd in range(2):
            at = slice(odd * mid, (odd + 1) * mid)
            re_part, im_part = (re[at], im[at]) if by_rows else (re[:, at], im[:, at])
            upper, lower = (-im_part, im_part) if from_left else (im_part, -im_part)
            ref[m, t, odd, :mid, :mid] = re_part.astype(bf16)
            ref[m, t, odd, :mid, mid:] = upper.astype(bf16)
            ref[m, t, odd, mid:, :mid] = lower.astype(bf16)
            ref[m, t, odd, mid:, mid:] = re_part.astype(bf16)

    row_at = lax.broadcasted_iota(jnp.int32, (pix, pix), 0)
    col_at = lax.broadcasted_iota(jnp.int32, (pix, pix), 1)
    order = lambda at: jnp.where(at < mid, 2 * at, 2 * at - (pix - 1))
    pick_rows = (col_at == order(row_at)).astype(f32).astype(bf16)
    pick_cols = (row_at == order(col_at)).astype(f32).astype(bf16)

    def exact(values, product):
        total = None
        for _ in range(3):
            term = values.astype(bf16)
            values = values - term.astype(f32)
            moved = product(term)
            total = moved if total is None else total + moved
        return total

    for m in range(mine):
        r0 = info[2 + 4 * m]
        c0 = info[4 + 4 * m]
        for t in range(3):
            put(lefts, m, t, *rolled(0, t, r0, 1), True, True)
            put(rights, m, t, *rolled(1, t, c0, 0), False, False)
        re, im = rolled(1, 0, r0, 0)
        put(lefts, m, 3, re, -im, False, True)
        re, im = rolled(0, 0, c0, 1)
        put(rights, m, 3, re, -im, True, False)
        for part in range(2):
            plane = probe[:, part * pix : (part + 1) * pix].astype(f32)
            plane = pltpu.roll(pltpu.roll(plane, r0, 0), c0, 1)
            psi0[m, part] = plane.astype(bf16)
        for below in range(2):
            rows = (row_at < r0) if below else (row_at >= r0)
            for col in range(2):
                low = jnp.where(info[3 + 4 * m] == col, c0, 0)
                high = jnp.where(info[3 + 4 * m] == col, pix, c0)
                inside = rows & (col_at >= low) & (col_at < high)
                masks[m, below, col] = jnp.where(inside, 1.0, 0.0).astype(bf16)
        seen = measured[info[0] * mine + m]
        seen = exact(seen, lambda v: jnp.dot(pick_rows, v, preferred_element_type=f32))
        light[m] = exact(seen, lambda v: jnp.dot(v, pick_cols, preferred_element_type=f32))


def main_kernel(groups, depth, mine, pix, pieces, info, *refs):
    count = len(pieces) + 1
    own, operands = refs[0], refs[1:count]
    lefts_any, rights_any, psi0_any, light_any, masks_any = refs[count : count + 5]
    outs = refs[count + 5 : count + 5 + 4 * groups]
    obj, tp, psi, lefts, rights, light, masks, grads, sems, tab_sems, out_sems = refs[count + 5 + 4 * groups :]
    layers = groups * depth
    half = depth // 2
    rank = info[0]
    core = info[1]
    members = range(mine)

    def layer_of(s, i):
        group = lax.rem(rank - s + groups, groups)
        return group * depth + i

    def table_copies(t):
        return [
            pltpu.make_async_copy(lefts_any.at[:, t], lefts.at[:, t], tab_sems.at[t, 0]),
            pltpu.make_async_copy(rights_any.at[:, t], rights.at[:, t], tab_sems.at[t, 1]),
        ]

    def wait_tables(t):
        for copy in table_copies(t):
            copy.wait()

    psi_copy = pltpu.make_async_copy(psi0_any, psi.at[0], tab_sems.at[4, 0])
    light_copy = pltpu.make_async_copy(light_any, light, tab_sems.at[4, 1])
    mask_copy = pltpu.make_async_copy(masks_any, masks, tab_sems.at[5, 0])
    psi_copy.start()
    mask_copy.start()
    for copy in table_copies(1) + table_copies(3):
        copy.start()
    for i in range(depth):
        j = layer_of(0, i)
        pltpu.make_async_copy(own.at[i], obj.at[j, 0], sems.at[j, 0]).start()
    for holds, ref in zip(pieces, operands):
        for c in range(2):
            if holds[c] is None:
                continue
            s, high, below = holds[c]

            @pl.when(core == c)
            def _():
                for i in range(half):
                    j = layer_of(s, high * half + i)
                    pltpu.make_async_copy(ref.at[i], obj.at[j, below], sems.at[j, below]).start()

    light_copy.start()
    for copy in table_copies(0) + table_copies(2):
        copy.start()

    def wait_object(j):
        for below in range(2):
            pltpu.make_async_copy(own.at[0], obj.at[j, below], sems.at[j, below]).wait()

    live = [info[5 + 4 * m].astype(jnp.float32) for m in members]
    f32 = jnp.float32
    bf16 = jnp.bfloat16

    def patch(j, m, part):
        total = None
        for below in range(2):
            for col in range(2):
                term = obj[j, below, part, :, col * pix : (col + 1) * pix] * masks[m, below, col]
                total = term if total is None else total + term
        return total

    mid = pix // 2
    cat = lambda parts, axis: jnp.concatenate(parts, axis=axis)

    def product(a, b):
        return jnp.dot(a, b, preferred_element_type=f32)

    def spectrum_of(t, pairs):
        halfway = []
        for m, (re, im) in zip(members, pairs):
            plus = cat([re[:mid] + re[mid:], im[:mid] + im[mid:]], 0).astype(bf16)
            minus = cat([re[:mid] - re[mid:], im[:mid] - im[mid:]], 0).astype(bf16)
            halfway.append((product(lefts[m, t, 0], plus), product(lefts[m, t, 1], minus)))
        found = []
        for m, groups_of_rows in zip(members, halfway):
            plus = cat([cat([g[:mid, :mid] + g[:mid, mid:], g[mid:, :mid] + g[mid:, mid:]], 1) for g in groups_of_rows], 0)
            minus = cat([cat([g[:mid, :mid] - g[:mid, mid:], g[mid:, :mid] - g[mid:, mid:]], 1) for g in groups_of_rows], 0)
            found.append((product(plus.astype(bf16), rights[m, t, 0]), product(minus.astype(bf16), rights[m, t, 1])))
        return found

    def wave_of(spectra):
        halfway = []
        for m, (even, odd) in zip(members, spectra):
            even, odd = even.astype(bf16), odd.astype(bf16)
            terms = []
            for half_at in range(2):
                at = slice(half_at * mid, (half_at + 1) * mid)
                stacked = cat([cat([even[at, :mid], odd[at, :mid]], 1), cat([even[at, mid:], odd[at, mid:]], 1)], 0)
                terms.append(product(lefts[m, 3, half_at], stacked))
            halfway.append(((terms[0] + terms[1]).astype(bf16), (terms[0] - terms[1]).astype(bf16)))
        found = []
        for m, blocks in zip(members, halfway):
            terms = []
            for half_at in range(2):
                at = slice(half_at * mid, (half_at + 1) * mid)
                rows = cat([cat([b[:mid, at], b[mid:, at]], 1) for b in blocks], 0)
                terms.append(product(rows, rights[m, 3, half_at]))
            near, far = terms[0] + terms[1], terms[0] - terms[1]
            found.append((cat([near[:, :mid], far[:, :mid]], 1), cat([near[:, mid:], far[:, mid:]], 1)))
        return found

    def entrance(j):
        pairs = []
        for m in members:
            tr, ti = patch(j, m, 0), patch(j, m, 1)
            tp[j, m, 0] = tr
            tp[j, m, 1] = ti
            pr, pi = psi[j, m, 0], psi[j, m, 1]
            pairs.append(((tr * pr - ti * pi).astype(f32), (tr * pi + ti * pr).astype(f32)))
        return pairs

    psi_copy.wait()
    mask_copy.wait()
    wait_tables(1)
    wait_tables(3)

    def forward(j, carry):
        wait_object(j)
        spectra = spectrum_of(1, entrance(j))
        for m, (re, im) in enumerate(wave_of(spectra)):
            psi[j + 1, m, 0] = re.astype(bf16)
            psi[j + 1, m, 1] = im.astype(bf16)
        return carry

    lax.fori_loop(0, layers - 1, forward, 0)
    wait_object(layers - 1)
    wait_tables(0)
    light_copy.wait()
    spectra = spectrum_of(0, entrance(layers - 1))
    tilted = []
    for m, parts in enumerate(spectra):
        scaled = []
        for odd, values in enumerate(parts):
            re, im = values[:, :mid], values[:, mid:]
            excess = (re * re + im * im - light[m, :, odd * mid : (odd + 1) * mid]) * live[m]
            scaled.append(cat([excess * re, excess * im], 1))
        tilted.append(tuple(scaled))
    exits = wave_of(tilted)

    def out_copies(s, i):
        place = s * depth + i
        copies = []
        for away in range(2):
            at = pl.multiple_of(((1 - core) if away else core) * pix, pix)
            for below in range(2):
                out = outs[(away * 2 + below) * groups + s]
                columns = grads.at[below, place, :, :, pl.ds(at, pix)]
                copies.append(pltpu.make_async_copy(columns, out.at[i], out_sems.at[away * 2 + below, place]))
        return copies

    def send_out(step, within):
        for s in range(groups):

            @pl.when(step == s)
            def _():
                for copy in out_copies(s, within):
                    copy.start()

    def scatter(j, exits):
        step = lax.rem(rank - j // depth + groups, groups)
        within = lax.rem(j, depth)
        place = step * depth + within
        terms = []
        for m, (re, im) in enumerate(exits):
            re, im = re.astype(bf16), im.astype(bf16)
            pr, pi = psi[j, m, 0], psi[j, m, 1]
            terms.append((pr * re + pi * im, pr * im - pi * re))
        for below in range(2):
            for col in range(2):
                for part in range(2):
                    total = None
                    for m in members:
                        term = terms[m][part] * masks[m, below, col]
                        total = term if total is None else total + term
                    grads[below, place, part, :, col * pix : (col + 1) * pix] = total
        send_out(step, within)

    def wave_grads(j, exits):
        pairs = []
        for m, (re, im) in enumerate(exits):
            re, im = re.astype(bf16), im.astype(bf16)
            tr, ti = tp[j, m, 0], tp[j, m, 1]
            pairs.append(((tr * re + ti * im).astype(f32), (tr * im - ti * re).astype(f32)))
        return pairs

    wait_tables(2)
    hold = tuple(part for pair in exits for part in pair)

    def backward(step, flat):
        j = layers - 1 - step
        exits = [(flat[2 * m], flat[2 * m + 1]) for m in members]
        scatter(j, exits)
        exits = wave_of(spectrum_of(2, wave_grads(j, exits)))
        return tuple(part for pair in exits for part in pair)

    hold = lax.fori_loop(0, layers - 1, backward, hold)
    scatter(0, [(hold[2 * m], hold[2 * m + 1]) for m in members])
    for s in range(groups):
        for i in range(depth):
            for copy in out_copies(s, i):
                copy.wait()


def body(object_field, offsets, counts, measured, probe_wave):
    depth, rows, _, cols = object_field.shape
    pix = probe_wave.shape[0]
    slots_here = offsets.shape[1]
    groups = lax.axis_size("slc")
    rank = lax.axis_index("slc").astype(jnp.int32)
    tile = lax.axis_index("tile").astype(jnp.int32)
    core = lax.axis_index("pos").astype(jnp.int32)
    mine = slots_here // groups
    layers = groups * depth
    first = rank * mine
    bf16 = jnp.bfloat16

    off = lax.dynamic_slice(offsets, (jnp.int32(0), first), (2, mine))
    in_tile = core * slots_here + first + jnp.arange(mine, dtype=jnp.int32)
    alive = (in_tile < counts[0]).astype(jnp.int32)
    places = jnp.stack([off[0] - tile * rows, off[1] // pix, off[1] % pix, alive], axis=1)
    info = jnp.concatenate([jnp.stack([rank, core]), places.reshape(-1)])

    planes = object_field.transpose(0, 2, 1, 3)
    half = depth // 2
    steps = range(1, groups)
    halves_of = lambda high: lax.dynamic_slice_in_dim(planes, high * half, half, axis=0)
    planes, info = lax.optimization_barrier((planes, info))
    first_half, last_half = halves_of(core), halves_of(1 - core)
    got_first = [split_roles(first_half, -1, s, 0, s == 1) for s in steps]

    smem = pl.BlockSpec(memory_space=pltpu.SMEM)
    vmem = pl.BlockSpec(memory_space=pltpu.VMEM)
    anywhere = pl.BlockSpec(memory_space=pl.ANY)
    tables_shape = jax.ShapeDtypeStruct((mine, 4, 2, pix, pix), bf16)
    lefts, rights, psi0, light, masks = pl.pallas_call(
        functools.partial(prep_kernel, mine, pix),
        out_shape=(
            tables_shape,
            tables_shape,
            jax.ShapeDtypeStruct((mine, 2, pix, pix), bf16),
            jax.ShapeDtypeStruct((mine, pix, pix), jnp.float32),
            jax.ShapeDtypeStruct((mine, 2, 2, pix, pix), bf16),
        ),
        in_specs=[smem, vmem, vmem, vmem],
        out_specs=(vmem,) * 5,
        compiler_params=pltpu.CompilerParams(vmem_limit_bytes=VMEM_LIMIT),
        cost_estimate=pl.CostEstimate(flops=8 * 10**9, bytes_accessed=8 * 2**20, transcendentals=0),
        name="tables",
    )(info, jnp.asarray(base_tables(pix)), probe_wave, measured)

    last_half, lefts, rights, psi0, light, masks = lax.optimization_barrier(
        (last_half, lefts, rights, psi0, light, masks)
    )
    got_last = [split_roles(last_half, -1, s, 0, s == 1) for s in steps]
    passed_on = [split_roles(got_first[s - 1], -1, s, 1) for s in steps]
    pieces, operands = [], []
    for s in steps:
        rim_hi, rim_lo = ((0, 1, 1), (0, 0, 1)) if s == 1 else (None, None)
        for array, holds in (
            (got_first[s - 1], ((s, 0, 0), rim_hi)),
            (got_last[s - 1], ((s, 1, 0), rim_lo)),
            (passed_on[s - 1], ((s, 0, 1), (s, 1, 1))),
        ):
            pieces += [holds, holds[::-1]]
            operands += [array, passed(array, "pos", 1)]

    outs = pl.pallas_call(
        functools.partial(main_kernel, groups, depth, mine, pix, tuple(pieces)),
        out_shape=(jax.ShapeDtypeStruct((depth, 2, rows, pix), bf16),) * (4 * groups),
        in_specs=[smem] + [anywhere] * (6 + len(operands)),
        out_specs=(anywhere,) * (4 * groups),
        scratch_shapes=[
            pltpu.VMEM((layers, 2, 2, pix, cols), bf16),
            pltpu.VMEM((layers, mine, 2, pix, pix), bf16),
            pltpu.VMEM((layers, mine, 2, pix, pix), bf16),
            pltpu.VMEM((mine, 4, 2, pix, pix), bf16),
            pltpu.VMEM((mine, 4, 2, pix, pix), bf16),
            pltpu.VMEM((mine, pix, pix), jnp.float32),
            pltpu.VMEM((mine, 2, 2, pix, pix), bf16),
            pltpu.VMEM((2, layers, 2, pix, cols), bf16),
            pltpu.SemaphoreType.DMA((layers, 2)),
            pltpu.SemaphoreType.DMA((6, 2)),
            pltpu.SemaphoreType.DMA((4, layers)),
        ],
        compiler_params=pltpu.CompilerParams(vmem_limit_bytes=VMEM_LIMIT),
        cost_estimate=pl.CostEstimate(flops=15 * 10**9, bytes_accessed=16 * 2**20, transcendentals=0),
        name="waves",
    )(info, planes, *operands, lefts, rights, psi0, light, masks)

    wide = lambda v: v.astype(jnp.float32)
    sums = {}
    for s in [*steps, 0]:
        for row_block in (1, 0):
            at = row_block * groups + s
            sums[row_block, s] = wide(outs[at]) + wide(passed(outs[2 * groups + at], "pos", 1))
    rim_lo = sums[1, 0][:half]
    rim_hi = sums[1, 0][half:].astype(bf16)
    tile_lo = sums[0, 0][:half]
    tile_hi = sums[0, 0][half:]
    for s in steps:
        rim, tile_part = sums[1, s], sums[0, s]
        rim_lo += wide(passed(rim[:half].astype(bf16), "slc", -s))
        other_hi = tile_part[half:] + wide(passed(rim[half:].astype(bf16), "tile", 1))
        tile_lo += wide(passed(tile_part[:half].astype(bf16), "slc", -s))
        tile_hi += wide(passed(other_hi.astype(bf16), "slc", -s))
    tile_hi += wide(passed(rim_hi, "tile", 1))
    tile_lo += wide(passed(rim_lo.astype(bf16), "tile", 1))
    return jnp.concatenate([tile_lo, tile_hi]).transpose(0, 2, 1, 3)


def solution(mesh):
    placed = (
        P(("grp", "slc"), "tile", None, None),
        P(None, ("grp", "tile", "pos")),
        P(("grp", "tile")),
        P(("grp", "tile", "pos"), None, None),
        P("grp", None),
    )
    return jax.shard_map(
        body,
        mesh=mesh,
        in_specs=placed,
        out_specs=P(("grp", "slc"), "tile", None, "pos"),
        check_vma=False,
    )
```

```python
import functools
import math

import jax
import jax.numpy as jnp
import ml_dtypes
import numpy as np
from jax import lax
from jax.experimental import pallas as pl
from jax.experimental.pallas import tpu as pltpu
from jax.sharding import PartitionSpec as P

VMEM_LIMIT = 38 * 1024 * 1024


def passed(array, axis, by):
    peers = lax.axis_size(axis)
    return lax.ppermute(array, axis, [(i, (i + by) % peers) for i in range(peers)])


def split_roles(array, tile_by, slc_by, slc_core, with_tile=True):
    tiles, groups, cores = (lax.axis_size(name) for name in ("tile", "slc", "pos"))
    at = lambda t, g, c: ((t % tiles) * groups + g % groups) * cores + c
    pairs = []
    for t in range(tiles):
        for g in range(groups):
            pairs.append((at(t, g, slc_core), at(t, g + slc_by, slc_core)))
            if with_tile:
                pairs.append((at(t, g, 1 - slc_core), at(t + tile_by, g, 1 - slc_core)))
    return lax.ppermute(array, ("tile", "slc", "pos"), pairs)


def base_tables(pix):
    index = np.arange(pix)
    angles = 2.0 * math.pi / pix * (np.outer(index, index) % pix)
    scale = 1.0 / math.sqrt(pix)
    rounded = lambda v: v.astype(np.float32).astype(ml_dtypes.bfloat16)
    wide = lambda v: rounded(v).astype(np.float64)
    w = wide(np.cos(angles) * scale) + 1j * wide(-np.sin(angles) * scale)
    freq = (index + pix // 2) % pix - pix // 2
    h = np.exp(-0.4j * math.pi / pix * (freq * freq))
    planes = []
    for factor in (np.ones_like(h), h, np.conj(h)):
        b = (factor[:, None] * w)[np.concatenate([index[::2], index[1::2]])]
        planes += [b.real, b.imag]
    stack = np.stack(planes)
    return rounded(np.stack([stack, stack.transpose(0, 2, 1)]))


def prep_kernel(mine, pix, info, base, probe, measured, lefts, rights, psi0, light, masks):
    bf16, f32 = jnp.bfloat16, jnp.float32
    mid = pix // 2

    def rolled(side, f, shift, axis):
        found = []
        for part in range(2):
            whole = pltpu.roll(base[side, 2 * f + part].astype(f32), shift, axis)
            found.append(whole[:, :mid] if axis else whole[:mid])
        return found

    def put(ref, m, t, re, im, by_rows, from_left):
        for odd in range(2):
            at = slice(odd * mid, (odd + 1) * mid)
            re_part, im_part = (re[at], im[at]) if by_rows else (re[:, at], im[:, at])
            upper, lower = (-im_part, im_part) if from_left else (im_part, -im_part)
            ref[m, t, odd, :mid, :mid] = re_part.astype(bf16)
            ref[m, t, odd, :mid, mid:] = upper.astype(bf16)
            ref[m, t, odd, mid:, :mid] = lower.astype(bf16)
            ref[m, t, odd, mid:, mid:] = re_part.astype(bf16)

    row_at = lax.broadcasted_iota(jnp.int32, (pix, pix), 0)
    col_at = lax.broadcasted_iota(jnp.int32, (pix, pix), 1)
    order = lambda at: jnp.where(at < mid, 2 * at, 2 * at - (pix - 1))
    pick_rows = (col_at == order(row_at)).astype(f32).astype(bf16)
    pick_cols = (row_at == order(col_at)).astype(f32).astype(bf16)

    def exact(values, product):
        total = None
        for _ in range(3):
            term = values.astype(bf16)
            values = values - term.astype(f32)
            moved = product(term)
            total = moved if total is None else total + moved
        return total

    for m in range(mine):
        r0 = info[2 + 4 * m]
        c0 = info[4 + 4 * m]
        for t in range(3):
            put(lefts, m, t, *rolled(0, t, r0, 1), True, True)
            put(rights, m, t, *rolled(1, t, c0, 0), False, False)
        re, im = rolled(1, 0, r0, 0)
        put(lefts, m, 3, re, -im, False, True)
        re, im = rolled(0, 0, c0, 1)
        put(rights, m, 3, re, -im, True, False)
        for part in range(2):
            plane = probe[:, part * pix : (part + 1) * pix].astype(f32)
            plane = pltpu.roll(pltpu.roll(plane, r0, 0), c0, 1)
            psi0[m, part] = plane.astype(bf16)
        for below in range(2):
            rows = (row_at < r0) if below else (row_at >= r0)
            for col in range(2):
                low = jnp.where(info[3 + 4 * m] == col, c0, 0)
                high = jnp.where(info[3 + 4 * m] == col, pix, c0)
                inside = rows & (col_at >= low) & (col_at < high)
                masks[m, below, col] = jnp.where(inside, 1.0, 0.0).astype(bf16)
        seen = measured[info[0] * mine + m]
        seen = exact(seen, lambda v: jnp.dot(pick_rows, v, preferred_element_type=f32))
        light[m] = exact(seen, lambda v: jnp.dot(v, pick_cols, preferred_element_type=f32))


def main_kernel(groups, depth, mine, pix, pieces, info, *refs):
    count = len(pieces) + 1
    own, operands = refs[0], refs[1:count]
    lefts_any, rights_any, psi0_any, light_any, masks_any = refs[count : count + 5]
    outs = refs[count + 5 : count + 5 + 4 * groups]
    obj, tp, psi, lefts, rights, light, masks, grads, sems, tab_sems, out_sems = refs[count + 5 + 4 * groups :]
    layers = groups * depth
    half = depth // 2
    rank = info[0]
    core = info[1]
    members = range(mine)

    def layer_of(s, i):
        group = lax.rem(rank - s + groups, groups)
        return group * depth + i

    def table_copies(t):
        return [
            pltpu.make_async_copy(lefts_any.at[:, t], lefts.at[:, t], tab_sems.at[t, 0]),
            pltpu.make_async_copy(rights_any.at[:, t], rights.at[:, t], tab_sems.at[t, 1]),
        ]

    def wait_tables(t):
        for copy in table_copies(t):
            copy.wait()

    psi_copy = pltpu.make_async_copy(psi0_any, psi.at[0], tab_sems.at[4, 0])
    light_copy = pltpu.make_async_copy(light_any, light, tab_sems.at[4, 1])
    mask_copy = pltpu.make_async_copy(masks_any, masks, tab_sems.at[5, 0])
    psi_copy.start()
    mask_copy.start()
    for copy in table_copies(1) + table_copies(3):
        copy.start()
    for i in range(depth):
        j = layer_of(0, i)
        pltpu.make_async_copy(own.at[i], obj.at[j, 0], sems.at[j, 0]).start()
    for holds, ref in zip(pieces, operands):
        for c in range(2):
            if holds[c] is None:
                continue
            s, high, below = holds[c]

            @pl.when(core == c)
            def _():
                for i in range(half):
                    j = layer_of(s, high * half + i)
                    pltpu.make_async_copy(ref.at[i], obj.at[j, below], sems.at[j, below]).start()

    light_copy.start()
    for copy in table_copies(0) + table_copies(2):
        copy.start()

    def wait_object(j):
        for below in range(2):
            pltpu.make_async_copy(own.at[0], obj.at[j, below], sems.at[j, below]).wait()

    live = [info[5 + 4 * m].astype(jnp.float32) for m in members]
    f32 = jnp.float32
    bf16 = jnp.bfloat16

    def patch(j, m, part):
        total = None
        for below in range(2):
            for col in range(2):
                term = obj[j, below, part, :, col * pix : (col + 1) * pix] * masks[m, below, col]
                total = term if total is None else total + term
        return total

    mid = pix // 2
    cat = lambda parts, axis: jnp.concatenate(parts, axis=axis)

    def product(a, b):
        return jnp.dot(a, b, preferred_element_type=f32)

    def spectrum_of(t, pairs):
        halfway = []
        for m, (re, im) in zip(members, pairs):
            plus = cat([re[:mid] + re[mid:], im[:mid] + im[mid:]], 0).astype(bf16)
            minus = cat([re[:mid] - re[mid:], im[:mid] - im[mid:]], 0).astype(bf16)
            halfway.append((product(lefts[m, t, 0], plus), product(lefts[m, t, 1], minus)))
        found = []
        for m, groups_of_rows in zip(members, halfway):
            plus = cat([cat([g[:mid, :mid] + g[:mid, mid:], g[mid:, :mid] + g[mid:, mid:]], 1) for g in groups_of_rows], 0)
            minus = cat([cat([g[:mid, :mid] - g[:mid, mid:], g[mid:, :mid] - g[mid:, mid:]], 1) for g in groups_of_rows], 0)
            found.append((product(plus.astype(bf16), rights[m, t, 0]), product(minus.astype(bf16), rights[m, t, 1])))
        return found

    def wave_of(spectra):
        halfway = []
        for m, (even, odd) in zip(members, spectra):
            even, odd = even.astype(bf16), odd.astype(bf16)
            terms = []
            for half_at in range(2):
                at = slice(half_at * mid, (half_at + 1) * mid)
                stacked = cat([cat([even[at, :mid], odd[at, :mid]], 1), cat([even[at, mid:], odd[at, mid:]], 1)], 0)
                terms.append(product(lefts[m, 3, half_at], stacked))
            halfway.append(((terms[0] + terms[1]).astype(bf16), (terms[0] - terms[1]).astype(bf16)))
        found = []
        for m, blocks in zip(members, halfway):
            terms = []
            for half_at in range(2):
                at = slice(half_at * mid, (half_at + 1) * mid)
                rows = cat([cat([b[:mid, at], b[mid:, at]], 1) for b in blocks], 0)
                terms.append(product(rows, rights[m, 3, half_at]))
            near, far = terms[0] + terms[1], terms[0] - terms[1]
            found.append((cat([near[:, :mid], far[:, :mid]], 1), cat([near[:, mid:], far[:, mid:]], 1)))
        return found

    def entrance(j):
        pairs = []
        for m in members:
            tr, ti = patch(j, m, 0), patch(j, m, 1)
            tp[j, m, 0] = tr
            tp[j, m, 1] = ti
            pr, pi = psi[j, m, 0], psi[j, m, 1]
            pairs.append(((tr * pr - ti * pi).astype(f32), (tr * pi + ti * pr).astype(f32)))
        return pairs

    psi_copy.wait()
    mask_copy.wait()
    wait_tables(1)
    wait_tables(3)

    def forward(j, carry):
        wait_object(j)
        spectra = spectrum_of(1, entrance(j))
        for m, (re, im) in enumerate(wave_of(spectra)):
            psi[j + 1, m, 0] = re.astype(bf16)
            psi[j + 1, m, 1] = im.astype(bf16)
        return carry

    lax.fori_loop(0, layers - 1, forward, 0)
    wait_object(layers - 1)
    wait_tables(0)
    light_copy.wait()
    spectra = spectrum_of(0, entrance(layers - 1))
    tilted = []
    for m, parts in enumerate(spectra):
        scaled = []
        for odd, values in enumerate(parts):
            re, im = values[:, :mid], values[:, mid:]
            excess = (re * re + im * im - light[m, :, odd * mid : (odd + 1) * mid]) * live[m]
            scaled.append(cat([excess * re, excess * im], 1))
        tilted.append(tuple(scaled))
    exits = wave_of(tilted)

    def out_copies(s, i):
        place = s * depth + i
        copies = []
        for away in range(2):
            at = pl.multiple_of(((1 - core) if away else core) * pix, pix)
            for below in range(2):
                out = outs[(away * 2 + below) * groups + s]
                columns = grads.at[below, place, :, :, pl.ds(at, pix)]
                copies.append(pltpu.make_async_copy(columns, out.at[i], out_sems.at[away * 2 + below, place]))
        return copies

    def send_out(step, within):
        for s in range(groups):

            @pl.when(step == s)
            def _():
                for copy in out_copies(s, within):
                    copy.start()

    def scatter(j, exits):
        step = lax.rem(rank - j // depth + groups, groups)
        within = lax.rem(j, depth)
        place = step * depth + within
        terms = []
        for m, (re, im) in enumerate(exits):
            re, im = re.astype(bf16), im.astype(bf16)
            pr, pi = psi[j, m, 0], psi[j, m, 1]
            terms.append((pr * re + pi * im, pr * im - pi * re))
        for below in range(2):
            for col in range(2):
                for part in range(2):
                    total = None
                    for m in members:
                        term = terms[m][part] * masks[m, below, col]
                        total = term if total is None else total + term
                    grads[below, place, part, :, col * pix : (col + 1) * pix] = total
        send_out(step, within)

    def wave_grads(j, exits):
        pairs = []
        for m, (re, im) in enumerate(exits):
            re, im = re.astype(bf16), im.astype(bf16)
            tr, ti = tp[j, m, 0], tp[j, m, 1]
            pairs.append(((tr * re + ti * im).astype(f32), (tr * im - ti * re).astype(f32)))
        return pairs

    wait_tables(2)
    hold = tuple(part for pair in exits for part in pair)

    def backward(step, flat):
        j = layers - 1 - step
        exits = [(flat[2 * m], flat[2 * m + 1]) for m in members]
        scatter(j, exits)
        exits = wave_of(spectrum_of(2, wave_grads(j, exits)))
        return tuple(part for pair in exits for part in pair)

    hold = lax.fori_loop(0, layers - 1, backward, hold)
    scatter(0, [(hold[2 * m], hold[2 * m + 1]) for m in members])
    for s in range(groups):
        for i in range(depth):
            for copy in out_copies(s, i):
                copy.wait()


def body(object_field, offsets, counts, measured, probe_wave):
    depth, rows, _, cols = object_field.shape
    pix = probe_wave.shape[0]
    slots_here = offsets.shape[1]
    groups = lax.axis_size("slc")
    rank = lax.axis_index("slc").astype(jnp.int32)
    tile = lax.axis_index("tile").astype(jnp.int32)
    core = lax.axis_index("pos").astype(jnp.int32)
    mine = slots_here // groups
    layers = groups * depth
    first = rank * mine
    bf16 = jnp.bfloat16

    off = lax.dynamic_slice(offsets, (jnp.int32(0), first), (2, mine))
    in_tile = core * slots_here + first + jnp.arange(mine, dtype=jnp.int32)
    alive = (in_tile < counts[0]).astype(jnp.int32)
    places = jnp.stack([off[0] - tile * rows, off[1] // pix, off[1] % pix, alive], axis=1)
    info = jnp.concatenate([jnp.stack([rank, core]), places.reshape(-1)])

    planes = object_field.transpose(0, 2, 1, 3)
    half = depth // 2
    steps = range(1, groups)
    halves_of = lambda high: lax.dynamic_slice_in_dim(planes, high * half, half, axis=0)
    planes, info = lax.optimization_barrier((planes, info))
    first_half, last_half = halves_of(core), halves_of(1 - core)
    got_first = [split_roles(first_half, -1, s, 0, s == 1) for s in steps]

    smem = pl.BlockSpec(memory_space=pltpu.SMEM)
    vmem = pl.BlockSpec(memory_space=pltpu.VMEM)
    anywhere = pl.BlockSpec(memory_space=pl.ANY)
    tables_shape = jax.ShapeDtypeStruct((mine, 4, 2, pix, pix), bf16)
    lefts, rights, psi0, light, masks = pl.pallas_call(
        functools.partial(prep_kernel, mine, pix),
        out_shape=(
            tables_shape,
            tables_shape,
            jax.ShapeDtypeStruct((mine, 2, pix, pix), bf16),
            jax.ShapeDtypeStruct((mine, pix, pix), jnp.float32),
            jax.ShapeDtypeStruct((mine, 2, 2, pix, pix), bf16),
        ),
        in_specs=[smem, vmem, vmem, vmem],
        out_specs=(vmem,) * 5,
        compiler_params=pltpu.CompilerParams(vmem_limit_bytes=VMEM_LIMIT),
        cost_estimate=pl.CostEstimate(flops=8 * 10**9, bytes_accessed=8 * 2**20, transcendentals=0),
        name="tables",
    )(info, jnp.asarray(base_tables(pix)), probe_wave, measured)

    last_half, lefts, rights, psi0, light, masks = lax.optimization_barrier(
        (last_half, lefts, rights, psi0, light, masks)
    )
    got_last = [split_roles(last_half, -1, s, 0, s == 1) for s in steps]
    passed_on = [split_roles(got_first[s - 1], -1, s, 1) for s in steps]
    pieces, operands = [], []
    for s in steps:
        rim_hi, rim_lo = ((0, 1, 1), (0, 0, 1)) if s == 1 else (None, None)
        for array, holds in (
            (got_first[s - 1], ((s, 0, 0), rim_hi)),
            (got_last[s - 1], ((s, 1, 0), rim_lo)),
            (passed_on[s - 1], ((s, 0, 1), (s, 1, 1))),
        ):
            pieces += [holds, holds[::-1]]
            operands += [array, passed(array, "pos", 1)]

    outs = pl.pallas_call(
        functools.partial(main_kernel, groups, depth, mine, pix, tuple(pieces)),
        out_shape=(jax.ShapeDtypeStruct((depth, 2, rows, pix), bf16),) * (4 * groups),
        in_specs=[smem] + [anywhere] * (6 + len(operands)),
        out_specs=(anywhere,) * (4 * groups),
        scratch_shapes=[
            pltpu.VMEM((layers, 2, 2, pix, cols), bf16),
            pltpu.VMEM((layers, mine, 2, pix, pix), bf16),
            pltpu.VMEM((layers, mine, 2, pix, pix), bf16),
            pltpu.VMEM((mine, 4, 2, pix, pix), bf16),
            pltpu.VMEM((mine, 4, 2, pix, pix), bf16),
            pltpu.VMEM((mine, pix, pix), jnp.float32),
            pltpu.VMEM((mine, 2, 2, pix, pix), bf16),
            pltpu.VMEM((2, layers, 2, pix, cols), bf16),
            pltpu.SemaphoreType.DMA((layers, 2)),
            pltpu.SemaphoreType.DMA((6, 2)),
            pltpu.SemaphoreType.DMA((4, layers)),
        ],
        compiler_params=pltpu.CompilerParams(vmem_limit_bytes=VMEM_LIMIT),
        cost_estimate=pl.CostEstimate(flops=15 * 10**9, bytes_accessed=16 * 2**20, transcendentals=0),
        name="waves",
    )(info, planes, *operands, lefts, rights, psi0, light, masks)

    wide = lambda v: v.astype(jnp.float32)
    sums = {}
    for s in [*steps, 0]:
        for row_block in (1, 0):
            at = row_block * groups + s
            sums[row_block, s] = wide(outs[at]) + wide(passed(outs[2 * groups + at], "pos", 1))
    for s in steps:
        ready = lax.optimization_barrier((sums[0, s], sums[1, 0], sums[0, 0]))
        sums[0, s], sums[1, 0], sums[0, 0] = ready
    rim_lo = sums[1, 0][:half]
    rim_hi = sums[1, 0][half:].astype(bf16)
    tile_lo = sums[0, 0][:half]
    tile_hi = sums[0, 0][half:]
    for s in steps:
        rim, tile_part = sums[1, s], sums[0, s]
        rim_lo += wide(passed(rim[:half].astype(bf16), "slc", -s))
        other_hi = tile_part[half:] + wide(passed(rim[half:].astype(bf16), "tile", 1))
        tile_lo += wide(passed(tile_part[:half].astype(bf16), "slc", -s))
        tile_hi += wide(passed(other_hi.astype(bf16), "slc", -s))
    tile_hi += wide(passed(rim_hi, "tile", 1))
    tile_lo += wide(passed(rim_lo.astype(bf16), "tile", 1))
    return jnp.concatenate([tile_lo, tile_hi]).transpose(0, 2, 1, 3)


def solution(mesh):
    placed = (
        P(("grp", "slc"), "tile", None, None),
        P(None, ("grp", "tile", "pos")),
        P(("grp", "tile")),
        P(("grp", "tile", "pos"), None, None),
        P("grp", None),
    )
    return jax.shard_map(
        body,
        mesh=mesh,
        in_specs=placed,
        out_specs=P(("grp", "slc"), "tile", None, "pos"),
        check_vma=False,
    )
```

```python
import functools
import math

import jax
import jax.numpy as jnp
import ml_dtypes
import numpy as np
from jax import lax
from jax.experimental import pallas as pl
from jax.experimental.pallas import tpu as pltpu
from jax.sharding import PartitionSpec as P

VMEM_LIMIT = 38 * 1024 * 1024


def passed(array, axis, by):
    peers = lax.axis_size(axis)
    return lax.ppermute(array, axis, [(i, (i + by) % peers) for i in range(peers)])


def split_roles(array, tile_by, slc_by, slc_core, with_tile=True):
    tiles, groups, cores = (lax.axis_size(name) for name in ("tile", "slc", "pos"))
    at = lambda t, g, c: ((t % tiles) * groups + g % groups) * cores + c
    pairs = []
    for t in range(tiles):
        for g in range(groups):
            pairs.append((at(t, g, slc_core), at(t, g + slc_by, slc_core)))
            if with_tile:
                pairs.append((at(t, g, 1 - slc_core), at(t + tile_by, g, 1 - slc_core)))
    return lax.ppermute(array, ("tile", "slc", "pos"), pairs)


def base_tables(pix):
    index = np.arange(pix)
    angles = 2.0 * math.pi / pix * (np.outer(index, index) % pix)
    scale = 1.0 / math.sqrt(pix)
    rounded = lambda v: v.astype(np.float32).astype(ml_dtypes.bfloat16)
    wide = lambda v: rounded(v).astype(np.float64)
    w = wide(np.cos(angles) * scale) + 1j * wide(-np.sin(angles) * scale)
    freq = (index + pix // 2) % pix - pix // 2
    h = np.exp(-0.4j * math.pi / pix * (freq * freq))
    planes = []
    for factor in (np.ones_like(h), h, np.conj(h)):
        b = (factor[:, None] * w)[np.concatenate([index[::2], index[1::2]])]
        planes += [b.real, b.imag]
    stack = np.stack(planes)
    return rounded(np.stack([stack, stack.transpose(0, 2, 1)]))


def prep_kernel(mine, pix, info, base, probe, measured, lefts, rights, psi0, light, masks):
    bf16, f32 = jnp.bfloat16, jnp.float32
    mid = pix // 2

    def rolled(side, f, shift, axis):
        found = []
        for part in range(2):
            whole = pltpu.roll(base[side, 2 * f + part].astype(f32), shift, axis)
            found.append(whole[:, :mid] if axis else whole[:mid])
        return found

    def put(ref, m, t, re, im, by_rows, from_left):
        for odd in range(2):
            at = slice(odd * mid, (odd + 1) * mid)
            re_part, im_part = (re[at], im[at]) if by_rows else (re[:, at], im[:, at])
            upper, lower = (-im_part, im_part) if from_left else (im_part, -im_part)
            ref[m, t, odd, :mid, :mid] = re_part.astype(bf16)
            ref[m, t, odd, :mid, mid:] = upper.astype(bf16)
            ref[m, t, odd, mid:, :mid] = lower.astype(bf16)
            ref[m, t, odd, mid:, mid:] = re_part.astype(bf16)

    row_at = lax.broadcasted_iota(jnp.int32, (pix, pix), 0)
    col_at = lax.broadcasted_iota(jnp.int32, (pix, pix), 1)
    order = lambda at: jnp.where(at < mid, 2 * at, 2 * at - (pix - 1))
    pick_rows = (col_at == order(row_at)).astype(f32).astype(bf16)
    pick_cols = (row_at == order(col_at)).astype(f32).astype(bf16)

    def exact(values, product):
        total = None
        for _ in range(3):
            term = values.astype(bf16)
            values = values - term.astype(f32)
            moved = product(term)
            total = moved if total is None else total + moved
        return total

    for m in range(mine):
        r0 = info[2 + 4 * m]
        c0 = info[4 + 4 * m]
        for t in range(3):
            put(lefts, m, t, *rolled(0, t, r0, 1), True, True)
            put(rights, m, t, *rolled(1, t, c0, 0), False, False)
        re, im = rolled(1, 0, r0, 0)
        put(lefts, m, 3, re, -im, False, True)
        re, im = rolled(0, 0, c0, 1)
        put(rights, m, 3, re, -im, True, False)
        for part in range(2):
            plane = probe[:, part * pix : (part + 1) * pix].astype(f32)
            plane = pltpu.roll(pltpu.roll(plane, r0, 0), c0, 1)
            psi0[m, part] = plane.astype(bf16)
        for below in range(2):
            rows = (row_at < r0) if below else (row_at >= r0)
            for col in range(2):
                low = jnp.where(info[3 + 4 * m] == col, c0, 0)
                high = jnp.where(info[3 + 4 * m] == col, pix, c0)
                inside = rows & (col_at >= low) & (col_at < high)
                masks[m, below, col] = jnp.where(inside, 1.0, 0.0).astype(bf16)
        seen = measured[info[0] * mine + m]
        seen = exact(seen, lambda v: jnp.dot(pick_rows, v, preferred_element_type=f32))
        light[m] = exact(seen, lambda v: jnp.dot(v, pick_cols, preferred_element_type=f32))


def main_kernel(groups, depth, mine, pix, pieces, info, *refs):
    count = len(pieces) + 1
    own, operands = refs[0], refs[1:count]
    lefts_any, rights_any, psi0_any, light_any, masks_any = refs[count : count + 5]
    outs = refs[count + 5 : count + 5 + 4 * groups]
    obj, tp, psi, lefts, rights, light, masks, grads, sems, tab_sems, out_sems = refs[count + 5 + 4 * groups :]
    layers = groups * depth
    half = depth // 2
    rank = info[0]
    core = info[1]
    members = range(mine)

    def layer_of(s, i):
        group = lax.rem(rank - s + groups, groups)
        return group * depth + i

    def table_copies(t):
        return [
            pltpu.make_async_copy(lefts_any.at[:, t], lefts.at[:, t], tab_sems.at[t, 0]),
            pltpu.make_async_copy(rights_any.at[:, t], rights.at[:, t], tab_sems.at[t, 1]),
        ]

    def wait_tables(t):
        for copy in table_copies(t):
            copy.wait()

    psi_copy = pltpu.make_async_copy(psi0_any, psi.at[0], tab_sems.at[4, 0])
    light_copy = pltpu.make_async_copy(light_any, light, tab_sems.at[4, 1])
    mask_copy = pltpu.make_async_copy(masks_any, masks, tab_sems.at[5, 0])
    psi_copy.start()
    mask_copy.start()
    for copy in table_copies(1) + table_copies(3):
        copy.start()
    for i in range(depth):
        j = layer_of(0, i)
        pltpu.make_async_copy(own.at[i], obj.at[j, 0], sems.at[j, 0]).start()
    for holds, ref in zip(pieces, operands):
        for c in range(2):
            if holds[c] is None:
                continue
            s, high, below = holds[c]

            @pl.when(core == c)
            def _():
                for i in range(half):
                    j = layer_of(s, high * half + i)
                    pltpu.make_async_copy(ref.at[i], obj.at[j, below], sems.at[j, below]).start()

    light_copy.start()
    for copy in table_copies(0) + table_copies(2):
        copy.start()

    def wait_object(j):
        for below in range(2):
            pltpu.make_async_copy(own.at[0], obj.at[j, below], sems.at[j, below]).wait()

    live = [info[5 + 4 * m].astype(jnp.float32) for m in members]
    f32 = jnp.float32
    bf16 = jnp.bfloat16

    def patch(j, m, part):
        total = None
        for below in range(2):
            for col in range(2):
                term = obj[j, below, part, :, col * pix : (col + 1) * pix] * masks[m, below, col]
                total = term if total is None else total + term
        return total

    mid = pix // 2
    cat = lambda parts, axis: jnp.concatenate(parts, axis=axis)

    def product(a, b):
        return jnp.dot(a, b, preferred_element_type=f32)

    def spectrum_of(t, pairs):
        halfway = []
        for m, (re, im) in zip(members, pairs):
            re, im = re.astype(bf16), im.astype(bf16)
            plus = cat([re[:mid] + re[mid:], im[:mid] + im[mid:]], 0).astype(bf16)
            minus = cat([re[:mid] - re[mid:], im[:mid] - im[mid:]], 0).astype(bf16)
            halfway.append((product(lefts[m, t, 0], plus), product(lefts[m, t, 1], minus)))
        found = []
        for m, groups_of_rows in zip(members, halfway):
            plus = cat([cat([g[:mid, :mid] + g[:mid, mid:], g[mid:, :mid] + g[mid:, mid:]], 1) for g in groups_of_rows], 0)
            minus = cat([cat([g[:mid, :mid] - g[:mid, mid:], g[mid:, :mid] - g[mid:, mid:]], 1) for g in groups_of_rows], 0)
            found.append((product(plus.astype(bf16), rights[m, t, 0]), product(minus.astype(bf16), rights[m, t, 1])))
        return found

    def wave_of(spectra):
        halfway = []
        for m, (even, odd) in zip(members, spectra):
            even, odd = even.astype(bf16), odd.astype(bf16)
            terms = []
            for half_at in range(2):
                at = slice(half_at * mid, (half_at + 1) * mid)
                stacked = cat([cat([even[at, :mid], odd[at, :mid]], 1), cat([even[at, mid:], odd[at, mid:]], 1)], 0)
                terms.append(product(lefts[m, 3, half_at], stacked))
            halfway.append(((terms[0] + terms[1]).astype(bf16), (terms[0] - terms[1]).astype(bf16)))
        found = []
        for m, blocks in zip(members, halfway):
            terms = []
            for half_at in range(2):
                at = slice(half_at * mid, (half_at + 1) * mid)
                rows = cat([cat([b[:mid, at], b[mid:, at]], 1) for b in blocks], 0)
                terms.append(product(rows, rights[m, 3, half_at]))
            near, far = terms[0] + terms[1], terms[0] - terms[1]
            found.append((cat([near[:, :mid], far[:, :mid]], 1), cat([near[:, mid:], far[:, mid:]], 1)))
        return found

    def entrance(j):
        pairs = []
        for m in members:
            tr, ti = patch(j, m, 0), patch(j, m, 1)
            tp[j, m, 0] = tr
            tp[j, m, 1] = ti
            pr, pi = psi[j, m, 0], psi[j, m, 1]
            pairs.append(((tr * pr - ti * pi).astype(f32), (tr * pi + ti * pr).astype(f32)))
        return pairs

    psi_copy.wait()
    mask_copy.wait()
    wait_tables(1)
    wait_tables(3)

    def forward(j, carry):
        wait_object(j)
        spectra = spectrum_of(1, entrance(j))
        for m, (re, im) in enumerate(wave_of(spectra)):
            psi[j + 1, m, 0] = re.astype(bf16)
            psi[j + 1, m, 1] = im.astype(bf16)
        return carry

    lax.fori_loop(0, layers - 1, forward, 0)
    wait_object(layers - 1)
    wait_tables(0)
    light_copy.wait()
    spectra = spectrum_of(0, entrance(layers - 1))
    tilted = []
    for m, parts in enumerate(spectra):
        scaled = []
        for odd, values in enumerate(parts):
            re, im = values[:, :mid], values[:, mid:]
            excess = (re * re + im * im - light[m, :, odd * mid : (odd + 1) * mid]) * live[m]
            scaled.append(cat([excess * re, excess * im], 1))
        tilted.append(tuple(scaled))
    exits = wave_of(tilted)

    def out_copies(s, i):
        place = s * depth + i
        copies = []
        for away in range(2):
            at = pl.multiple_of(((1 - core) if away else core) * pix, pix)
            for below in range(2):
                out = outs[(away * 2 + below) * groups + s]
                columns = grads.at[below, place, :, :, pl.ds(at, pix)]
                copies.append(pltpu.make_async_copy(columns, out.at[i], out_sems.at[away * 2 + below, place]))
        return copies

    def send_out(step, within):
        for s in range(groups):

            @pl.when(step == s)
            def _():
                for copy in out_copies(s, within):
                    copy.start()

    def scatter(j, exits):
        step = lax.rem(rank - j // depth + groups, groups)
        within = lax.rem(j, depth)
        place = step * depth + within
        terms = []
        for m, (re, im) in enumerate(exits):
            re, im = re.astype(bf16), im.astype(bf16)
            pr, pi = psi[j, m, 0], psi[j, m, 1]
            terms.append((pr * re + pi * im, pr * im - pi * re))
        for below in range(2):
            for col in range(2):
                for part in range(2):
                    total = None
                    for m in members:
                        term = terms[m][part] * masks[m, below, col]
                        total = term if total is None else total + term
                    grads[below, place, part, :, col * pix : (col + 1) * pix] = total
        send_out(step, within)

    def wave_grads(j, exits):
        pairs = []
        for m, (re, im) in enumerate(exits):
            re, im = re.astype(bf16), im.astype(bf16)
            tr, ti = tp[j, m, 0], tp[j, m, 1]
            pairs.append(((tr * re + ti * im).astype(f32), (tr * im - ti * re).astype(f32)))
        return pairs

    wait_tables(2)
    hold = tuple(part for pair in exits for part in pair)

    def backward(step, flat):
        j = layers - 1 - step
        exits = [(flat[2 * m], flat[2 * m + 1]) for m in members]
        scatter(j, exits)
        exits = wave_of(spectrum_of(2, wave_grads(j, exits)))
        return tuple(part for pair in exits for part in pair)

    hold = lax.fori_loop(0, layers - 1, backward, hold)
    scatter(0, [(hold[2 * m], hold[2 * m + 1]) for m in members])
    for s in range(groups):
        for i in range(depth):
            for copy in out_copies(s, i):
                copy.wait()


def body(object_field, offsets, counts, measured, probe_wave):
    depth, rows, _, cols = object_field.shape
    pix = probe_wave.shape[0]
    slots_here = offsets.shape[1]
    groups = lax.axis_size("slc")
    rank = lax.axis_index("slc").astype(jnp.int32)
    tile = lax.axis_index("tile").astype(jnp.int32)
    core = lax.axis_index("pos").astype(jnp.int32)
    mine = slots_here // groups
    layers = groups * depth
    first = rank * mine
    bf16 = jnp.bfloat16

    off = lax.dynamic_slice(offsets, (jnp.int32(0), first), (2, mine))
    in_tile = core * slots_here + first + jnp.arange(mine, dtype=jnp.int32)
    alive = (in_tile < counts[0]).astype(jnp.int32)
    places = jnp.stack([off[0] - tile * rows, off[1] // pix, off[1] % pix, alive], axis=1)
    info = jnp.concatenate([jnp.stack([rank, core]), places.reshape(-1)])

    planes = object_field.transpose(0, 2, 1, 3)
    half = depth // 2
    steps = range(1, groups)
    halves_of = lambda high: lax.dynamic_slice_in_dim(planes, high * half, half, axis=0)
    planes, info = lax.optimization_barrier((planes, info))
    first_half, last_half = halves_of(core), halves_of(1 - core)
    got_first = [split_roles(first_half, -1, s, 0, s == 1) for s in steps]

    smem = pl.BlockSpec(memory_space=pltpu.SMEM)
    vmem = pl.BlockSpec(memory_space=pltpu.VMEM)
    anywhere = pl.BlockSpec(memory_space=pl.ANY)
    tables_shape = jax.ShapeDtypeStruct((mine, 4, 2, pix, pix), bf16)
    lefts, rights, psi0, light, masks = pl.pallas_call(
        functools.partial(prep_kernel, mine, pix),
        out_shape=(
            tables_shape,
            tables_shape,
            jax.ShapeDtypeStruct((mine, 2, pix, pix), bf16),
            jax.ShapeDtypeStruct((mine, pix, pix), jnp.float32),
            jax.ShapeDtypeStruct((mine, 2, 2, pix, pix), bf16),
        ),
        in_specs=[smem, vmem, vmem, vmem],
        out_specs=(vmem,) * 5,
        compiler_params=pltpu.CompilerParams(vmem_limit_bytes=VMEM_LIMIT),
        cost_estimate=pl.CostEstimate(flops=8 * 10**9, bytes_accessed=8 * 2**20, transcendentals=0),
        name="tables",
    )(info, jnp.asarray(base_tables(pix)), probe_wave, measured)

    last_half, lefts, rights, psi0, light, masks = lax.optimization_barrier(
        (last_half, lefts, rights, psi0, light, masks)
    )
    got_last = [split_roles(last_half, -1, s, 0, s == 1) for s in steps]
    passed_on = [split_roles(got_first[s - 1], -1, s, 1) for s in steps]
    pieces, operands = [], []
    for s in steps:
        rim_hi, rim_lo = ((0, 1, 1), (0, 0, 1)) if s == 1 else (None, None)
        for array, holds in (
            (got_first[s - 1], ((s, 0, 0), rim_hi)),
            (got_last[s - 1], ((s, 1, 0), rim_lo)),
            (passed_on[s - 1], ((s, 0, 1), (s, 1, 1))),
        ):
            pieces += [holds, holds[::-1]]
            operands += [array, passed(array, "pos", 1)]

    outs = pl.pallas_call(
        functools.partial(main_kernel, groups, depth, mine, pix, tuple(pieces)),
        out_shape=(jax.ShapeDtypeStruct((depth, 2, rows, pix), bf16),) * (4 * groups),
        in_specs=[smem] + [anywhere] * (6 + len(operands)),
        out_specs=(anywhere,) * (4 * groups),
        scratch_shapes=[
            pltpu.VMEM((layers, 2, 2, pix, cols), bf16),
            pltpu.VMEM((layers, mine, 2, pix, pix), bf16),
            pltpu.VMEM((layers, mine, 2, pix, pix), bf16),
            pltpu.VMEM((mine, 4, 2, pix, pix), bf16),
            pltpu.VMEM((mine, 4, 2, pix, pix), bf16),
            pltpu.VMEM((mine, pix, pix), jnp.float32),
            pltpu.VMEM((mine, 2, 2, pix, pix), bf16),
            pltpu.VMEM((2, layers, 2, pix, cols), bf16),
            pltpu.SemaphoreType.DMA((layers, 2)),
            pltpu.SemaphoreType.DMA((6, 2)),
            pltpu.SemaphoreType.DMA((4, layers)),
        ],
        compiler_params=pltpu.CompilerParams(vmem_limit_bytes=VMEM_LIMIT),
        cost_estimate=pl.CostEstimate(flops=15 * 10**9, bytes_accessed=16 * 2**20, transcendentals=0),
        name="waves",
    )(info, planes, *operands, lefts, rights, psi0, light, masks)

    wide = lambda v: v.astype(jnp.float32)
    sums = {}
    for s in [*steps, 0]:
        for row_block in (1, 0):
            at = row_block * groups + s
            sums[row_block, s] = wide(outs[at]) + wide(passed(outs[2 * groups + at], "pos", 1))
    for s in steps:
        ready = lax.optimization_barrier((sums[0, s], sums[1, 0], sums[0, 0]))
        sums[0, s], sums[1, 0], sums[0, 0] = ready
    rim_lo = sums[1, 0][:half]
    rim_hi = sums[1, 0][half:].astype(bf16)
    tile_lo = sums[0, 0][:half]
    tile_hi = sums[0, 0][half:]
    for s in steps:
        rim, tile_part = sums[1, s], sums[0, s]
        rim_lo += wide(passed(rim[:half].astype(bf16), "slc", -s))
        other_hi = tile_part[half:] + wide(passed(rim[half:].astype(bf16), "tile", 1))
        tile_lo += wide(passed(tile_part[:half].astype(bf16), "slc", -s))
        tile_hi += wide(passed(other_hi.astype(bf16), "slc", -s))
    tile_hi += wide(passed(rim_hi, "tile", 1))
    tile_lo += wide(passed(rim_lo.astype(bf16), "tile", 1))
    return jnp.concatenate([tile_lo, tile_hi]).transpose(0, 2, 1, 3)


def solution(mesh):
    placed = (
        P(("grp", "slc"), "tile", None, None),
        P(None, ("grp", "tile", "pos")),
        P(("grp", "tile")),
        P(("grp", "tile", "pos"), None, None),
        P("grp", None),
    )
    return jax.shard_map(
        body,
        mesh=mesh,
        in_specs=placed,
        out_specs=P(("grp", "slc"), "tile", None, "pos"),
        check_vma=False,
    )
```
